32 devices in a mesh: dp: 16 (over z, x, core), seq: 2 (over y).
Axes of the slice: x: 2, y: 2, z: 4, core: 2. Of those that a mesh axis runs over, the one named last changes fastest.
Arguments:
- inputs: float32 [32, 1024, 1024], P('dp', 'seq'), may hold values from -6 to 6
- grad_out: float32 [32, 1024, 1024], P('dp', 'seq'), may hold values from -6 to 6
- random_blocks: int32 [32, 16, 16, 3], P('dp', None, 'seq'), may hold values from 1 to 14, as said below
- w_query: bfloat16 [1024, 1024], P(('dp', 'seq')), may hold values from -0.1875 to 0.1875
- w_key: bfloat16 [1024, 1024], P(('dp', 'seq')), may hold values from -0.1875 to 0.1875
- w_value: bfloat16 [1024, 1024], P(('dp', 'seq')), may hold values from -0.1875 to 0.1875
- w_out: bfloat16 [1024, 1024], P(('dp', 'seq')), may hold values from -3 to 3
- w_up: bfloat16 [1024, 4096], P(('dp', 'seq')), may hold values from -0.1875 to 0.1875
- w_down: bfloat16 [4096, 1024], P(('dp', 'seq')), may hold values from -0.125 to 0.125
- ln1_gain: bfloat16 [1024], P(('dp', 'seq')), may hold values from 0.5 to 1.5
- ln1_bias: bfloat16 [1024], P(('dp', 'seq')), may hold values from -4 to 4
- query_bias: bfloat16 [1024], P(('dp', 'seq')), may hold values from -6 to 6
- value_bias: bfloat16 [1024], P(('dp', 'seq')), may hold values from -1.5 to 1.5
- out_bias: bfloat16 [1024], P(('dp', 'seq')), may hold values from -4 to 4
- ln2_gain: bfloat16 [1024], P(('dp', 'seq')), may hold values from 0.5 to 1.5
- ln2_bias: bfloat16 [1024], P(('dp', 'seq')), may hold values from -4 to 4
- up_bias: bfloat16 [4096], P(('dp', 'seq')), may hold values from -6 to 6
- down_bias: bfloat16 [1024], P(('dp', 'seq')), may hold values from -4 to 4
Outputs:
- outputs: float32 [32, 1024, 1024], P('dp', 'seq')
- grad_inputs: float32 [32, 1024, 1024], P('dp', 'seq')
- grad_w_query: float32 [1024, 1024], P(('dp', 'seq'))
- grad_w_key: float32 [1024, 1024], P(('dp', 'seq'))
- grad_w_value: float32 [1024, 1024], P(('dp', 'seq'))
- grad_w_out: float32 [1024, 1024], P(('dp', 'seq'))
- grad_w_up: float32 [1024, 4096], P(('dp', 'seq'))
- grad_w_down: float32 [4096, 1024], P(('dp', 'seq'))
- grad_ln1_gain: float32 [1024], P(('dp', 'seq'))
- grad_ln1_bias: float32 [1024], P(('dp', 'seq'))
- grad_query_bias: float32 [1024], P(('dp', 'seq'))
- grad_value_bias: float32 [1024], P(('dp', 'seq'))
- grad_out_bias: float32 [1024], P(('dp', 'seq'))
- grad_ln2_gain: float32 [1024], P(('dp', 'seq'))
- grad_ln2_bias: float32 [1024], P(('dp', 'seq'))
- grad_up_bias: float32 [4096], P(('dp', 'seq'))
- grad_down_bias: float32 [1024], P(('dp', 'seq'))
The draws below stay inside these ranges and needn't reach their ends.
Inputs may be any that keep to these rules, and one draw needn't show every extreme that they name: `random_blocks`: for each sequence, head and query block: 3 different key blocks, none equal to the query block or to a block beside it, and none equal to 0 or 15.
All inputs are finite; a program needn't handle non-finite values.
Results may differ from the reference program's by a relative error of at most 0.013.
Values may be sent and summed in bfloat16 or wider, within the bound.
No kernel may reach another device: no remote copies, remote signals or barrier semaphores. Data moves between devices by JAX's collectives and lax.ppermute only.
A program may use at most 384 MiB of HBM per device.

```python
import jax
import jax.numpy as jnp
from jax import lax

D = 1024
HEADS = 16
FF = 4096
BLOCK = 64
RANDOM = 3
SEQ_BLOCKS = 16
SEQUENCES = 32
LENGTH = 1024


def draw_random_blocks(key, part):
    key = jax.random.fold_in(key, 11)
    column = jnp.arange(SEQ_BLOCKS, dtype=jnp.int32)
    row_ids = column[:, None]
    allowed = (column[None, :] >= 1) & (column[None, :] <= SEQ_BLOCKS - 2) & (jnp.abs(column[None, :] - row_ids) > 1)
    ranking = jax.random.randint(key, (SEQUENCES, HEADS, SEQ_BLOCKS, SEQ_BLOCKS), 0, 1 << 20, dtype=jnp.int32) * 128 + column
    ranking = jnp.where(allowed, ranking, -1)
    top_values, chosen = lax.top_k(ranking, RANDOM)
    return chosen.astype(jnp.int32)


def shard_levels(rng, extent, cuts, least, high):
    gain = 1.0
    for axis_at, shards_of in cuts:
        steps = jax.random.uniform(jax.random.fold_in(jax.random.fold_in(rng, 6), axis_at), (shards_of,), jnp.float32, least / len(cuts), high / len(cuts))
        gain = gain * jnp.repeat(jnp.exp(steps), extent[axis_at] // shards_of).reshape((-1,) + (1,) * (len(extent) - 1 - axis_at))
    return gain


def noise(own_key, extent, scale, reach, shards=(), kind=jnp.bfloat16):
    entries = scale * jax.random.normal(own_key, extent, jnp.float32)
    if shards:
        entries = entries * shard_levels(own_key, extent, shards, -0.22, 0.18)
    return jnp.clip(entries, -reach, reach).astype(kind)


def setup_inputs(seed: int = 0) -> dict:
    splits = jax.random.split(jax.random.key(seed), 19)
    inputs = noise(splits[0], (SEQUENCES, LENGTH, D), 1.0, 6.0, ((0, 16), (1, 2)), jnp.float32)
    grad_out = noise(splits[1], (SEQUENCES, LENGTH, D), 1.0, 6.0, ((0, 16), (1, 2)), jnp.float32)
    random_blocks = draw_random_blocks(jax.random.fold_in(splits[18], 71), 0)
    w_query = noise(splits[3], (D, D), D ** -0.5, 0.1875, ((0, 32),))
    w_key = noise(splits[4], (D, D), D ** -0.5, 0.1875, ((0, 32),))
    w_value = noise(splits[5], (D, D), D ** -0.5, 0.1875, ((0, 32),))
    w_out = noise(splits[6], (D, D), (D // (4 * BLOCK)) ** -0.5, 3.0, ((0, 32),))
    w_up = noise(splits[7], (D, FF), D ** -0.5, 0.1875, ((0, 32),))
    w_down = noise(splits[8], (FF, D), (FF // 2) ** -0.5, 0.125, ((0, 32),))
    ln1_gain = jnp.clip(1.0 + 0.1 * jax.random.normal(splits[9], (D,), jnp.float32), 0.5, 1.5).astype(jnp.bfloat16)
    ln1_bias = noise(splits[10], (D,), 0.3, 4.0, ((0, 32),))
    query_bias = noise(splits[11], (D,), 0.5, 6.0, ((0, 32),))
    value_bias = noise(splits[12], (D,), 0.1, 1.5, ((0, 32),))
    out_bias = noise(splits[13], (D,), 0.3, 4.0, ((0, 32),))
    ln2_gain = jnp.clip(1.0 + 0.1 * jax.random.normal(splits[14], (D,), jnp.float32), 0.5, 1.5).astype(jnp.bfloat16)
    ln2_bias = noise(splits[15], (D,), 0.3, 4.0, ((0, 32),))
    up_bias = noise(splits[16], (FF,), 0.5, 6.0, ((0, 32),))
    down_bias = noise(splits[17], (D,), 0.3, 4.0, ((0, 32),))
    return {"inputs": inputs, "grad_out": grad_out, "random_blocks": random_blocks, "w_query": w_query, "w_key": w_key, "w_value": w_value, "w_out": w_out, "w_up": w_up, "w_down": w_down, "ln1_gain": ln1_gain, "ln1_bias": ln1_bias, "query_bias": query_bias, "value_bias": value_bias, "out_bias": out_bias, "ln2_gain": ln2_gain, "ln2_bias": ln2_bias, "up_bias": up_bias, "down_bias": down_bias}


@jax.custom_vjp
def low(v):
    return lax.optimization_barrier(v.astype(jnp.bfloat16)).astype(jnp.float32)

@jax.custom_vjp
def low_back(v):
    return v

def low_keep(v):
    return (low(v), None)

def low_pass(kept, grad):
    return (grad,)

def back_keep(v):
    return (v, None)

def back_low(kept, grad):
    return (low(grad),)
low.defvjp(low_keep, low_pass)
low_back.defvjp(back_keep, back_low)
eps_norm = 1e-05
neg_fill = -1e+30
highest = lax.Precision.HIGHEST

def layer_norm(values, norm_gain, norm_shift):
    centre = values - lax.optimization_barrier(jnp.mean(values, axis=-1, keepdims=True))
    spread = lax.optimization_barrier(jnp.mean(centre * centre, axis=-1, keepdims=True))
    return centre * lax.rsqrt(spread + eps_norm) * norm_gain + norm_shift

def matmul(left, right):
    return jnp.dot(left, right, preferred_element_type=jnp.float32, precision=highest)

def attention(queries, key_rows, value_rows, random_ids):
    length, model_width = queries.shape
    head_dim = model_width // HEADS
    blocks = length // BLOCK
    score_scale = head_dim ** (-0.5)

    def split_heads(table):
        return table.reshape(blocks, BLOCK, HEADS, head_dim).transpose(2, 0, 1, 3)
    query_heads = split_heads(queries)
    key_heads = split_heads(key_rows)
    value_heads = split_heads(value_rows)
    block_ids = jnp.arange(blocks, dtype=jnp.int32)
    window = jnp.stack([block_ids - 1, block_ids, block_ids + 1], axis=1)
    inside = (window >= 1) & (window <= blocks - 2)
    window = jnp.clip(window, 0, blocks - 1)
    end_blocks = jnp.broadcast_to(jnp.array([0, blocks - 1], jnp.int32), (blocks, 2))
    fixed_slots = jnp.concatenate([end_blocks, window], axis=1)
    key_slots = jnp.concatenate([jnp.broadcast_to(fixed_slots[None], (HEADS, blocks, 5)), random_ids.astype(jnp.int32)], axis=2)
    key_valid = jnp.concatenate([jnp.ones((blocks, 2), jnp.bool_), inside, jnp.ones((blocks, random_ids.shape[2]), jnp.bool_)], axis=1)
    key_valid = jnp.repeat(key_valid, BLOCK, axis=1)
    head_index = jnp.arange(HEADS)[:, None, None]
    slot_count = key_slots.shape[2]
    key_picked = key_heads[head_index, key_slots].reshape(HEADS, blocks, slot_count * BLOCK, head_dim)
    value_picked = value_heads[head_index, key_slots].reshape(HEADS, blocks, slot_count * BLOCK, head_dim)
    raw_scores = jnp.einsum('hqid,hqkd->hqik', query_heads, key_picked, precision=highest)
    scores = jnp.where(key_valid[None, :, None, :], low_back(raw_scores) * score_scale, neg_fill)
    attn_prob = low(jax.nn.softmax(scores, axis=-1))
    sparse_out = jnp.einsum('hqik,hqkd->hqid', attn_prob, value_picked, precision=highest)
    edge_query = query_heads[:, jnp.array([0, blocks - 1], jnp.int32)]
    key_flat = key_heads.reshape(HEADS, length, head_dim)
    value_flat = value_heads.reshape(HEADS, length, head_dim)
    raw_edge = jnp.einsum('hgid,hkd->hgik', edge_query, key_flat, precision=highest)
    edge_prob = low(jax.nn.softmax(low_back(raw_edge) * score_scale, axis=-1))
    edge_out = jnp.einsum('hgik,hkd->hgid', edge_prob, value_flat, precision=highest)
    mixed_heads = sparse_out.at[:, 0].set(edge_out[:, 0]).at[:, blocks - 1].set(edge_out[:, 1])
    return mixed_heads.transpose(1, 2, 0, 3).reshape(length, model_width)

def encoder_layer(seq_rows, params, random_ids):
    w_query, w_key, w_value, w_out, w_up, w_down, ln1_gain, ln1_bias, query_bias, value_bias, out_bias, ln2_gain, ln2_bias, up_bias, down_bias = params
    normed = low(layer_norm(seq_rows, ln1_gain, ln1_bias))
    queries = low(low_back(matmul(normed, w_query) + query_bias))
    key_rows = low(low_back(matmul(normed, w_key)))
    value_rows = low(low_back(matmul(normed, w_value) + value_bias))
    mixed_low = low(low_back(attention(queries, key_rows, value_rows, random_ids)))
    middle = seq_rows + low_back(matmul(mixed_low, w_out) + out_bias)
    normed_two = low(layer_norm(middle, ln2_gain, ln2_bias))
    hidden_pre = low_back(matmul(normed_two, w_up) + up_bias)
    hidden_low = low(jax.nn.gelu(hidden_pre, approximate=True))
    return middle + low_back(matmul(hidden_low, w_down) + down_bias)

def reference(inputs, grad_out, random_blocks, w_query, w_key, w_value, w_out, w_up, w_down, ln1_gain, ln1_bias, query_bias, value_bias, out_bias, ln2_gain, ln2_bias, up_bias, down_bias):
    params = tuple((weight_arr.astype(jnp.float32) for weight_arr in (w_query, w_key, w_value, w_out, w_up, w_down, ln1_gain, ln1_bias, query_bias, value_bias, out_bias, ln2_gain, ln2_bias, up_bias, down_bias)))

    def per_sequence(totals, sequence):
        seq_rows, seq_grad, random_ids = sequence
        result, pullback = jax.vjp(lambda rows_in, params_in: encoder_layer(rows_in, params_in, random_ids), seq_rows, params)
        grad_rows, grad_params = pullback(seq_grad)
        return (jax.tree.map(jnp.add, totals, grad_params), (result, grad_rows))
    zeroes = jax.tree.map(jnp.zeros_like, params)
    totals, (results, grad_rows) = lax.scan(per_sequence, zeroes, (inputs, grad_out, random_blocks))
    return (results, grad_rows, totals[0], totals[1], totals[2], totals[3], totals[4], totals[5], totals[6], totals[7], totals[8], totals[9], totals[10], totals[11], totals[12], totals[13], totals[14])
```

```python
import jax
import jax.numpy as jnp
from jax import lax
from jax.experimental import pallas as pl
from jax.experimental.pallas import tpu as pltpu
from jax.sharding import PartitionSpec as P

HEADS = 16
BLOCK = 64
BOTH = ("dp", "seq")


eps_norm = 1e-05
neg_fill = -1e30


def layer_norm(values, norm_gain, norm_shift):
    centre = values - jnp.mean(values, axis=-1, keepdims=True)
    spread = jnp.mean(centre * centre, axis=-1, keepdims=True)
    return centre * lax.rsqrt(spread + eps_norm) * norm_gain + norm_shift


def gelu_tanh(values):
    return jax.nn.gelu(values, approximate=True)


def project(left, right):
    return jnp.dot(left, right, preferred_element_type=jnp.float32)


def project_back(grad_rows, weight):
    return lax.dot_general(
        grad_rows, weight, (((1,), (1,)), ((), ())), preferred_element_type=jnp.float32
    )


def weight_grad(left, grad_rows):
    return lax.dot_general(
        left, grad_rows, (((0,), (0,)), ((), ())), preferred_element_type=jnp.float32
    )


def column_sum(grad_rows):
    return jnp.sum(grad_rows, axis=0, dtype=jnp.float32)


def to_table(block_rows):
    block_count = block_rows.shape[0] // BLOCK
    head_dim = block_rows.shape[1] // HEADS
    shaped = block_rows.reshape(block_count, BLOCK, HEADS, head_dim)
    return shaped.transpose(2, 0, 1, 3).reshape(HEADS, block_count, BLOCK * head_dim)


def from_table(table):
    block_count = table.shape[1]
    head_dim = table.shape[2] // BLOCK
    shaped = table.reshape(HEADS, block_count, BLOCK, head_dim)
    return shaped.transpose(1, 2, 0, 3).reshape(block_count * BLOCK, HEADS * head_dim)


def key_layout(first_block, local_blocks, all_blocks, random_ids):
    query_ids = first_block + jnp.arange(local_blocks, dtype=jnp.int32)
    window = jnp.stack([query_ids - 1, query_ids, query_ids + 1], axis=1)
    inside = (window >= 1) & (window <= all_blocks - 2)
    window = jnp.clip(window, 0, all_blocks - 1)
    end_blocks = jnp.broadcast_to(jnp.array([0, all_blocks - 1], jnp.int32), (local_blocks, 2))
    fixed_slots = jnp.concatenate([end_blocks, window], axis=1)
    key_slots = jnp.concatenate(
        [jnp.broadcast_to(fixed_slots[None], (HEADS, local_blocks, 5)), random_ids], axis=2
    )
    key_valid = jnp.concatenate(
        [
            jnp.ones((local_blocks, 2), jnp.bool_),
            inside,
            jnp.ones((local_blocks, random_ids.shape[2]), jnp.bool_),
        ],
        axis=1,
    )
    return (key_slots, jnp.repeat(key_valid, BLOCK, axis=1))


def pick_blocks(table, key_slots):
    head_index = jnp.arange(HEADS)[:, None, None]
    picked = table[head_index, key_slots]
    head_dim = table.shape[2] // BLOCK
    return picked.reshape(HEADS, key_slots.shape[1], key_slots.shape[2] * BLOCK, head_dim)


def sparse_scores(query_heads, key_picked, key_valid, score_scale):
    raw_scores = jnp.einsum(
        "hqid,hqkd->hqik", query_heads, key_picked, preferred_element_type=jnp.float32
    )
    return jnp.where(key_valid[None, :, None, :], raw_scores * score_scale, neg_fill)


def dense_scores(query_block, key_flat, score_scale):
    return (
        jnp.einsum("hid,hkd->hik", query_block, key_flat, preferred_element_type=jnp.float32)
        * score_scale
    )


def dense_forward(query_block, key_flat, value_flat, score_scale):
    scores = dense_scores(query_block, key_flat, score_scale)
    top_score = jnp.max(scores, axis=-1, keepdims=True)
    expos = jnp.exp(scores - top_score)
    totals = jnp.sum(expos, axis=-1, keepdims=True)
    attn_prob = (expos / totals).astype(jnp.bfloat16)
    result = jnp.einsum("hik,hkd->ihd", attn_prob, value_flat, preferred_element_type=jnp.float32)
    return (result, (top_score + jnp.log(totals))[..., 0])


def softmax_back(attn_prob, grad_prob, score_scale):
    inner = jnp.sum(attn_prob * grad_prob, axis=-1, keepdims=True)
    return (attn_prob * (grad_prob - inner) * score_scale).astype(jnp.bfloat16)


def dense_backward(query_block, key_flat, value_flat, grad_block, log_total, score_scale):
    attn_prob = jnp.exp(dense_scores(query_block, key_flat, score_scale) - log_total[..., None])
    grad_prob = jnp.einsum(
        "ihd,hkd->hik", grad_block, value_flat, preferred_element_type=jnp.float32
    )
    grad_value = jnp.einsum(
        "hik,ihd->hkd",
        attn_prob.astype(jnp.bfloat16),
        grad_block,
        preferred_element_type=jnp.float32,
    )
    grad_scores = softmax_back(attn_prob, grad_prob, score_scale)
    grad_query = jnp.einsum(
        "hik,hkd->ihd", grad_scores, key_flat, preferred_element_type=jnp.float32
    )
    grad_key = jnp.einsum(
        "hik,hid->hkd", grad_scores, query_block, preferred_element_type=jnp.float32
    )
    return (grad_query, grad_key, grad_value)


def run_forward(weights, in_rows, random_ids):
    (
        w_query,
        w_key,
        w_value,
        w_out,
        w_up,
        w_down,
        ln1_gain,
        ln1_bias,
        query_bias,
        value_bias,
        out_bias,
        ln2_gain,
        ln2_bias,
        up_bias,
        down_bias,
    ) = weights
    normed, pull_first = jax.vjp(
        layer_norm, in_rows, ln1_gain.astype(jnp.float32), ln1_bias.astype(jnp.float32)
    )
    normed_low = normed.astype(jnp.bfloat16)
    queries = (project(normed_low, w_query) + query_bias.astype(jnp.float32)).astype(jnp.bfloat16)
    key_rows = project(normed_low, w_key).astype(jnp.bfloat16)
    value_rows = (project(normed_low, w_value) + value_bias.astype(jnp.float32)).astype(
        jnp.bfloat16
    )
    key_all, value_all = (
        lax.all_gather(key_rows, "seq", axis=0, tiled=True),
        lax.all_gather(value_rows, "seq", axis=0, tiled=True),
    )
    place = lax.axis_index("seq")
    ranks = lax.axis_size("seq")
    local_blocks = in_rows.shape[0] // BLOCK
    all_blocks = key_all.shape[0] // BLOCK
    head_dim = queries.shape[1] // HEADS
    score_scale = head_dim ** (-0.5)
    key_slots, key_valid = key_layout(place * local_blocks, local_blocks, all_blocks, random_ids)
    key_table = to_table(key_all)
    value_table = to_table(value_all)
    key_picked = pick_blocks(key_table, key_slots)
    value_picked = pick_blocks(value_table, key_slots)
    query_heads = to_table(queries).reshape(HEADS, local_blocks, BLOCK, head_dim)
    scores = sparse_scores(query_heads, key_picked, key_valid, score_scale)
    top_score = jnp.max(scores, axis=-1, keepdims=True)
    expos = jnp.exp(scores - top_score)
    totals = jnp.sum(expos, axis=-1, keepdims=True)
    prob_low = (expos / totals).astype(jnp.bfloat16)
    log_sparse = (top_score + jnp.log(totals))[..., 0]
    sparse_out = jnp.einsum(
        "hqik,hqkd->qihd", prob_low, value_picked, preferred_element_type=jnp.float32
    )
    is_edge = (place == 0) | (place == ranks - 1)
    edge_slot = jnp.where(place == 0, 0, local_blocks - 1)
    key_flat = key_table.reshape(HEADS, all_blocks * BLOCK, head_dim)
    value_flat = value_table.reshape(HEADS, all_blocks * BLOCK, head_dim)
    query_edge = lax.dynamic_index_in_dim(query_heads, edge_slot, 1, keepdims=False)
    edge_out, log_edge = lax.cond(
        is_edge,
        lambda: dense_forward(query_edge, key_flat, value_flat, score_scale),
        lambda: (
            jnp.zeros((BLOCK, HEADS, head_dim), jnp.float32),
            jnp.zeros((HEADS, BLOCK), jnp.float32),
        ),
    )
    current = lax.dynamic_index_in_dim(sparse_out, edge_slot, 0, keepdims=False)
    mixed_heads = lax.dynamic_update_index_in_dim(
        sparse_out, jnp.where(is_edge, edge_out, current), edge_slot, 0
    )
    mixed_low = mixed_heads.reshape(in_rows.shape[0], queries.shape[1]).astype(jnp.bfloat16)
    middle = in_rows + (project(mixed_low, w_out) + out_bias.astype(jnp.float32))
    normed_two, pull_second = jax.vjp(
        layer_norm, middle, ln2_gain.astype(jnp.float32), ln2_bias.astype(jnp.float32)
    )
    normed_two_low = normed_two.astype(jnp.bfloat16)
    hidden_pre = project(normed_two_low, w_up) + up_bias.astype(jnp.float32)
    hidden, pull_gelu = jax.vjp(gelu_tanh, hidden_pre)
    hidden_low = hidden.astype(jnp.bfloat16)
    result = middle + (project(hidden_low, w_down) + down_bias.astype(jnp.float32))
    saved = {
        "pull_first": pull_first,
        "pull_second": pull_second,
        "pull_gelu": pull_gelu,
        "normed_low": normed_low,
        "normed_two_low": normed_two_low,
        "hidden_low": hidden_low,
        "mixed_low": mixed_low,
        "query_heads": query_heads,
        "query_edge": query_edge,
        "key_picked": key_picked,
        "value_picked": value_picked,
        "key_flat": key_flat,
        "value_flat": value_flat,
        "key_slots": key_slots,
        "key_valid": key_valid,
        "log_sparse": log_sparse,
        "log_edge": log_edge,
        "is_edge": is_edge,
        "edge_slot": edge_slot,
    }
    return (saved, result)


def run_backward(weights, saved, grad_rows):
    (
        w_query,
        w_key,
        w_value,
        w_out,
        w_up,
        w_down,
        ln1_gain,
        ln1_bias,
        query_bias,
        value_bias,
        out_bias,
        ln2_gain,
        ln2_bias,
        up_bias,
        down_bias,
    ) = weights
    query_heads = saved["query_heads"]
    key_picked = saved["key_picked"]
    value_picked = saved["value_picked"]
    key_slots = saved["key_slots"]
    is_edge = saved["is_edge"]
    edge_slot = saved["edge_slot"]
    local_blocks = query_heads.shape[1]
    head_dim = query_heads.shape[3]
    all_blocks = saved["key_flat"].shape[1] // BLOCK
    score_scale = head_dim ** (-0.5)
    token_count = grad_rows.shape[0]
    grad_ff_low = grad_rows.astype(jnp.bfloat16)
    grad_w_down = weight_grad(saved["hidden_low"], grad_ff_low)
    grad_down_bias = column_sum(grad_ff_low)
    (grad_pre,) = saved["pull_gelu"](project_back(grad_ff_low, w_down))
    grad_pre_low = grad_pre.astype(jnp.bfloat16)
    grad_w_up = weight_grad(saved["normed_two_low"], grad_pre_low)
    grad_up_bias = column_sum(grad_pre_low)
    grad_normed_two = project_back(grad_pre_low, w_up)
    grad_middle, grad_ln2_gain, grad_ln2_bias = saved["pull_second"](grad_normed_two)
    grad_middle = grad_middle + grad_rows
    grad_attn_low = grad_middle.astype(jnp.bfloat16)
    grad_w_out = weight_grad(saved["mixed_low"], grad_attn_low)
    grad_out_bias = column_sum(grad_attn_low)
    grad_mixed = (
        project_back(grad_attn_low, w_out)
        .astype(jnp.bfloat16)
        .reshape(local_blocks, BLOCK, HEADS, head_dim)
    )
    block_ids = jnp.arange(local_blocks, dtype=jnp.int32)
    keep_sparse = jnp.where(is_edge & (block_ids == edge_slot), 0.0, 1.0).astype(jnp.bfloat16)
    grad_sparse = grad_mixed * keep_sparse[:, None, None, None]
    scores = sparse_scores(query_heads, key_picked, saved["key_valid"], score_scale)
    attn_prob = jnp.exp(scores - saved["log_sparse"][..., None])
    grad_prob = jnp.einsum(
        "qihd,hqkd->hqik", grad_sparse, value_picked, preferred_element_type=jnp.float32
    )
    grad_value_picked = jnp.einsum(
        "hqik,qihd->hqkd",
        attn_prob.astype(jnp.bfloat16),
        grad_sparse,
        preferred_element_type=jnp.float32,
    )
    grad_scores = softmax_back(attn_prob, grad_prob, score_scale)
    grad_query_sparse = jnp.einsum(
        "hqik,hqkd->qihd", grad_scores, key_picked, preferred_element_type=jnp.float32
    )
    grad_key_picked = jnp.einsum(
        "hqik,hqid->hqkd", grad_scores, query_heads, preferred_element_type=jnp.float32
    )
    head_index = jnp.arange(HEADS)[:, None, None]
    slot_count = key_slots.shape[2]
    table_shape = (HEADS, all_blocks, BLOCK * head_dim)
    grad_key_table = (
        jnp.zeros(table_shape, jnp.float32)
        .at[head_index, key_slots]
        .add(grad_key_picked.reshape(HEADS, local_blocks, slot_count, BLOCK * head_dim))
    )
    grad_value_table = (
        jnp.zeros(table_shape, jnp.float32)
        .at[head_index, key_slots]
        .add(grad_value_picked.reshape(HEADS, local_blocks, slot_count, BLOCK * head_dim))
    )
    grad_edge_block = lax.dynamic_index_in_dim(grad_mixed, edge_slot, 0, keepdims=False)
    flat_shape = (HEADS, all_blocks * BLOCK, head_dim)
    grad_query_edge, grad_key_edge, grad_value_edge = lax.cond(
        is_edge,
        lambda: dense_backward(
            saved["query_edge"],
            saved["key_flat"],
            saved["value_flat"],
            grad_edge_block,
            saved["log_edge"],
            score_scale,
        ),
        lambda: (
            jnp.zeros((BLOCK, HEADS, head_dim), jnp.float32),
            jnp.zeros(flat_shape, jnp.float32),
            jnp.zeros(flat_shape, jnp.float32),
        ),
    )
    grad_key_table = grad_key_table + grad_key_edge.reshape(table_shape)
    grad_value_table = grad_value_table + grad_value_edge.reshape(table_shape)
    grad_key_own, grad_value_own = (
        lax.psum_scatter(
            from_table(grad_key_table).astype(jnp.bfloat16), "seq", scatter_dimension=0, tiled=True
        ).astype(jnp.float32),
        lax.psum_scatter(
            from_table(grad_value_table).astype(jnp.bfloat16),
            "seq",
            scatter_dimension=0,
            tiled=True,
        ).astype(jnp.float32),
    )
    current = lax.dynamic_index_in_dim(grad_query_sparse, edge_slot, 0, keepdims=False)
    grad_query_all = lax.dynamic_update_index_in_dim(
        grad_query_sparse, current + grad_query_edge, edge_slot, 0
    )
    grad_query_low = grad_query_all.reshape(token_count, HEADS * head_dim).astype(jnp.bfloat16)
    grad_key_low = grad_key_own.astype(jnp.bfloat16)
    grad_value_low = grad_value_own.astype(jnp.bfloat16)
    normed_low = saved["normed_low"]
    grad_w_query = weight_grad(normed_low, grad_query_low)
    grad_w_key = weight_grad(normed_low, grad_key_low)
    grad_w_value = weight_grad(normed_low, grad_value_low)
    grad_query_bias = column_sum(grad_query_low)
    grad_value_bias = column_sum(grad_value_low)
    grad_normed = (
        project_back(grad_query_low, w_query)
        + project_back(grad_key_low, w_key)
        + project_back(grad_value_low, w_value)
    )
    grad_inputs, grad_ln1_gain, grad_ln1_bias = saved["pull_first"](grad_normed)
    grad_inputs = grad_inputs + grad_middle
    grads = (
        grad_w_query,
        grad_w_key,
        grad_w_value,
        grad_w_out,
        grad_w_up,
        grad_w_down,
        grad_ln1_gain,
        grad_ln1_bias,
        grad_query_bias,
        grad_value_bias,
        grad_out_bias,
        grad_ln2_gain,
        grad_ln2_bias,
        grad_up_bias,
        grad_down_bias,
    )
    return (grad_inputs, grads)


def on_device(inputs, grad_out, random_blocks, *shards):
    weights = tuple(lax.all_gather(part, BOTH, axis=0, tiled=True) for part in shards)

    def micro_step(totals, sequence):
        in_rows, grad_rows, random_ids = sequence
        saved, result = run_forward(weights, in_rows, random_ids)
        grad_in, grads = run_backward(weights, saved, grad_rows)
        return (tuple(left + right for left, right in zip(totals, grads)), (result, grad_in))

    initial = tuple(jnp.zeros(weight.shape, jnp.float32) for weight in weights)
    totals, (results, grads_in) = lax.scan(micro_step, initial, (inputs, grad_out, random_blocks))
    summed = tuple(
        lax.psum_scatter(total, BOTH, scatter_dimension=0, tiled=True) for total in totals
    )
    return (results, grads_in) + summed


F32, BF16 = jnp.float32, jnp.bfloat16
PAIR = 128
TIMES = dict(
    cast_far=1,
    join_first=2,
    join_up=2,
    join_plane=2,
    small_vectors=2,
    norm_project=2.2,
    attn_forward=5,
    out_norm=2,
    join_low=2.5,
    feed_forward=9,
    split_add=0.6,
    merge_add=3,
    middle_back=12,
    grad_wide=1.8,
    attn_backward=5,
    split_depth=1.5,
    input_back=4,
    pack_vectors=3,
    fill_far=1.5,
    last_add=1.5,
)
COST = 0.3 * 1e9
NEAR = tuple((dx, dc, dy) for dx in range(2) for dc in range(2) for dy in range(2))


def contract(left, right, left_dim, right_dim):
    return lax.dot_general(
        left, right, (((left_dim,), (right_dim,)), ((), ())), preferred_element_type=F32
    )


def held(*shape):
    zeros = (0,) * len(shape)
    return pl.BlockSpec(shape, lambda *_: zeros, pipeline_mode=pl.Buffered(1))


def whole_ref():
    return pl.BlockSpec(memory_space=pltpu.HBM)


def call(body, name, grid, in_specs, out_specs, out_shape, args, scratch=(), vmem=24, alias=None):
    spec = pltpu.PrefetchScalarGridSpec(
        num_scalar_prefetch=1,
        grid=grid,
        in_specs=in_specs,
        out_specs=out_specs,
        scratch_shapes=scratch,
    )
    return pl.pallas_call(
        body,
        grid_spec=spec,
        out_shape=out_shape,
        name=name,
        input_output_aliases=alias or {},
        compiler_params=pltpu.CompilerParams(vmem_limit_bytes=vmem << 20),
        cost_estimate=pl.CostEstimate(
            flops=int(TIMES[name] * grid[0] * COST), bytes_accessed=1, transcendentals=1
        ),
    )(*args)


def shape_of(kind, *shape):
    return jax.ShapeDtypeStruct(shape, kind)


def norm_parts(values):
    mean = jnp.mean(values, axis=-1, keepdims=True)
    centre = values - mean
    spread = jnp.mean(centre * centre, axis=-1, keepdims=True)
    scale = lax.rsqrt(spread + eps_norm)
    return centre * scale, scale


def norm_back(unit, scale, gain, grad):
    inner = grad * gain
    first = jnp.mean(inner, axis=-1, keepdims=True)
    second = jnp.mean(inner * unit, axis=-1, keepdims=True)
    return scale * (inner - first - unit * second)


def column(values):
    return jnp.sum(values, axis=0, keepdims=True)


def gelu_both(values):
    root = 2 * 0.7978845608028654
    cubic = root * 0.044715
    turn = -1.4426950408889634
    square = values * values
    power = jnp.exp2(jnp.minimum(values * (turn * root + (turn * cubic) * square), 126.0))
    part = pl.reciprocal(1.0 + power, approx=True)
    hidden = values * part
    return hidden, part + (hidden - hidden * part) * (root + (3 * cubic) * square)


def flip(value, bit):
    return 1 - value if bit else value


def parts_copies(place_ref, part_refs, weight, sems, start, size, into, chunk):
    copies = []
    for at, (dx, dc, dy) in enumerate(NEAR):
        spot = (slice(None), flip(place_ref[1], dx), flip(place_ref[2], dc), flip(place_ref[3], dy))
        copies.append(
            pltpu.make_async_copy(
                part_refs[at].at[:, :, pl.ds(start, size)],
                weight.at[spot + (slice(None), pl.ds(into, size))],
                sems.at[chunk, at],
            )
        )
    return copies


def weight_scratch(part, columns):
    depth, rows, _ = part.shape
    return pltpu.VMEM((depth, 2, 2, 2, rows, columns), BF16)


def flat(value):
    return value.reshape(-1, value.shape[-1])


def depth_copies(place_ref, part_refs, weight, sems):
    depth = weight.shape[0]
    copies = []
    for step in range(depth):
        there = lax.rem(place_ref[0] + depth - step, depth)
        for dc in range(2):
            core = flip(place_ref[2], dc)
            copies.append(
                pltpu.make_async_copy(
                    part_refs[2 * step + dc], weight.at[there, :, core], sems.at[there, dc]
                )
            )
    return copies


def depth_wait(place_ref, part_refs, weight, sems, at):
    for dc in range(2):
        core = flip(place_ref[2], dc)
        pltpu.make_async_copy(part_refs[dc], weight.at[at, :, core], sems.at[at, dc]).wait()


def own_spec(step, width, parts):
    return pl.BlockSpec((1, step, width), lambda i, p: (p[3], jnp.minimum(i, parts - 1), 0))


def far_spec(step, width, parts):
    return pl.BlockSpec((step, width), lambda i, _: (jnp.maximum(i - parts, 0), 0))


def join(place, blocks, moves, shapes, name):
    def body(place_ref, *refs):
        ins, outs = refs[: len(blocks)], refs[len(blocks) :]
        for i, cut, j, spot in moves:
            outs[j][spot(place_ref)] = ins[i][cut]

    return call(
        body,
        name,
        (1,),
        [held(*block.shape) for block in blocks],
        [held(*shape) for shape in shapes],
        [shape_of(BF16, *shape) for shape in shapes],
        (place,) + tuple(blocks),
        vmem=10,
    )


def join_low(place, grad_out, far):
    half, width = far.shape

    def body(place_ref, own_ref, far_ref, low_ref, sum_ref):
        low = own_ref[0].astype(BF16)
        low_ref[:half] = low
        low_ref[half:] = far_ref[...]
        sum_ref[...] = column(low.astype(F32)) + column(far_ref[...].astype(F32))

    return call(
        body,
        "join_low",
        (1,),
        [
            pl.BlockSpec((1, half, width), lambda i, p: (p[3], 0, 0), pipeline_mode=pl.Buffered(1)),
            held(half, width),
        ],
        [held(2 * half, width), held(1, width)],
        [shape_of(BF16, 2 * half, width), shape_of(F32, 1, width)],
        (place, grad_out, far),
        vmem=12,
    )


def cast_far(place, values):
    _, half, width = values.shape
    step = half // 2

    def body(place_ref, values_ref, out_ref):
        out_ref[...] = values_ref[0].astype(BF16)

    return call(
        body,
        "cast_far",
        (half // step,),
        [pl.BlockSpec((1, step, width), lambda i, p: (1 - p[3], i, 0))],
        pl.BlockSpec((step, width), lambda i, _: (i, 0)),
        shape_of(BF16, half, width),
        (place, values),
        vmem=6,
    )


def norm_project(place, inputs, far, gain, shift, left, right, bias):
    half, width = far.shape
    columns = bias.shape[1]
    step = 512
    left_steps = left[0].shape[-1] // step
    steps = columns // step
    sub = 256

    def body(place_ref, own_ref, far_ref, gain_ref, shift_ref, bias_ref, *refs):
        left_refs, right_refs = refs[:8], refs[8:16]
        normed_ref, out_ref, weight, sems = refs[16:]
        at = pl.program_id(0)

        def copies(chunk):
            refs, start = (left_refs, chunk) if chunk < left_steps else (right_refs, chunk - left_steps)
            return parts_copies(place_ref, refs, weight, sems, start * step, step, chunk * step, chunk)

        @pl.when(at == 0)
        def _():
            for chunk in range(steps):
                for copy in copies(chunk):
                    copy.start()
            for start, rows in ((0, own_ref[0]), (half, far_ref[...])):
                unit, _ = norm_parts(rows.astype(F32))
                normed_ref[start : start + half, :] = (
                    unit * gain_ref[...] + shift_ref[...]
                ).astype(BF16)

        for chunk in range(steps):
            @pl.when(at == chunk)
            def _():
                for copy in copies(chunk):
                    copy.wait()

        cut = pl.ds(pl.multiple_of(at * step, step), step)
        part = flat(weight[:, :, :, :, :, cut])
        for start in range(0, 2 * half, sub):
            result = contract(normed_ref[start : start + sub], part, 1, 0) + bias_ref[...]
            out_ref[start : start + sub] = result.astype(BF16)

    return call(
        body,
        "norm_project",
        (steps,),
        [
            pl.BlockSpec((1, half, width), lambda i, p: (p[3], 0, 0), pipeline_mode=pl.Buffered(1)),
            held(half, width),
            held(1, width),
            held(1, width),
            pl.BlockSpec((1, step), lambda i, _: (0, i)),
        ]
        + [whole_ref()] * 16,
        [
            pl.BlockSpec((2 * half, width), lambda i, _: (0, 0)),
            pl.BlockSpec((2 * half, step), lambda i, _: (0, i)),
        ],
        [shape_of(BF16, 2 * half, width), shape_of(BF16, 2 * half, columns)],
        (place, inputs, far, gain, shift, bias) + tuple(left) + tuple(right),
        scratch=[weight_scratch(left[0], columns), pltpu.SemaphoreType.DMA((steps, 8))],
        vmem=56,
    )


def out_norm(place, mixed, right, bias, inputs, far, gain, shift, down_bias):
    half, width = far.shape
    step = 256
    parts = half // step

    def body(place_ref, mixed_ref, bias_ref, own_ref, far_ref, gain_ref, shift_ref, down_ref, *refs):
        right_refs = refs[:8]
        middle_ref, normed_ref, start_ref, weight, sems = refs[8:]

        @pl.when(pl.program_id(0) == 0)
        def _():
            copies = parts_copies(place_ref, right_refs, weight, sems, width, width, 0, 0)
            for copy in copies:
                copy.start()
            for copy in copies:
                copy.wait()

        near = pl.program_id(0) < parts
        rows = jnp.where(near, own_ref[0], far_ref[...].astype(F32))
        middle = rows + (contract(mixed_ref[...], flat(weight[...]), 1, 0) + bias_ref[...])
        middle_ref[...] = middle
        start_ref[...] = middle + down_ref[...]
        unit, _ = norm_parts(middle)
        normed_ref[...] = (unit * gain_ref[...] + shift_ref[...]).astype(BF16)

    here = pl.BlockSpec((step, width), lambda i, _: (i, 0))
    return call(
        body,
        "out_norm",
        (2 * parts,),
        [
            here,
            held(1, width),
            own_spec(step, width, parts),
            far_spec(step, width, parts),
            held(1, width),
            held(1, width),
            held(1, width),
        ]
        + [whole_ref()] * 8,
        [here, here, here],
        [shape_of(F32, 2 * half, width), shape_of(BF16, 2 * half, width), shape_of(F32, 2 * half, width)],
        (place, mixed, bias, inputs, far, gain, shift, down_bias) + tuple(right),
        scratch=[weight_scratch(right[0], width), pltpu.SemaphoreType.DMA((1, 8))],
        vmem=56,
    )


def fill_far(place, partial, base, delta):
    _, half, width = base.shape
    step = 256

    def body(place_ref, partial_ref, base_ref, delta_ref, out_ref):
        out_ref[0] = base_ref[0] + delta_ref[...].astype(F32)

    there = pl.BlockSpec((1, step, width), lambda i, p: (1 - p[3], i, 0))
    return call(
        body,
        "fill_far",
        (half // step,),
        [whole_ref(), there, pl.BlockSpec((step, width), lambda i, _: (i, 0))],
        there,
        shape_of(F32, 2, half, width),
        (place, partial, base, delta),
        alias={1: 0},
        vmem=8,
    )


def grad_wide(place, left, rights, rows, pieces, before=()):
    tokens, tall = left.shape
    width = rights[0].shape[1]
    step = 512
    each = width // step
    steps = each * len(rights)
    group = 4 * rows
    per = steps // pieces
    total = width * len(rights)

    def body(place_ref, left_ref, *refs):
        right_refs = refs[: len(rights)]
        outs = refs[len(rights) + len(before) : -1]
        sums = refs[-1]
        at = pl.program_id(0)
        for which, right_ref in enumerate(right_refs):
            @pl.when(at // each == which)
            def _():
                result = contract(left_ref[...], right_ref[...], 0, 0)
                sums[...] = result.reshape(tall // group, 2, group // 2, step)

        for piece in range(pieces):
            @pl.when(at // per == piece)
            def _():
                outs[2 * piece][...] = sums[:, place_ref[2]].astype(BF16)
                outs[2 * piece + 1][...] = sums[:, 1 - place_ref[2]].astype(BF16)

    def right_at(which):
        return lambda i, _: (0, jnp.clip(i - which * each, 0, each - 1))

    wide_total = before[0].shape[-1] if before else total // pieces
    start = (wide_total - total // pieces) // step

    def out_at(piece):
        return lambda i, _: (0, 0, start + jnp.clip(i - piece * per, 0, per - 1))

    return call(
        body,
        "grad_wide",
        (steps,),
        [held(tokens, tall)]
        + [pl.BlockSpec((tokens, step), right_at(i)) for i in range(len(rights))]
        + [whole_ref()] * len(before),
        [
            pl.BlockSpec((tall // group, group // 2, step), out_at(piece))
            for piece in range(pieces)
            for _ in range(2)
        ],
        [shape_of(BF16, tall // group, group // 2, wide_total)] * (2 * pieces),
        (place, left) + tuple(rights) + tuple(before),
        scratch=[pltpu.VMEM((tall // group, 2, group // 2, step), F32)],
        vmem=20,
        alias={2 + len(rights) + i: i for i in range(len(before))},
    )


def feed_forward(place, first, count, depth, normed, grad_low, up_parts, down_parts, up_bias, far, state, wide):
    tokens, width = normed.shape
    half = tokens // 2
    hidden_width = up_bias.shape[1]
    step = hidden_width // (2 * depth)
    steps = 2 * count
    rows = down_parts[0].shape[-2]
    group = width // (2 * depth)
    last = first + count == depth
    sub = 256
    columns, offset, before = wide
    offset = offset // step

    def body(place_ref, normed_ref, grad_ref, bias_ref, far_ref, out_in, back_in, *refs):
        up_refs, down_refs = refs[:8], refs[8 : 8 + 2 * depth]
        refs = refs[8 + 2 * depth + len(before) :]
        tall_mine, tall_other, wide_mine, wide_other, sum_ref, back_ref = refs[:6]
        if last:
            out_ref, delta_ref = refs[6:8]
            total, refs = refs[8], refs[9:]
        else:
            total, refs = refs[6], refs[7:]
        up, down, up_sems, down_sems, hidden, before_low, tall_sums, wide_sums = refs
        at = pl.program_id(0)
        slot = lax.rem(at, 2)

        def up_copies(index, into):
            start = pl.multiple_of((2 * first + index) * step, step)
            copies = []
            for which, (dx, dc, dy) in enumerate(NEAR):
                x, c, y = flip(place_ref[1], dx), flip(place_ref[2], dc), flip(place_ref[3], dy)
                copies.append(
                    pltpu.make_async_copy(
                        up_refs[which].at[:, :, pl.ds(start, step)],
                        up.at[into, :, x, c, y],
                        up_sems.at[into, which],
                    )
                )
            return copies

        def down_copies(index, into, turn):
            x = lax.rem(index, 2)
            return [
                pltpu.make_async_copy(
                    down_refs[2 * turn + dc].at[x],
                    down.at[into, flip(place_ref[2], dc)],
                    down_sems.at[into, dc],
                )
                for dc in range(2)
            ]

        def begin(index, into):
            for copy in up_copies(index, into):
                copy.start()
            away = lax.rem(place_ref[0] + depth - first - index // 2, depth)
            for turn in range(depth):
                @pl.when(away == turn)
                def _():
                    for copy in down_copies(index, into, turn):
                        copy.start()

        @pl.when(at == 0)
        def _():
            begin(0, 0)
            total[...] = out_in[...]
            back_ref[...] = back_in[...] if first else jnp.zeros((tokens, width), F32)

        @pl.when(at + 1 < steps)
        def _():
            begin(at + 1, 1 - slot)

        for copy in up_copies(at, slot) + down_copies(at, slot, 0):
            copy.wait()
        up_part, down_part = flat(up[slot]), flat(down[slot])
        bias_sum = jnp.zeros((1, step), F32)
        for start in range(0, tokens, sub):
            cut = slice(start, start + sub)
            hidden_part, slope = gelu_both(contract(normed_ref[cut], up_part, 1, 0) + bias_ref[...])
            hidden_low = hidden_part.astype(BF16)
            hidden[cut] = hidden_low
            total[cut] += contract(hidden_low, down_part, 1, 0)
            low = (contract(grad_ref[cut], down_part, 1, 1) * slope).astype(BF16)
            before_low[cut] = low
            bias_sum += column(low.astype(F32))
            back_ref[cut] += contract(low, up_part, 1, 1)
        sum_ref[...] = bias_sum
        tall_sums[...] = contract(hidden[...], grad_ref[...], 0, 0).reshape(tall_sums.shape)
        tall_mine[0] = tall_sums[place_ref[2]].astype(BF16)
        tall_other[0] = tall_sums[1 - place_ref[2]].astype(BF16)
        wide_sums[...] = contract(normed_ref[...], before_low[...], 0, 0).reshape(wide_sums.shape)
        wide_mine[...] = wide_sums[:, place_ref[2]].astype(BF16)
        wide_other[...] = wide_sums[:, 1 - place_ref[2]].astype(BF16)

        if last:
            @pl.when(at == steps - 1)
            def _():
                out_ref[0] = total[:half]
                delta_ref[...] = (total[half:] - far_ref[...].astype(F32)).astype(BF16)

    full = held(tokens, width)
    tall = pl.BlockSpec((1, 2 * rows, width), lambda i, _: (i, 0, 0))
    broad = pl.BlockSpec((2 * depth, group // 2, step), lambda i, _: (0, 0, offset + i))
    bias_spec = pl.BlockSpec((1, step), lambda i, _: (0, 2 * first + i))
    out_specs = [tall, tall, broad, broad, pl.BlockSpec((1, step), lambda i, _: (0, i)), full]
    out_shape = [shape_of(BF16, steps, 2 * rows, width)] * 2
    out_shape += [shape_of(BF16, 2 * depth, group // 2, columns)] * 2
    out_shape += [shape_of(F32, 1, steps * step), shape_of(F32, tokens, width)]
    scratch = [
        pltpu.VMEM((2, depth, 2, 2, 2, group // 4, step), BF16),
        pltpu.VMEM((2, 2, 2, rows, width), BF16),
        pltpu.SemaphoreType.DMA((2, 8)),
        pltpu.SemaphoreType.DMA((2, 2)),
        pltpu.VMEM((tokens, step), BF16),
        pltpu.VMEM((tokens, step), BF16),
        pltpu.VMEM((2, 2 * rows, width), F32),
        pltpu.VMEM((2 * depth, 2, group // 2, step), F32),
    ]
    if last:
        out_specs += [
            pl.BlockSpec((1, half, width), lambda i, p: (p[3], 0, 0), pipeline_mode=pl.Buffered(1)),
            held(half, width),
        ]
        out_shape += [shape_of(F32, 2, half, width), shape_of(BF16, half, width)]
        scratch = [pltpu.VMEM((tokens, width), F32)] + scratch
    else:
        out_specs += [full]
        out_shape += [shape_of(F32, tokens, width)]
    args = (place, normed, grad_low, up_bias, far) + tuple(state) + tuple(up_parts) + tuple(down_parts)
    alias = {len(args) + i: 2 + i for i in range(len(before))}
    return call(
        body,
        "feed_forward",
        (steps,),
        [full, full, bias_spec, held(half, width), full, full]
        + [whole_ref()] * (8 + 2 * depth + len(before)),
        out_specs,
        out_shape,
        args + tuple(before),
        scratch=scratch,
        vmem=50,
        alias=alias,
    )


def middle_back(place, grad_normed, middle, gain, grad_out, far, right):
    half, width = far.shape
    step = 256
    parts = half // step

    def body(place_ref, grad_ref, middle_ref, gain_ref, own_ref, far_ref, *refs):
        right_refs = refs[:8]
        total_ref, low_ref, mixed_ref = refs[8:11]
        sums = refs[11:14]
        weight, sems = refs[14:]
        at = pl.program_id(0)

        def copies():
            return parts_copies(place_ref, right_refs, weight, sems, width, width, 0, 0)

        @pl.when(at == 0)
        def _():
            for copy in copies():
                copy.start()
            for ref in sums:
                ref[...] = jnp.zeros_like(ref)

        grad_normed = grad_ref[...]
        unit, scale = norm_parts(middle_ref[...])
        out_grad = jnp.where(at < parts, own_ref[0], far_ref[...].astype(F32))
        total = out_grad + norm_back(unit, scale, gain_ref[...], grad_normed)
        total_ref[...] = total
        low = total.astype(BF16)
        low_ref[...] = low
        sums[0][...] += column(grad_normed * unit)
        sums[1][...] += column(grad_normed)
        sums[2][...] += column(low.astype(F32))

        @pl.when(at == 0)
        def _():
            for copy in copies():
                copy.wait()

        mixed_ref[...] = contract(low, flat(weight[...]), 1, 1).astype(BF16)

    here = pl.BlockSpec((step, width), lambda i, _: (i, 0))
    vector = pl.BlockSpec((1, width), lambda i, _: (0, 0))
    tokens = 2 * half
    return call(
        body,
        "middle_back",
        (2 * parts,),
        [here, here, held(1, width), own_spec(step, width, parts), far_spec(step, width, parts)]
        + [whole_ref()] * 8,
        [here, here, here, vector, vector, vector],
        [shape_of(F32, tokens, width), shape_of(BF16, tokens, width), shape_of(BF16, tokens, width)]
        + [shape_of(F32, 1, width)] * 3,
        (place, grad_normed, middle, gain, grad_out, far) + tuple(right),
        scratch=[weight_scratch(right[0], width), pltpu.SemaphoreType.DMA((1, 8))],
        vmem=24,
    )


def input_back(place, grads, left, right, inputs, far, gain, middle_grad, far_grad):
    half, width = far.shape
    step = 256
    parts = half // step

    def body(
        place_ref, query_ref, key_ref, value_ref, own_ref, far_ref, gain_ref, middle_ref, far_grad_ref, *refs
    ):
        left_refs, right_refs = refs[:8], refs[8:16]
        out_ref, delta_ref = refs[16:18]
        sums = refs[18:22]
        gain_sum_ref, shift_sum_ref, query_sum_ref, value_sum_ref = sums
        weight, sems = refs[22:]
        at = pl.program_id(0)

        def copies():
            result = []
            for chunk, part_refs in enumerate((left_refs, left_refs, right_refs)):
                result += parts_copies(
                    place_ref, part_refs, weight, sems, (chunk % 2) * width, width, chunk * width, chunk
                )
            return result

        @pl.when(at == 0)
        def _():
            for copy in copies():
                copy.start()
            for ref in sums:
                ref[...] = jnp.zeros_like(ref)

        @pl.when(at == 0)
        def _():
            for copy in copies():
                copy.wait()

        def part(chunk):
            return flat(weight[:, :, :, :, :, chunk * width : (chunk + 1) * width])

        grad_normed = contract(query_ref[...], part(0), 1, 1)
        grad_normed += contract(key_ref[...], part(1), 1, 1)
        grad_normed += contract(value_ref[...], part(2), 1, 1)
        rows = jnp.where(at < parts, own_ref[0], far_ref[...].astype(F32))
        unit, scale = norm_parts(rows)
        gain_sum_ref[...] += column(grad_normed * unit)
        shift_sum_ref[...] += column(grad_normed)
        query_sum_ref[...] += column(query_ref[...].astype(F32))
        value_sum_ref[...] += column(value_ref[...].astype(F32))
        result = middle_ref[...] + norm_back(unit, scale, gain_ref[...], grad_normed)

        @pl.when(at < parts)
        def _():
            out_ref[0] = result

        @pl.when(at >= parts)
        def _():
            delta_ref[...] = (result - far_grad_ref[...].astype(F32)).astype(BF16)

    here = pl.BlockSpec((step, width), lambda i, _: (i, 0))
    vector = pl.BlockSpec((1, width), lambda i, _: (0, 0))
    return call(
        body,
        "input_back",
        (2 * parts,),
        [
            here,
            here,
            here,
            own_spec(step, width, parts),
            far_spec(step, width, parts),
            held(1, width),
            here,
            far_spec(step, width, parts),
        ]
        + [whole_ref()] * 16,
        [own_spec(step, width, parts), far_spec(step, width, parts), vector, vector, vector, vector],
        [shape_of(F32, 2, half, width), shape_of(BF16, half, width)] + [shape_of(F32, 1, width)] * 4,
        (place,) + tuple(grads) + (inputs, far, gain, middle_grad, far_grad) + tuple(left) + tuple(right),
        scratch=[weight_scratch(left[0], 3 * width), pltpu.SemaphoreType.DMA((3, 8))],
        vmem=56,
    )


def split_add(place, mine, came, spot):
    groups, _, rows, columns = mine.shape

    def body(place_ref, mine_ref, came_ref, sent_ref, kept_ref):
        for ref, at in ((sent_ref, 1 - place_ref[spot]), (kept_ref, place_ref[spot])):
            ref[0] = (mine_ref[0, at].astype(F32) + came_ref[0, at].astype(F32)).astype(BF16)

    block = pl.BlockSpec((1, 2, rows, columns), lambda i, _: (i, 0, 0, 0))
    out = pl.BlockSpec((1, rows, columns), lambda i, _: (i, 0, 0))
    return call(
        body,
        "split_add",
        (groups,),
        [block, block],
        [out, out],
        [shape_of(BF16, groups, rows, columns)] * 2,
        (place, mine, came),
        vmem=8,
    )


def split_depth(place, pairs):
    depth, rows = pairs[0][0].shape[:2]
    widths = [mine.shape[2] for mine, _ in pairs]
    total = sum(widths)

    def body(place_ref, *refs):
        outs = refs[2 * len(pairs) :]
        for step, ref in enumerate(outs):
            at = lax.rem(place_ref[0] + step, depth)
            start = 0
            for which, width in enumerate(widths):
                value = refs[2 * which][at].astype(F32) + refs[2 * which + 1][at].astype(F32)
                ref[:, start : start + width] = value.astype(ref.dtype)
                start += width

    return call(
        body,
        "split_depth",
        (1,),
        [held(depth, rows, width) for width in widths for _ in range(2)],
        [held(rows, total)] * depth,
        [shape_of(F32, rows, total)] + [shape_of(BF16, rows, total)] * (depth - 1),
        (place,) + tuple(value for pair in pairs for value in pair),
        vmem=8,
    )


def last_add(place, own, came, cuts):
    rows, total = own.shape

    def body(place_ref, own_ref, *refs):
        value = own_ref[...]
        for ref in refs[: len(came)]:
            value = value + ref[...].astype(F32)
        for ref, (start, stop) in zip(refs[len(came) :], cuts):
            ref[...] = value[:, start:stop]

    return call(
        body,
        "last_add",
        (1,),
        [held(rows, total)] * (1 + len(came)),
        [held(rows, stop - start) for start, stop in cuts],
        [shape_of(F32, rows, stop - start) for start, stop in cuts],
        (place, own) + tuple(came),
        vmem=6,
    )


def spread_rows(count, per, size, row):
    span = size * per
    lane = lax.broadcasted_iota(jnp.int32, (per, count * span), 1)
    line = lax.broadcasted_iota(jnp.int32, (per, count * span), 0)
    return jnp.where(lane % span == row * per + line, 1.0, 0.0)


def chosen_rows(count, span):
    lane = lax.broadcasted_iota(jnp.int32, (count, count * span), 1)
    line = lax.broadcasted_iota(jnp.int32, (count, count * span), 0)
    return lane // span == line


def small_vectors(place, right, start, sizes, per):
    depth, rows, _ = right[0].shape
    count = depth * 8

    def body(place_ref, *refs):
        part_refs, outs, held_rows = refs[:8], refs[8:-1], refs[-1]
        for at, (dx, dc, dy) in enumerate(NEAR):
            x, c, y = flip(place_ref[1], dx), flip(place_ref[2], dc), flip(place_ref[3], dy)
            held_rows[:, x, c, y] = part_refs[at][...].astype(F32)
        table = held_rows[...].reshape(count, rows, PAIR)
        at = 0
        for ref, size in zip(outs, sizes):
            chosen = chosen_rows(count, size * per)
            line = jnp.zeros((1, count * size * per), F32)
            for row in range(size):
                spread = spread_rows(count, per, size, row).astype(BF16)
                wide = contract(table[:, at + row, :per].astype(BF16), spread, 1, 0)
                line += column(jnp.where(chosen, wide, 0.0))
            at += size
            ref[...] = line

    return call(
        body,
        "small_vectors",
        (1,),
        [pl.BlockSpec((depth, rows, PAIR), lambda i, _: (0, 0, start // PAIR))] * 8,
        [held(1, count * size * per) for size in sizes],
        [shape_of(F32, 1, count * size * per) for size in sizes],
        (place,) + tuple(right),
        scratch=[pltpu.VMEM((depth, 2, 2, 2, rows, PAIR), F32)],
        vmem=12,
    )


def pack_vectors(place, vectors, sizes, per):
    count = vectors[0].shape[1] // (sizes[0] * per)

    def body(place_ref, *refs):
        out = refs[-1]
        at = 0
        for ref, size in zip(refs[:-1], sizes):
            chosen = chosen_rows(count, size * per)
            wide = jnp.where(chosen, jnp.broadcast_to(ref[...], (count, count * size * per)), 0.0)
            for row in range(size):
                out[at + row] = lax.dot_general(
                    wide,
                    spread_rows(count, per, size, row),
                    (((1,), (1,)), ((), ())),
                    precision=lax.Precision.HIGHEST,
                    preferred_element_type=F32,
                )
            at += size

    return call(
        body,
        "pack_vectors",
        (1,),
        [held(*vector.shape) for vector in vectors],
        held(sum(sizes), count, per),
        shape_of(F32, sum(sizes), count, per),
        (place,) + tuple(vectors),
        vmem=12,
    )


def merge_add(place, mine, came, spot):
    counts = [part.shape[0] for part in mine]
    _, _, rows, columns = mine[0].shape

    def body(place_ref, *refs):
        sent_ref, kept_ref = refs[2 * len(mine) :]
        start = 0
        for which, count in enumerate(counts):
            for ref, at in ((sent_ref, 1 - place_ref[spot]), (kept_ref, place_ref[spot])):
                total = refs[which][:, at].astype(F32) + refs[len(mine) + which][:, at].astype(F32)
                ref[start : start + count] = total.astype(BF16)
            start += count

    shape = (sum(counts), rows, columns)
    return call(
        body,
        "merge_add",
        (1,),
        [held(*part.shape) for part in mine + came],
        [held(*shape)] * 2,
        [shape_of(BF16, *shape)] * 2,
        (place,) + tuple(mine) + tuple(came),
        vmem=12,
    )


def attn_forward_kernel(q_ref, k_ref, v_ref, bias_ref, prob_ref, mixed_ref, total_ref):
    tokens, lanes = q_ref.shape
    half = lanes // 2
    lane = lax.broadcasted_iota(jnp.int32, (tokens, lanes), 1)
    block = lax.broadcasted_iota(jnp.int32, (tokens, lanes), 0) // BLOCK
    scale = half ** -0.5
    q = q_ref[...].astype(jnp.float32) * scale
    k = k_ref[...].astype(jnp.float32)
    v = v_ref[...].astype(jnp.float32)
    sides = []
    for head in range(2):
        own = (lane >= half) if head else (lane < half)
        first = 0 if head else half
        bias = jnp.broadcast_to(bias_ref[head][:, None, :], (tokens // BLOCK, BLOCK, lanes)).reshape(tokens, lanes)
        q_ext = jnp.where(own, q, jnp.where(lane - first == block, 1.0, 0.0)).astype(jnp.bfloat16)
        k_ext = jnp.where(own, k, bias).astype(jnp.bfloat16)
        v_ext = jnp.where(own, v, 1.0).astype(jnp.bfloat16)
        sides.append((q_ext, k_ext, v_ext))
    rows = 256
    low_lane = lax.broadcasted_iota(jnp.int32, (rows, lanes), 1) < half
    for start in range(0, tokens, rows):
        sums = []
        for head, (q_ext, k_ext, v_ext) in enumerate(sides):
            scores = contract(q_ext[start:start + rows], k_ext, 1, 1)
            top = jnp.max(scores, axis=1, keepdims=True)
            prob = jnp.exp(scores - top).astype(jnp.bfloat16)
            prob_ref[head, start:start + rows, :] = prob
            sums.append(contract(prob, v_ext, 1, 0))
        result = jnp.where(low_lane, sums[0], sums[1])
        totals = pltpu.roll(jnp.where(low_lane, sums[1], sums[0]), half, 1)
        mixed_ref[start:start + rows, :] = (result / totals).astype(jnp.bfloat16)
        total_ref[start:start + rows, :] = totals

def attn_backward_kernel(q_ref, k_ref, v_ref, prob_ref, mixed_ref, total_ref, grad_ref, dq_ref, dk_ref, dv_ref):
    tokens, lanes = q_ref.shape
    half = lanes // 2
    scale = half ** -0.5
    lane = lax.broadcasted_iota(jnp.int32, (tokens, lanes), 1)
    grad = grad_ref[...].astype(jnp.float32) / total_ref[...]
    inner = grad * mixed_ref[...].astype(jnp.float32)
    grad_low = grad.astype(jnp.bfloat16)
    q_turned = q_ref[...].T
    grad_turned = grad_low.T
    v = v_ref[...].astype(jnp.float32)
    k = k_ref[...]
    rows = 256
    low_lane = lax.broadcasted_iota(jnp.int32, (rows, lanes), 1) < half
    dq = [[None, None] for _ in range(tokens // rows)]
    dk, dv = [], []
    for head in range(2):
        own = (lane >= half) if head else (lane < half)
        first = 0 if head else half
        minus = -jnp.sum(jnp.where(own, inner, 0.0), axis=1, keepdims=True)
        high = minus.astype(jnp.bfloat16).astype(jnp.float32)
        grad_ext = jnp.where(own, grad, jnp.where(lane == first, high, jnp.where(lane == first + 1, minus - high, 0.0))).astype(jnp.bfloat16)
        v_ext = jnp.where(own, v, jnp.where(lane - first < 2, 1.0, 0.0)).astype(jnp.bfloat16)
        dk_sum = dv_sum = None
        for index in range(tokens // rows):
            part = slice(index * rows, (index + 1) * rows)
            prob = prob_ref[head, part, :]
            spread = contract(grad_ext[part], v_ext, 1, 1)
            grad_scores = (prob.astype(jnp.float32) * spread).astype(jnp.bfloat16)
            dq[index][head] = contract(grad_scores, k, 1, 0)
            rows_of = slice(head * half, (head + 1) * half)
            dk_part = contract(q_turned[rows_of, part], grad_scores, 1, 0)
            dv_part = contract(grad_turned[rows_of, part], prob, 1, 0)
            dk_sum = dk_part if dk_sum is None else dk_sum + dk_part
            dv_sum = dv_part if dv_sum is None else dv_sum + dv_part
        dk.append(dk_sum)
        dv.append(dv_sum)
    for index, pair in enumerate(dq):
        dq_ref[index * rows:(index + 1) * rows, :] = (jnp.where(low_lane, pair[0], pair[1]) * scale).astype(jnp.bfloat16)
    dk_ref[...] = (jnp.concatenate(dk, axis=0) * scale).T.astype(jnp.bfloat16)
    dv_ref[...] = jnp.concatenate(dv, axis=0).T.astype(jnp.bfloat16)


def attn_forward(place, qkv, bias, first, count, before=()):
    tokens, width = qkv.shape[0], qkv.shape[1] // 3
    pairs = width // PAIR

    def at(part):
        return pl.BlockSpec((tokens, PAIR), lambda i, _: (0, part * pairs + first + i))

    def body(place_ref, *refs):
        attn_forward_kernel(*refs[:4], *refs[4 + len(before) :])

    return call(
        body,
        "attn_forward",
        (count,),
        [at(0), at(1), at(2), pl.BlockSpec((2, tokens // BLOCK, PAIR), lambda i, _: (first + i, 0, 0))]
        + [whole_ref()] * len(before),
        [pl.BlockSpec((2, tokens, tokens), lambda i, _: (first + i, 0, 0)), at(0), at(0)],
        [
            shape_of(BF16, 2 * pairs, tokens, tokens),
            shape_of(BF16, tokens, width),
            shape_of(F32, tokens, width),
        ],
        (place, qkv, qkv, qkv, bias) + tuple(before),
        vmem=28,
        alias={5 + i: i for i in range(len(before))},
    )


def attn_backward(place, qkv, prob, mixed, total, grad, first, count, before=()):
    tokens, width = qkv.shape[0], qkv.shape[1] // 3
    pairs = width // PAIR

    def at(part):
        return pl.BlockSpec((tokens, PAIR), lambda i, _: (0, part * pairs + first + i))

    def body(place_ref, *refs):
        attn_backward_kernel(*refs[:7], *refs[7 + len(before) :])

    return call(
        body,
        "attn_backward",
        (count,),
        [at(0), at(1), at(2), pl.BlockSpec((2, tokens, tokens), lambda i, _: (first + i, 0, 0))]
        + [at(0)] * 3
        + [whole_ref()] * len(before),
        [at(0)] * 3,
        [shape_of(BF16, tokens, width)] * 3,
        (place, qkv, qkv, qkv, prob, mixed, total, grad) + tuple(before),
        vmem=28,
        alias={8 + i: i for i in range(len(before))},
    )


def key_bias(random_ids, block_ids):
    heads, blocks, _ = random_ids.shape
    row, col = block_ids[:, None], block_ids[None, :]
    last = blocks - 1
    fixed = (row == 0) | (row == last) | (col == 0) | (col == last) | (jnp.abs(row - col) <= 1)
    drawn = jnp.any(random_ids[:, :, :, None] == block_ids, axis=2)
    bias = jnp.where(fixed[None] | drawn, 0.0, -1e30)
    bias = bias.transpose(0, 2, 1).reshape(heads // 2, 2, blocks, blocks)
    lanes = 128
    even = jnp.pad(bias[:, 0], ((0, 0), (0, 0), (lanes // 2, lanes // 2 - blocks)))
    odd = jnp.pad(bias[:, 1], ((0, 0), (0, 0), (0, lanes - blocks)))
    return jnp.stack([even, odd], axis=1).reshape(heads, blocks, lanes)


def pair_swap(value, axis, bit):
    size = lax.axis_size(axis)
    return lax.ppermute(value, axis, [(i, i ^ bit) for i in range(size)])


def pick(value, index, axis):
    return lax.dynamic_index_in_dim(value, index, axis, keepdims=False)


def swap_x(value):
    return pair_swap(value, "dp", 2)


def swap_core(value):
    return pair_swap(value, "dp", 1)


def swap_y(value):
    return pair_swap(value, "seq", 1)


def ring_z(value, step):
    size = lax.axis_size("dp")
    return lax.ppermute(value, "dp", [(i, (i + 4 * step) % size) for i in range(size)])


def tie(*values):
    return lax.optimization_barrier(values)


def sum_all(values):
    depth = lax.axis_size("dp") // 4
    for swap in (swap_core, swap_x, swap_y):
        values = values + swap(values)
    total = values
    for step in range(1, depth):
        total = total + ring_z(values, step)
    return total


class Reduce:
    def __init__(self, place, rows, x_first):
        self.place, self.rows, self.x_first = place, rows, x_first

    def begin(self, mine, other):
        self.mine, self.came = mine, swap_core(other)

    def first(self):
        groups, tall, columns = self.mine.shape
        if self.x_first:
            shape = (groups // 2, 2, tall, columns)
        else:
            shape = (groups, 2, self.rows, columns)
        spot, swap = (1, swap_x) if self.x_first else (3, swap_y)
        sent, kept = split_add(self.place, self.mine.reshape(shape), self.came.reshape(shape), spot)
        self.mine, self.came = kept, swap(sent)

    def second(self, *others):
        spot, swap = (3, swap_y) if self.x_first else (1, swap_x)
        mine, came = [], []
        for part in (self,) + others:
            shape = (-1, 2, self.rows, part.mine.shape[-1])
            mine.append(part.mine.reshape(shape))
            came.append(part.came.reshape(shape))
        if others:
            sent, kept = merge_add(self.place, mine, came, spot)
        else:
            sent, kept = split_add(self.place, mine[0], came[0], spot)
        self.mine, self.came = kept, swap(sent)

    def third(self, *others):
        pairs = [(self.mine, self.came)] + [(other.mine, other.came) for other in others]
        own, *sent = split_depth(self.place, pairs)
        self.mine = own
        self.came = [ring_z(block, step + 1) for step, block in enumerate(sent)]

    def last(self, cuts=None):
        return last_add(self.place, self.mine, self.came, cuts or [(0, self.mine.shape[1])])

    def hold(self, *others):
        self.mine, self.came, others = tie(self.mine, self.came, others)
        return others


def split_depth_spot(place_ref, step, depth):
    return lax.rem(place_ref[0] + depth - step, depth)


def join_depth(place, blocks, cuts, name):
    depth = len(blocks)
    rows = blocks[0].shape[0]
    moves = []
    for step in range(depth):
        for j, (start, stop) in enumerate(cuts):
            cut = (slice(None), slice(start, stop))
            moves.append((step, cut, j, lambda p, step=step: split_depth_spot(p, step, depth)))
    return join(place, blocks, moves, [(depth, rows, stop - start) for start, stop in cuts], name)


def join_plane(place, blocks):
    moves = []
    for at, (dx, dy) in enumerate(((0, 0), (1, 0), (0, 1), (1, 1))):
        moves.append(
            (at, (), 0, lambda p, dx=dx, dy=dy: (flip(p[1], dx), flip(p[3], dy)))
        )
    return join(place, blocks, moves, [(2, 2) + blocks[0].shape], "join_plane")[0]


def near_parts(own, by_x, by_y, by_xy, cores):
    blocks = {(0, 0): own, (1, 0): by_x, (0, 1): by_y, (1, 1): by_xy}
    return [cores[dx, dy] if dc else blocks[dx, dy] for dx, dc, dy in NEAR]


def paired(inputs, grad_out, random_blocks, *shards):
    depth = lax.axis_size("dp") // 4
    dp, y = lax.axis_index("dp"), lax.axis_index("seq")
    z, x, c = dp // 4, (dp // 2) % 2, dp % 2
    spots = (z, x, c, y)
    place = jnp.stack(spots).astype(jnp.int32)
    w_query, w_key, w_value, w_out, w_up, w_down = shards[:6]
    vectors = shards[6:]
    half, width = inputs.shape[1:]
    rows, tall_rows, hidden_width = w_up.shape[0], w_down.shape[0], w_up.shape[1]
    pairs = width // PAIR
    ring = range(1, depth)

    small = jnp.concatenate([vector.reshape(-1, rows) for vector in vectors])
    small = jnp.pad(small, ((0, rows - small.shape[0]), (0, PAIR - rows)))
    shard = jnp.concatenate([w_query, w_key, w_value, w_out, small], axis=1)
    turned = [shard] + [ring_z(shard, step) for step in ring]
    down_x = swap_x(w_down)
    far_rows = swap_y(cast_far(place, inputs))
    far_grad_low = cast_far(place, grad_out)
    turned, down_x, far_rows, w_up, w_down, random_blocks = tie(
        turned, down_x, far_rows, w_up, w_down, random_blocks
    )
    cut = 2 * width
    left, right = join_depth(place, turned, [(0, cut), (cut, shard.shape[1])], "join_first")
    left_y, right_x = swap_y(left), swap_x(right)
    up_turned = {1: ring_z(w_up, 1), depth - 1: ring_z(w_up, depth - 1)}
    down_y, down_xy = swap_y(w_down), swap_y(down_x)
    left_y, right_x, up_turned, down_y, down_xy, down_x = tie(
        left_y, right_x, up_turned, down_y, down_xy, down_x
    )
    left_x, left_xy = swap_x(left), swap_x(left_y)
    right_y, right_xy = swap_y(right), swap_y(right_x)
    for step in ring:
        if step not in up_turned:
            up_turned[step] = ring_z(w_up, step)
    left_x, left_xy, right_y, right_xy, up_turned, left_y, right_x, down_x, random_blocks = tie(
        left_x, left_xy, right_y, right_xy, up_turned, left_y, right_x, down_x, random_blocks
    )
    (up_own,) = join_depth(place, [w_up] + [up_turned[step] for step in ring], [(0, hidden_width)], "join_up")
    plane = join_plane(place, [w_down, down_x, down_y, down_xy])
    up_own, plane, left, left_x, left_y, left_xy, right, right_x, right_y, right_xy = tie(
        up_own, plane, left, left_x, left_y, left_xy, right, right_x, right_y, right_xy
    )
    up_y = swap_y(up_own)
    left_core = {
        (0, 0): swap_core(left), (0, 1): swap_core(left_y),
        (1, 0): swap_core(left_x), (1, 1): swap_core(left_xy),
    }
    right_core = {
        (0, 0): swap_core(right), (0, 1): swap_core(right_y),
        (1, 0): swap_core(right_x), (1, 1): swap_core(right_xy),
    }
    random_far = swap_y(pick(random_blocks, 1 - y, 0))
    left_parts = near_parts(left, left_x, left_y, left_xy, left_core)
    right_parts = near_parts(right, right_x, right_y, right_xy, right_core)
    sizes = [vector.shape[0] // rows for vector in vectors]
    local_blocks = half // BLOCK
    ids = jnp.arange(2 * local_blocks, dtype=jnp.int32)
    block_ids = (ids + y * local_blocks) % (2 * local_blocks)
    random_ids = jnp.concatenate([pick(random_blocks, y, 0), random_far], axis=1)
    bias = key_bias(random_ids, block_ids)
    left_parts, right_parts, plane, bias = tie(left_parts, right_parts, plane, bias)

    planes = {0: plane, 1: ring_z(plane, 1), depth - 1: ring_z(plane, depth - 1)}
    spans = small_vectors(place, right_parts, cut, sizes, rows)
    (
        ln1_gain,
        ln1_bias,
        query_bias,
        value_bias,
        out_bias,
        ln2_gain,
        ln2_bias,
        up_bias,
        down_bias,
    ) = spans
    qkv_bias = jnp.concatenate([query_bias, jnp.zeros_like(query_bias), value_bias], axis=1)
    normed_low, qkv = norm_project(
        place, inputs, far_rows, ln1_gain, ln1_bias, left_parts, right_parts, qkv_bias
    )
    qkv, up_y = tie(qkv, up_y)
    up_x, up_xy = swap_x(up_own), swap_x(up_y)
    attended = attn_forward(place, qkv, bias, 0, pairs // 2)
    attended, planes, far_grad_low = tie(attended, planes, far_grad_low)
    for step in ring:
        if step not in planes:
            planes[step] = ring_z(planes[0], step)
    far_grad = swap_y(far_grad_low)
    prob, mixed_low, totals = attn_forward(place, qkv, bias, pairs // 2, pairs - pairs // 2, attended)
    middle, normed_two_low, start_out = out_norm(
        place, mixed_low, right_parts, out_bias, inputs, far_rows, ln2_gain, ln2_bias, down_bias
    )
    normed_two_low, up_x, up_xy, far_grad = tie(normed_two_low, up_x, up_xy, far_grad)
    up_core = {
        (0, 0): swap_core(up_own), (0, 1): swap_core(up_y),
        (1, 0): swap_core(up_x), (1, 1): swap_core(up_xy),
    }
    up_parts = near_parts(up_own, up_x, up_y, up_xy, up_core)
    down_parts = [part for step in range(depth) for part in (planes[step], swap_core(planes[step]))]
    grad_ff_low, grad_down_bias = join_low(place, grad_out, far_grad)

    down_sums = [Reduce(place, tall_rows, True) for _ in range(3)]
    near_sum = Reduce(place, rows, False)
    wide_sum = Reduce(place, rows, True)
    out_sum = Reduce(place, rows, True)
    left_sum = Reduce(place, rows, True)
    right_sum = Reduce(place, rows, False)

    def feed(first, count, state, wide):
        return feed_forward(
            place, first, count, depth, normed_two_low, grad_ff_low, up_parts, down_parts, up_bias,
            far_rows, state, wide,
        )

    near = depth // 2
    near_width = hidden_width // 2
    each = hidden_width // depth
    mine, other, up_mine, up_other, bias_0, back, total = feed(
        0, near, (start_out, start_out), (near_width, 0, ())
    )
    down_sums[0].begin(mine, other)
    near_sum.begin(up_mine, up_other)
    mine, other, up_mine, up_other, bias_1, back, total = feed(
        near, depth - 1 - near, (total, back), (near_width, 0, ())
    )
    (back,) = down_sums[0].hold(back)
    (back,) = near_sum.hold(back)
    down_sums[1].begin(mine, other)
    down_sums[0].first()
    near_sum.first()
    down_sums[0].mine, near_sum.mine, back = tie(down_sums[0].mine, near_sum.mine, back)
    mine, other, up_mine, up_other, bias_2, back, out_part, out_delta = feed(
        depth - 1, 1, (total, back), (near_width, (depth - 1 - near) * each, (up_mine, up_other))
    )
    (back,) = down_sums[0].hold(back)
    (back,) = near_sum.hold(back)
    (back,) = down_sums[1].hold(back)
    down_sums[2].begin(mine, other)
    wide_sum.begin(up_mine, up_other)
    down_sums[1].first()
    down_sums[1].mine, back = tie(down_sums[1].mine, back)
    grad_up_bias = jnp.concatenate([bias_0, bias_1, bias_2], axis=1)
    grad_middle, grad_attn_low, grad_mixed_low, grad_ln2_gain, grad_ln2_bias, grad_out_bias = middle_back(
        place, back, middle, ln2_gain, grad_out, far_grad, right_parts
    )
    out_sum.begin(*grad_wide(place, mixed_low, (grad_attn_low,), rows, 1))
    out_sum.mine, grad_mixed_low = tie(out_sum.mine, grad_mixed_low)
    (grad_mixed_low,) = down_sums[1].hold(grad_mixed_low)
    (grad_mixed_low,) = down_sums[2].hold(grad_mixed_low)
    (grad_mixed_low,) = wide_sum.hold(grad_mixed_low)
    down_sums[2].first()
    near_sum.second()
    down_sums[2].mine, near_sum.mine, grad_mixed_low, out_delta = tie(
        down_sums[2].mine, near_sum.mine, grad_mixed_low, out_delta
    )
    out_far = swap_y(out_delta)
    grads = attn_backward(place, qkv, prob, mixed_low, totals, grad_mixed_low, 0, pairs // 2)
    grads, out_far = tie(grads, out_far)
    (grads,) = near_sum.hold(grads)
    (grads,) = down_sums[2].hold(grads)
    (grads,) = out_sum.hold(grads)
    wide_sum.first()
    near_sum.third()
    down_sums[0].second(*down_sums[1:])
    down_sum = down_sums[0]
    down_sum.mine, near_sum.mine, wide_sum.mine, out_sum.mine, grads = tie(
        down_sum.mine, near_sum.mine, wide_sum.mine, out_sum.mine, grads
    )
    grads = attn_backward(
        place, qkv, prob, mixed_low, totals, grad_mixed_low, pairs // 2, pairs - pairs // 2, grads
    )
    (grads,) = near_sum.hold(grads)
    (grads,) = wide_sum.hold(grads)
    (grads,) = down_sum.hold(grads)
    out_sum.first()
    wide_sum.second()
    down_sum.third()
    out_sum.mine, wide_sum.mine, down_sum.mine, grads = tie(
        out_sum.mine, wide_sum.mine, down_sum.mine, grads
    )
    wide = grad_wide(place, normed_low, grads, rows, 2)
    (wide,) = out_sum.hold(wide)
    (wide,) = wide_sum.hold(wide)
    left_sum.begin(*wide[:2])
    right_sum.begin(*wide[2:])
    out_sum.second()
    (grad_up_near,) = near_sum.last()
    left_sum.mine, grads, grad_up_near, out_sum.mine = tie(left_sum.mine, grads, grad_up_near, out_sum.mine)
    (grads,) = left_sum.hold(grads)
    left_sum.first()
    (grads,) = right_sum.hold(grads)
    right_sum.first()
    left_sum.mine, right_sum.mine, grads = tie(left_sum.mine, right_sum.mine, grads)
    in_part, in_delta, grad_ln1_gain, grad_ln1_bias, grad_query_bias, grad_value_bias = input_back(
        place, grads, left_parts, right_parts, inputs, far_rows, ln1_gain, grad_middle, far_grad
    )
    (in_delta,) = left_sum.hold(in_delta)
    left_sum.second()
    (in_delta,) = right_sum.hold(in_delta)
    right_sum.second()
    left_sum.mine, right_sum.mine, in_delta, grad_ln1_gain, wide_sum.mine = tie(
        left_sum.mine, right_sum.mine, in_delta, grad_ln1_gain, wide_sum.mine
    )
    (grad_ln1_gain,) = out_sum.hold(grad_ln1_gain)
    (grad_ln1_gain,) = down_sum.hold(grad_ln1_gain)
    wide_sum.third(out_sum)
    (grad_w_down,) = down_sum.last()
    wide_sum.mine, in_delta, grad_ln1_gain, grad_w_down = tie(
        wide_sum.mine, in_delta, grad_ln1_gain, grad_w_down
    )
    in_delta, grad_ln1_gain = left_sum.hold(in_delta, grad_ln1_gain)
    in_delta, grad_ln1_gain = right_sum.hold(in_delta, grad_ln1_gain)
    left_sum.third(right_sum)
    left_sum.mine, in_delta, grad_ln1_gain = tie(left_sum.mine, in_delta, grad_ln1_gain)
    grad_vectors = (
        grad_ln1_gain,
        grad_ln1_bias,
        grad_query_bias,
        grad_value_bias,
        grad_out_bias,
        grad_ln2_gain,
        grad_ln2_bias,
        grad_up_bias,
        grad_down_bias,
    )
    in_far = swap_y(in_delta)
    packed = pick(sum_all(pack_vectors(place, grad_vectors, sizes, rows)), dp * 2 + y, 1)
    result = fill_far(place, out_part, inputs, out_far)
    grad_up_far, grad_w_out = wide_sum.last([(0, near_width), (near_width, near_width + width)])
    grad_w_up = jnp.concatenate([grad_up_near, grad_up_far], axis=1)
    grad_in = fill_far(place, in_part, grad_out, in_far)
    out_vectors = []
    at = 0
    for size in sizes:
        out_vectors.append(packed[at : at + size].reshape(-1))
        at += size
    qkv_cuts = [(part * width, (part + 1) * width) for part in range(3)]
    return (
        (result, grad_in)
        + tuple(left_sum.last(qkv_cuts))
        + (grad_w_out, grad_w_up, grad_w_down)
        + tuple(out_vectors)
    )


def solution(mesh):
    tokens, table, matrix, vector = P("dp", "seq", None), P("dp", None, "seq", None), P(BOTH, None), P(BOTH)
    in_specs = (tokens, tokens, table) + (matrix,) * 6 + (vector,) * 9
    out_specs = (tokens, tokens) + (matrix,) * 6 + (vector,) * 9
    paired_fits = mesh.shape["seq"] == 2 and mesh.shape["dp"] % 4 == 0

    def body(inputs, *rest):
        whole = paired if paired_fits and inputs.shape[0] == 2 else on_device
        return whole(inputs, *rest)

    return jax.shard_map(
        body, mesh=mesh, in_specs=in_specs, out_specs=out_specs, check_vma=False
    )
```

```python
import jax
import jax.numpy as jnp
from jax import lax
from jax.experimental import pallas as pl
from jax.experimental.pallas import tpu as pltpu
from jax.sharding import PartitionSpec as P

HEADS = 16
BLOCK = 64
BOTH = ("dp", "seq")


eps_norm = 1e-05
neg_fill = -1e30


def layer_norm(values, norm_gain, norm_shift):
    centre = values - jnp.mean(values, axis=-1, keepdims=True)
    spread = jnp.mean(centre * centre, axis=-1, keepdims=True)
    return centre * lax.rsqrt(spread + eps_norm) * norm_gain + norm_shift


def gelu_tanh(values):
    return jax.nn.gelu(values, approximate=True)


def project(left, right):
    return jnp.dot(left, right, preferred_element_type=jnp.float32)


def project_back(grad_rows, weight):
    return lax.dot_general(
        grad_rows, weight, (((1,), (1,)), ((), ())), preferred_element_type=jnp.float32
    )


def weight_grad(left, grad_rows):
    return lax.dot_general(
        left, grad_rows, (((0,), (0,)), ((), ())), preferred_element_type=jnp.float32
    )


def column_sum(grad_rows):
    return jnp.sum(grad_rows, axis=0, dtype=jnp.float32)


def to_table(block_rows):
    block_count = block_rows.shape[0] // BLOCK
    head_dim = block_rows.shape[1] // HEADS
    shaped = block_rows.reshape(block_count, BLOCK, HEADS, head_dim)
    return shaped.transpose(2, 0, 1, 3).reshape(HEADS, block_count, BLOCK * head_dim)


def from_table(table):
    block_count = table.shape[1]
    head_dim = table.shape[2] // BLOCK
    shaped = table.reshape(HEADS, block_count, BLOCK, head_dim)
    return shaped.transpose(1, 2, 0, 3).reshape(block_count * BLOCK, HEADS * head_dim)


def key_layout(first_block, local_blocks, all_blocks, random_ids):
    query_ids = first_block + jnp.arange(local_blocks, dtype=jnp.int32)
    window = jnp.stack([query_ids - 1, query_ids, query_ids + 1], axis=1)
    inside = (window >= 1) & (window <= all_blocks - 2)
    window = jnp.clip(window, 0, all_blocks - 1)
    end_blocks = jnp.broadcast_to(jnp.array([0, all_blocks - 1], jnp.int32), (local_blocks, 2))
    fixed_slots = jnp.concatenate([end_blocks, window], axis=1)
    key_slots = jnp.concatenate(
        [jnp.broadcast_to(fixed_slots[None], (HEADS, local_blocks, 5)), random_ids], axis=2
    )
    key_valid = jnp.concatenate(
        [
            jnp.ones((local_blocks, 2), jnp.bool_),
            inside,
            jnp.ones((local_blocks, random_ids.shape[2]), jnp.bool_),
        ],
        axis=1,
    )
    return (key_slots, jnp.repeat(key_valid, BLOCK, axis=1))


def pick_blocks(table, key_slots):
    head_index = jnp.arange(HEADS)[:, None, None]
    picked = table[head_index, key_slots]
    head_dim = table.shape[2] // BLOCK
    return picked.reshape(HEADS, key_slots.shape[1], key_slots.shape[2] * BLOCK, head_dim)


def sparse_scores(query_heads, key_picked, key_valid, score_scale):
    raw_scores = jnp.einsum(
        "hqid,hqkd->hqik", query_heads, key_picked, preferred_element_type=jnp.float32
    )
    return jnp.where(key_valid[None, :, None, :], raw_scores * score_scale, neg_fill)


def dense_scores(query_block, key_flat, score_scale):
    return (
        jnp.einsum("hid,hkd->hik", query_block, key_flat, preferred_element_type=jnp.float32)
        * score_scale
    )


def dense_forward(query_block, key_flat, value_flat, score_scale):
    scores = dense_scores(query_block, key_flat, score_scale)
    top_score = jnp.max(scores, axis=-1, keepdims=True)
    expos = jnp.exp(scores - top_score)
    totals = jnp.sum(expos, axis=-1, keepdims=True)
    attn_prob = (expos / totals).astype(jnp.bfloat16)
    result = jnp.einsum("hik,hkd->ihd", attn_prob, value_flat, preferred_element_type=jnp.float32)
    return (result, (top_score + jnp.log(totals))[..., 0])


def softmax_back(attn_prob, grad_prob, score_scale):
    inner = jnp.sum(attn_prob * grad_prob, axis=-1, keepdims=True)
    return (attn_prob * (grad_prob - inner) * score_scale).astype(jnp.bfloat16)


def dense_backward(query_block, key_flat, value_flat, grad_block, log_total, score_scale):
    attn_prob = jnp.exp(dense_scores(query_block, key_flat, score_scale) - log_total[..., None])
    grad_prob = jnp.einsum(
        "ihd,hkd->hik", grad_block, value_flat, preferred_element_type=jnp.float32
    )
    grad_value = jnp.einsum(
        "hik,ihd->hkd",
        attn_prob.astype(jnp.bfloat16),
        grad_block,
        preferred_element_type=jnp.float32,
    )
    grad_scores = softmax_back(attn_prob, grad_prob, score_scale)
    grad_query = jnp.einsum(
        "hik,hkd->ihd", grad_scores, key_flat, preferred_element_type=jnp.float32
    )
    grad_key = jnp.einsum(
        "hik,hid->hkd", grad_scores, query_block, preferred_element_type=jnp.float32
    )
    return (grad_query, grad_key, grad_value)


def run_forward(weights, in_rows, random_ids):
    (
        w_query,
        w_key,
        w_value,
        w_out,
        w_up,
        w_down,
        ln1_gain,
        ln1_bias,
        query_bias,
        value_bias,
        out_bias,
        ln2_gain,
        ln2_bias,
        up_bias,
        down_bias,
    ) = weights
    normed, pull_first = jax.vjp(
        layer_norm, in_rows, ln1_gain.astype(jnp.float32), ln1_bias.astype(jnp.float32)
    )
    normed_low = normed.astype(jnp.bfloat16)
    queries = (project(normed_low, w_query) + query_bias.astype(jnp.float32)).astype(jnp.bfloat16)
    key_rows = project(normed_low, w_key).astype(jnp.bfloat16)
    value_rows = (project(normed_low, w_value) + value_bias.astype(jnp.float32)).astype(
        jnp.bfloat16
    )
    key_all, value_all = (
        lax.all_gather(key_rows, "seq", axis=0, tiled=True),
        lax.all_gather(value_rows, "seq", axis=0, tiled=True),
    )
    place = lax.axis_index("seq")
    ranks = lax.axis_size("seq")
    local_blocks = in_rows.shape[0] // BLOCK
    all_blocks = key_all.shape[0] // BLOCK
    head_dim = queries.shape[1] // HEADS
    score_scale = head_dim ** (-0.5)
    key_slots, key_valid = key_layout(place * local_blocks, local_blocks, all_blocks, random_ids)
    key_table = to_table(key_all)
    value_table = to_table(value_all)
    key_picked = pick_blocks(key_table, key_slots)
    value_picked = pick_blocks(value_table, key_slots)
    query_heads = to_table(queries).reshape(HEADS, local_blocks, BLOCK, head_dim)
    scores = sparse_scores(query_heads, key_picked, key_valid, score_scale)
    top_score = jnp.max(scores, axis=-1, keepdims=True)
    expos = jnp.exp(scores - top_score)
    totals = jnp.sum(expos, axis=-1, keepdims=True)
    prob_low = (expos / totals).astype(jnp.bfloat16)
    log_sparse = (top_score + jnp.log(totals))[..., 0]
    sparse_out = jnp.einsum(
        "hqik,hqkd->qihd", prob_low, value_picked, preferred_element_type=jnp.float32
    )
    is_edge = (place == 0) | (place == ranks - 1)
    edge_slot = jnp.where(place == 0, 0, local_blocks - 1)
    key_flat = key_table.reshape(HEADS, all_blocks * BLOCK, head_dim)
    value_flat = value_table.reshape(HEADS, all_blocks * BLOCK, head_dim)
    query_edge = lax.dynamic_index_in_dim(query_heads, edge_slot, 1, keepdims=False)
    edge_out, log_edge = lax.cond(
        is_edge,
        lambda: dense_forward(query_edge, key_flat, value_flat, score_scale),
        lambda: (
            jnp.zeros((BLOCK, HEADS, head_dim), jnp.float32),
            jnp.zeros((HEADS, BLOCK), jnp.float32),
        ),
    )
    current = lax.dynamic_index_in_dim(sparse_out, edge_slot, 0, keepdims=False)
    mixed_heads = lax.dynamic_update_index_in_dim(
        sparse_out, jnp.where(is_edge, edge_out, current), edge_slot, 0
    )
    mixed_low = mixed_heads.reshape(in_rows.shape[0], queries.shape[1]).astype(jnp.bfloat16)
    middle = in_rows + (project(mixed_low, w_out) + out_bias.astype(jnp.float32))
    normed_two, pull_second = jax.vjp(
        layer_norm, middle, ln2_gain.astype(jnp.float32), ln2_bias.astype(jnp.float32)
    )
    normed_two_low = normed_two.astype(jnp.bfloat16)
    hidden_pre = project(normed_two_low, w_up) + up_bias.astype(jnp.float32)
    hidden, pull_gelu = jax.vjp(gelu_tanh, hidden_pre)
    hidden_low = hidden.astype(jnp.bfloat16)
    result = middle + (project(hidden_low, w_down) + down_bias.astype(jnp.float32))
    saved = {
        "pull_first": pull_first,
        "pull_second": pull_second,
        "pull_gelu": pull_gelu,
        "normed_low": normed_low,
        "normed_two_low": normed_two_low,
        "hidden_low": hidden_low,
        "mixed_low": mixed_low,
        "query_heads": query_heads,
        "query_edge": query_edge,
        "key_picked": key_picked,
        "value_picked": value_picked,
        "key_flat": key_flat,
        "value_flat": value_flat,
        "key_slots": key_slots,
        "key_valid": key_valid,
        "log_sparse": log_sparse,
        "log_edge": log_edge,
        "is_edge": is_edge,
        "edge_slot": edge_slot,
    }
    return (saved, result)


def run_backward(weights, saved, grad_rows):
    (
        w_query,
        w_key,
        w_value,
        w_out,
        w_up,
        w_down,
        ln1_gain,
        ln1_bias,
        query_bias,
        value_bias,
        out_bias,
        ln2_gain,
        ln2_bias,
        up_bias,
        down_bias,
    ) = weights
    query_heads = saved["query_heads"]
    key_picked = saved["key_picked"]
    value_picked = saved["value_picked"]
    key_slots = saved["key_slots"]
    is_edge = saved["is_edge"]
    edge_slot = saved["edge_slot"]
    local_blocks = query_heads.shape[1]
    head_dim = query_heads.shape[3]
    all_blocks = saved["key_flat"].shape[1] // BLOCK
    score_scale = head_dim ** (-0.5)
    token_count = grad_rows.shape[0]
    grad_ff_low = grad_rows.astype(jnp.bfloat16)
    grad_w_down = weight_grad(saved["hidden_low"], grad_ff_low)
    grad_down_bias = column_sum(grad_ff_low)
    (grad_pre,) = saved["pull_gelu"](project_back(grad_ff_low, w_down))
    grad_pre_low = grad_pre.astype(jnp.bfloat16)
    grad_w_up = weight_grad(saved["normed_two_low"], grad_pre_low)
    grad_up_bias = column_sum(grad_pre_low)
    grad_normed_two = project_back(grad_pre_low, w_up)
    grad_middle, grad_ln2_gain, grad_ln2_bias = saved["pull_second"](grad_normed_two)
    grad_middle = grad_middle + grad_rows
    grad_attn_low = grad_middle.astype(jnp.bfloat16)
    grad_w_out = weight_grad(saved["mixed_low"], grad_attn_low)
    grad_out_bias = column_sum(grad_attn_low)
    grad_mixed = (
        project_back(grad_attn_low, w_out)
        .astype(jnp.bfloat16)
        .reshape(local_blocks, BLOCK, HEADS, head_dim)
    )
    block_ids = jnp.arange(local_blocks, dtype=jnp.int32)
    keep_sparse = jnp.where(is_edge & (block_ids == edge_slot), 0.0, 1.0).astype(jnp.bfloat16)
    grad_sparse = grad_mixed * keep_sparse[:, None, None, None]
    scores = sparse_scores(query_heads, key_picked, saved["key_valid"], score_scale)
    attn_prob = jnp.exp(scores - saved["log_sparse"][..., None])
    grad_prob = jnp.einsum(
        "qihd,hqkd->hqik", grad_sparse, value_picked, preferred_element_type=jnp.float32
    )
    grad_value_picked = jnp.einsum(
        "hqik,qihd->hqkd",
        attn_prob.astype(jnp.bfloat16),
        grad_sparse,
        preferred_element_type=jnp.float32,
    )
    grad_scores = softmax_back(attn_prob, grad_prob, score_scale)
    grad_query_sparse = jnp.einsum(
        "hqik,hqkd->qihd", grad_scores, key_picked, preferred_element_type=jnp.float32
    )
    grad_key_picked = jnp.einsum(
        "hqik,hqid->hqkd", grad_scores, query_heads, preferred_element_type=jnp.float32
    )
    head_index = jnp.arange(HEADS)[:, None, None]
    slot_count = key_slots.shape[2]
    table_shape = (HEADS, all_blocks, BLOCK * head_dim)
    grad_key_table = (
        jnp.zeros(table_shape, jnp.float32)
        .at[head_index, key_slots]
        .add(grad_key_picked.reshape(HEADS, local_blocks, slot_count, BLOCK * head_dim))
    )
    grad_value_table = (
        jnp.zeros(table_shape, jnp.float32)
        .at[head_index, key_slots]
        .add(grad_value_picked.reshape(HEADS, local_blocks, slot_count, BLOCK * head_dim))
    )
    grad_edge_block = lax.dynamic_index_in_dim(grad_mixed, edge_slot, 0, keepdims=False)
    flat_shape = (HEADS, all_blocks * BLOCK, head_dim)
    grad_query_edge, grad_key_edge, grad_value_edge = lax.cond(
        is_edge,
        lambda: dense_backward(
            saved["query_edge"],
            saved["key_flat"],
            saved["value_flat"],
            grad_edge_block,
            saved["log_edge"],
            score_scale,
        ),
        lambda: (
            jnp.zeros((BLOCK, HEADS, head_dim), jnp.float32),
            jnp.zeros(flat_shape, jnp.float32),
            jnp.zeros(flat_shape, jnp.float32),
        ),
    )
    grad_key_table = grad_key_table + grad_key_edge.reshape(table_shape)
    grad_value_table = grad_value_table + grad_value_edge.reshape(table_shape)
    grad_key_own, grad_value_own = (
        lax.psum_scatter(
            from_table(grad_key_table).astype(jnp.bfloat16), "seq", scatter_dimension=0, tiled=True
        ).astype(jnp.float32),
        lax.psum_scatter(
            from_table(grad_value_table).astype(jnp.bfloat16),
            "seq",
            scatter_dimension=0,
            tiled=True,
        ).astype(jnp.float32),
    )
    current = lax.dynamic_index_in_dim(grad_query_sparse, edge_slot, 0, keepdims=False)
    grad_query_all = lax.dynamic_update_index_in_dim(
        grad_query_sparse, current + grad_query_edge, edge_slot, 0
    )
    grad_query_low = grad_query_all.reshape(token_count, HEADS * head_dim).astype(jnp.bfloat16)
    grad_key_low = grad_key_own.astype(jnp.bfloat16)
    grad_value_low = grad_value_own.astype(jnp.bfloat16)
    normed_low = saved["normed_low"]
    grad_w_query = weight_grad(normed_low, grad_query_low)
    grad_w_key = weight_grad(normed_low, grad_key_low)
    grad_w_value = weight_grad(normed_low, grad_value_low)
    grad_query_bias = column_sum(grad_query_low)
    grad_value_bias = column_sum(grad_value_low)
    grad_normed = (
        project_back(grad_query_low, w_query)
        + project_back(grad_key_low, w_key)
        + project_back(grad_value_low, w_value)
    )
    grad_inputs, grad_ln1_gain, grad_ln1_bias = saved["pull_first"](grad_normed)
    grad_inputs = grad_inputs + grad_middle
    grads = (
        grad_w_query,
        grad_w_key,
        grad_w_value,
        grad_w_out,
        grad_w_up,
        grad_w_down,
        grad_ln1_gain,
        grad_ln1_bias,
        grad_query_bias,
        grad_value_bias,
        grad_out_bias,
        grad_ln2_gain,
        grad_ln2_bias,
        grad_up_bias,
        grad_down_bias,
    )
    return (grad_inputs, grads)


def on_device(inputs, grad_out, random_blocks, *shards):
    weights = tuple(lax.all_gather(part, BOTH, axis=0, tiled=True) for part in shards)

    def micro_step(totals, sequence):
        in_rows, grad_rows, random_ids = sequence
        saved, result = run_forward(weights, in_rows, random_ids)
        grad_in, grads = run_backward(weights, saved, grad_rows)
        return (tuple(left + right for left, right in zip(totals, grads)), (result, grad_in))

    initial = tuple(jnp.zeros(weight.shape, jnp.float32) for weight in weights)
    totals, (results, grads_in) = lax.scan(micro_step, initial, (inputs, grad_out, random_blocks))
    summed = tuple(
        lax.psum_scatter(total, BOTH, scatter_dimension=0, tiled=True) for total in totals
    )
    return (results, grads_in) + summed


F32, BF16 = jnp.float32, jnp.bfloat16
PAIR = 128
TIMES = dict(
    cast_far=1,
    join_first=2,
    join_beside=1,
    join_up=2,
    join_plane=2,
    small_vectors=2,
    norm_project=0.3,
    attn_forward=0.5,
    out_norm=0.3,
    join_low=0.3,
    feed_forward=9,
    split_add=0.1,
    merge_add=0.3,
    beside_add=0.3,
    middle_back=12,
    grad_wide=1.8,
    attn_backward=5,
    split_depth=0.3,
    input_back=0.25,
    pack_vectors=0.3,
    fill_far=0.05,
    last_add=0.05,
)
COST = 0.3 * 1e9
NEAR = tuple((dx, dc, dy) for dx in range(2) for dc in range(2) for dy in range(2))


def contract(left, right, left_dim, right_dim):
    return lax.dot_general(
        left, right, (((left_dim,), (right_dim,)), ((), ())), preferred_element_type=F32
    )


def held(*shape):
    zeros = (0,) * len(shape)
    return pl.BlockSpec(shape, lambda *_: zeros, pipeline_mode=pl.Buffered(1))


def whole_ref():
    return pl.BlockSpec(memory_space=pltpu.HBM)


def call(body, name, grid, in_specs, out_specs, out_shape, args, scratch=(), vmem=24, alias=None):
    spec = pltpu.PrefetchScalarGridSpec(
        num_scalar_prefetch=1,
        grid=grid,
        in_specs=in_specs,
        out_specs=out_specs,
        scratch_shapes=scratch,
    )
    return pl.pallas_call(
        body,
        grid_spec=spec,
        out_shape=out_shape,
        name=name,
        input_output_aliases=alias or {},
        compiler_params=pltpu.CompilerParams(vmem_limit_bytes=vmem << 20),
        cost_estimate=pl.CostEstimate(
            flops=int(TIMES[name] * grid[0] * COST), bytes_accessed=1, transcendentals=1
        ),
    )(*args)


def shape_of(kind, *shape):
    return jax.ShapeDtypeStruct(shape, kind)


def norm_parts(values):
    mean = jnp.mean(values, axis=-1, keepdims=True)
    centre = values - mean
    spread = jnp.mean(centre * centre, axis=-1, keepdims=True)
    scale = lax.rsqrt(spread + eps_norm)
    return centre * scale, scale


def norm_back(unit, scale, gain, grad):
    inner = grad * gain
    first = jnp.mean(inner, axis=-1, keepdims=True)
    second = jnp.mean(inner * unit, axis=-1, keepdims=True)
    return scale * (inner - first - unit * second)


def column(values):
    return jnp.sum(values, axis=0, keepdims=True)


def gelu_both(values):
    root = 2 * 0.7978845608028654
    cubic = root * 0.044715
    turn = -1.4426950408889634
    square = values * values
    power = jnp.exp2(jnp.minimum(values * (turn * root + (turn * cubic) * square), 126.0))
    part = pl.reciprocal(1.0 + power, approx=True)
    hidden = values * part
    return hidden, part + (hidden - hidden * part) * (root + (3 * cubic) * square)


def flip(value, bit):
    return 1 - value if bit else value


def parts_copies(place_ref, part_refs, weight, sems, start, size, into, chunk):
    copies = []
    for at, (dx, dc, dy) in enumerate(NEAR):
        spot = (slice(None), flip(place_ref[1], dx), flip(place_ref[2], dc), flip(place_ref[3], dy))
        copies.append(
            pltpu.make_async_copy(
                part_refs[at].at[:, :, pl.ds(start, size)],
                weight.at[spot + (slice(None), pl.ds(into, size))],
                sems.at[chunk, at],
            )
        )
    return copies


def weight_scratch(part, columns):
    depth, rows, _ = part.shape
    return pltpu.VMEM((depth, 2, 2, 2, rows, columns), BF16)


def flat(value):
    return value.reshape(-1, value.shape[-1])


def depth_copies(place_ref, part_refs, weight, sems):
    depth = weight.shape[0]
    copies = []
    for step in range(depth):
        there = lax.rem(place_ref[0] + depth - step, depth)
        for dc in range(2):
            core = flip(place_ref[2], dc)
            copies.append(
                pltpu.make_async_copy(
                    part_refs[2 * step + dc], weight.at[there, :, core], sems.at[there, dc]
                )
            )
    return copies


def depth_wait(place_ref, part_refs, weight, sems, at):
    for dc in range(2):
        core = flip(place_ref[2], dc)
        pltpu.make_async_copy(part_refs[dc], weight.at[at, :, core], sems.at[at, dc]).wait()


def own_spec(step, width, parts):
    return pl.BlockSpec((1, step, width), lambda i, p: (p[3], jnp.minimum(i, parts - 1), 0))


def far_spec(step, width, parts):
    return pl.BlockSpec((step, width), lambda i, _: (jnp.maximum(i - parts, 0), 0))


def join(place, blocks, moves, shapes, name):
    def body(place_ref, *refs):
        ins, outs = refs[: len(blocks)], refs[len(blocks) :]
        for i, cut, j, spot in moves:
            outs[j][spot(place_ref)] = ins[i][cut]

    return call(
        body,
        name,
        (1,),
        [held(*block.shape) for block in blocks],
        [held(*shape) for shape in shapes],
        [shape_of(BF16, *shape) for shape in shapes],
        (place,) + tuple(blocks),
        vmem=10,
    )


def join_beside(place, blocks):
    rows = blocks[0].shape[0]
    widths = [block.shape[1] for block in blocks]

    def body(place_ref, *refs):
        start = 0
        for ref, width in zip(refs, widths):
            refs[-1][:, start : start + width] = ref[...]
            start += width

    return call(
        body,
        "join_beside",
        (1,),
        [held(*block.shape) for block in blocks],
        held(rows, sum(widths)),
        shape_of(BF16, rows, sum(widths)),
        (place,) + tuple(blocks),
        vmem=4,
    )


def join_low(place, grad_out, far):
    half, width = far.shape

    def body(place_ref, own_ref, far_ref, low_ref, sum_ref):
        low = own_ref[0].astype(BF16)
        low_ref[:half] = low
        low_ref[half:] = far_ref[...]
        sum_ref[...] = column(low.astype(F32)) + column(far_ref[...].astype(F32))

    return call(
        body,
        "join_low",
        (1,),
        [
            pl.BlockSpec((1, half, width), lambda i, p: (p[3], 0, 0), pipeline_mode=pl.Buffered(1)),
            held(half, width),
        ],
        [held(2 * half, width), held(1, width)],
        [shape_of(BF16, 2 * half, width), shape_of(F32, 1, width)],
        (place, grad_out, far),
        vmem=12,
    )


def cast_far(place, values):
    _, half, width = values.shape
    step = half // 2

    def body(place_ref, values_ref, out_ref):
        out_ref[...] = values_ref[0].astype(BF16)

    return call(
        body,
        "cast_far",
        (half // step,),
        [pl.BlockSpec((1, step, width), lambda i, p: (1 - p[3], i, 0))],
        pl.BlockSpec((step, width), lambda i, _: (i, 0)),
        shape_of(BF16, half, width),
        (place, values),
        vmem=6,
    )


def norm_project(place, inputs, far, gain, shift, left, right, bias):
    half, width = far.shape
    columns = bias.shape[1]
    step = 512
    left_steps = left[0].shape[-1] // step
    steps = columns // step
    sub = 256

    def body(place_ref, own_ref, far_ref, gain_ref, shift_ref, bias_ref, *refs):
        left_refs, right_refs = refs[:8], refs[8:16]
        normed_ref, out_ref, weight, sems = refs[16:]
        at = pl.program_id(0)

        def copies(chunk):
            refs, start = (left_refs, chunk) if chunk < left_steps else (right_refs, chunk - left_steps)
            return parts_copies(place_ref, refs, weight, sems, start * step, step, chunk * step, chunk)

        @pl.when(at == 0)
        def _():
            for chunk in range(steps):
                for copy in copies(chunk):
                    copy.start()
            for start, rows in ((0, own_ref[0]), (half, far_ref[...])):
                unit, _ = norm_parts(rows.astype(F32))
                normed_ref[start : start + half, :] = (
                    unit * gain_ref[...] + shift_ref[...]
                ).astype(BF16)

        for chunk in range(steps):
            @pl.when(at == chunk)
            def _():
                for copy in copies(chunk):
                    copy.wait()

        cut = pl.ds(pl.multiple_of(at * step, step), step)
        part = flat(weight[:, :, :, :, :, cut])
        for start in range(0, 2 * half, sub):
            result = contract(normed_ref[start : start + sub], part, 1, 0) + bias_ref[...]
            out_ref[start : start + sub] = result.astype(BF16)

    return call(
        body,
        "norm_project",
        (steps,),
        [
            pl.BlockSpec((1, half, width), lambda i, p: (p[3], 0, 0), pipeline_mode=pl.Buffered(1)),
            held(half, width),
            held(1, width),
            held(1, width),
            pl.BlockSpec((1, step), lambda i, _: (0, i)),
        ]
        + [whole_ref()] * 16,
        [
            pl.BlockSpec((2 * half, width), lambda i, _: (0, 0)),
            pl.BlockSpec((2 * half, step), lambda i, _: (0, i)),
        ],
        [shape_of(BF16, 2 * half, width), shape_of(BF16, 2 * half, columns)],
        (place, inputs, far, gain, shift, bias) + tuple(left) + tuple(right),
        scratch=[weight_scratch(left[0], columns), pltpu.SemaphoreType.DMA((steps, 8))],
        vmem=56,
    )


def out_norm(place, mixed, right, bias, inputs, far, gain, shift, down_bias):
    half, width = far.shape
    step = 256
    parts = half // step

    def body(place_ref, mixed_ref, bias_ref, own_ref, far_ref, gain_ref, shift_ref, down_ref, *refs):
        right_refs = refs[:8]
        middle_ref, normed_ref, start_ref, weight, sems = refs[8:]

        @pl.when(pl.program_id(0) == 0)
        def _():
            copies = parts_copies(place_ref, right_refs, weight, sems, width, width, 0, 0)
            for copy in copies:
                copy.start()
            for copy in copies:
                copy.wait()

        near = pl.program_id(0) < parts
        rows = jnp.where(near, own_ref[0], far_ref[...].astype(F32))
        middle = rows + (contract(mixed_ref[...], flat(weight[...]), 1, 0) + bias_ref[...])
        middle_ref[...] = middle
        start_ref[...] = middle + down_ref[...]
        unit, _ = norm_parts(middle)
        normed_ref[...] = (unit * gain_ref[...] + shift_ref[...]).astype(BF16)

    here = pl.BlockSpec((step, width), lambda i, _: (i, 0))
    return call(
        body,
        "out_norm",
        (2 * parts,),
        [
            here,
            held(1, width),
            own_spec(step, width, parts),
            far_spec(step, width, parts),
            held(1, width),
            held(1, width),
            held(1, width),
        ]
        + [whole_ref()] * 8,
        [here, here, here],
        [shape_of(F32, 2 * half, width), shape_of(BF16, 2 * half, width), shape_of(F32, 2 * half, width)],
        (place, mixed, bias, inputs, far, gain, shift, down_bias) + tuple(right),
        scratch=[weight_scratch(right[0], width), pltpu.SemaphoreType.DMA((1, 8))],
        vmem=56,
    )


def fill_far(place, partial, base, delta):
    _, half, width = base.shape
    step = 256

    def body(place_ref, partial_ref, base_ref, delta_ref, out_ref):
        out_ref[0] = base_ref[0] + delta_ref[...].astype(F32)

    there = pl.BlockSpec((1, step, width), lambda i, p: (1 - p[3], i, 0))
    return call(
        body,
        "fill_far",
        (half // step,),
        [whole_ref(), there, pl.BlockSpec((step, width), lambda i, _: (i, 0))],
        there,
        shape_of(F32, 2, half, width),
        (place, partial, base, delta),
        alias={1: 0},
        vmem=8,
    )


def grad_wide(place, left, rights, rows, pieces, before=()):
    tokens, tall = left.shape
    width = rights[0].shape[1]
    step = 512
    each = width // step
    steps = each * len(rights)
    group = 4 * rows
    per = steps // pieces
    total = width * len(rights)

    def body(place_ref, left_ref, *refs):
        right_refs = refs[: len(rights)]
        outs = refs[len(rights) + len(before) : -1]
        sums = refs[-1]
        at = pl.program_id(0)
        for which, right_ref in enumerate(right_refs):
            @pl.when(at // each == which)
            def _():
                result = contract(left_ref[...], right_ref[...], 0, 0)
                sums[...] = result.reshape(tall // group, 2, group // 2, step)

        for piece in range(pieces):
            @pl.when(at // per == piece)
            def _():
                outs[2 * piece][...] = sums[:, place_ref[2]].astype(BF16)
                outs[2 * piece + 1][...] = sums[:, 1 - place_ref[2]].astype(BF16)

    def right_at(which):
        return lambda i, _: (0, jnp.clip(i - which * each, 0, each - 1))

    wide_total = before[0].shape[-1] if before else total // pieces
    start = (wide_total - total // pieces) // step

    def out_at(piece):
        return lambda i, _: (0, 0, start + jnp.clip(i - piece * per, 0, per - 1))

    return call(
        body,
        "grad_wide",
        (steps,),
        [held(tokens, tall)]
        + [pl.BlockSpec((tokens, step), right_at(i)) for i in range(len(rights))]
        + [whole_ref()] * len(before),
        [
            pl.BlockSpec((tall // group, group // 2, step), out_at(piece))
            for piece in range(pieces)
            for _ in range(2)
        ],
        [shape_of(BF16, tall // group, group // 2, wide_total)] * (2 * pieces),
        (place, left) + tuple(rights) + tuple(before),
        scratch=[pltpu.VMEM((tall // group, 2, group // 2, step), F32)],
        vmem=20,
        alias={2 + len(rights) + i: i for i in range(len(before))},
    )


def feed_forward(place, first, count, depth, normed, grad_low, up_parts, down_parts, up_bias, far, state, wide):
    tokens, width = normed.shape
    half = tokens // 2
    hidden_width = up_bias.shape[1]
    step = hidden_width // (2 * depth)
    steps = 2 * count
    rows = down_parts[0].shape[-2]
    group = width // (2 * depth)
    last = first + count == depth
    columns, offset, before = wide
    offset = offset // step
    lines = up_parts[0].shape[1]
    beside = (up_parts[0].shape[-1] - hidden_width) // width
    rows = rows + beside * lines

    def body(place_ref, bias_ref, normed_in, grad_in, far_in, out_in, back_in, *refs):
        up_refs, down_refs = refs[:8], refs[8 : 8 + 2 * depth]
        refs = refs[8 + 2 * depth + len(before) :]
        tall_mine, tall_other, wide_mine, wide_other, sum_ref, back_out = refs[:6]
        outs = refs[6:8] if last else refs[6:7]
        refs = refs[6 + len(outs) :]
        normed_ref, grad_ref, far_ref, total, back, delta = refs[:6]
        up, down, up_sems, down_sems, beside_sems, state_sems, tall_sums, wide_sums = refs[6:]
        at = pl.program_id(0)
        slot = lax.rem(at, 2)

        def up_copies(index, into):
            start = pl.multiple_of((2 * first + index) * step, step)
            copies = []
            for which, (dx, dc, dy) in enumerate(NEAR):
                x, c, y = flip(place_ref[1], dx), flip(place_ref[2], dc), flip(place_ref[3], dy)
                copies.append(
                    pltpu.make_async_copy(
                        up_refs[which].at[:, :, pl.ds(start, step)],
                        up.at[into, :, x, c, y],
                        up_sems.at[into, which],
                    )
                )
            return copies

        def down_copies(index, into, turn):
            x = lax.rem(index, 2)
            return [
                pltpu.make_async_copy(
                    down_refs[2 * turn + dc].at[x],
                    down.at[into, flip(place_ref[2], dc), :, pl.ds(0, rows - beside * lines)],
                    down_sems.at[into, dc],
                )
                for dc in range(2)
            ]

        def beside_copies(index, into, dx):
            copies = []
            for dc in range(2):
                for dy in range(2):
                    which = NEAR.index((dx, dc, dy))
                    c, y = flip(place_ref[2], dc), flip(place_ref[3], dy)
                    for part in range(beside):
                        copies.append(
                            pltpu.make_async_copy(
                                up_refs[which].at[
                                    first + index // 2, :, pl.ds(hidden_width + part * width, width)
                                ],
                                down.at[into, c, y, pl.ds(rows - (beside - part) * lines, lines)],
                                beside_sems.at[into, len(copies)],
                            )
                        )
            return copies

        def begin(index, into):
            for copy in up_copies(index, into):
                copy.start()
            away = lax.rem(place_ref[0] + depth - first - index // 2, depth)
            for turn in range(depth):
                @pl.when(away == turn)
                def _():
                    for copy in down_copies(index, into, turn):
                        copy.start()
            for dx in range(2):
                @pl.when(flip(place_ref[1], dx) == lax.rem(index, 2))
                def _():
                    for copy in beside_copies(index, into, dx):
                        copy.start()

        normed_copy = pltpu.make_async_copy(normed_in, normed_ref, state_sems.at[0])
        grad_copy = pltpu.make_async_copy(grad_in, grad_ref, state_sems.at[1])
        out_copy = pltpu.make_async_copy(out_in, total, state_sems.at[2])
        if first:
            back_copy = pltpu.make_async_copy(back_in, back, state_sems.at[3])
        back_away = pltpu.make_async_copy(back, back_out, state_sems.at[5])
        if last:
            far_copy = pltpu.make_async_copy(far_in, far_ref, state_sems.at[4])
            away = [
                pltpu.make_async_copy(
                    total.at[pl.ds(0, half)], outs[0].at[place_ref[3]], state_sems.at[6]
                ),
                pltpu.make_async_copy(delta, outs[1], state_sems.at[7]),
            ]
        else:
            away = [pltpu.make_async_copy(total, outs[0], state_sems.at[6])]

        @pl.when(at == 0)
        def _():
            normed_copy.start()
            begin(0, 0)
            grad_copy.start()
            out_copy.start()
            if first:
                back_copy.start()
            else:
                back[...] = jnp.zeros((tokens, width), F32)
            if last:
                far_copy.start()
            normed_copy.wait()

        @pl.when(at + 1 < steps)
        def _():
            begin(at + 1, 1 - slot)

        for copy in up_copies(at, slot):
            copy.wait()
        up_part = flat(up[slot])
        before_gelu = contract(normed_ref[...], up_part, 1, 0) + bias_ref[...]
        hidden, slope = gelu_both(before_gelu)
        hidden = hidden.astype(BF16)

        @pl.when(at == 0)
        def _():
            grad_copy.wait()

        tall = contract(hidden, grad_ref[...], 0, 0).astype(BF16)
        tall_sums[...] = tall.reshape(tall_sums.shape)
        tall_mine[0] = tall_sums[place_ref[2]]
        tall_other[0] = tall_sums[1 - place_ref[2]]

        for copy in down_copies(at, slot, 0) + beside_copies(at, slot, 0):
            copy.wait()

        @pl.when(at == 0)
        def _():
            out_copy.wait()
            if first:
                back_copy.wait()
            if last:
                far_copy.wait()

        down_part = flat(down[slot])
        total[...] += contract(hidden, down_part, 1, 0)

        @pl.when(at == steps - 1)
        def _():
            if last:
                delta[...] = (total[half:] - far_ref[...].astype(F32)).astype(BF16)
            for copy in away:
                copy.start()

        low = (contract(grad_ref[...], down_part, 1, 1) * slope).astype(BF16)
        back[...] += contract(low, up_part, 1, 1)

        @pl.when(at == steps - 1)
        def _():
            back_away.start()

        sum_ref[...] = column(low.astype(F32))
        broad = contract(normed_ref[...], low, 0, 0).astype(BF16)
        wide_sums[...] = broad.reshape(wide_sums.shape)
        wide_mine[...] = wide_sums[:, place_ref[2]]
        wide_other[...] = wide_sums[:, 1 - place_ref[2]]

        @pl.when(at == steps - 1)
        def _():
            for copy in away + [back_away]:
                copy.wait()

    tall_spec = pl.BlockSpec((1, 2 * rows, width), lambda i, _: (i, 0, 0))
    broad_spec = pl.BlockSpec((2 * depth, group // 2, step), lambda i, _: (0, 0, offset + i))
    sum_spec = pl.BlockSpec((1, step), lambda i, _: (0, i))
    out_specs = [tall_spec, tall_spec, broad_spec, broad_spec, sum_spec, whole_ref()]
    out_shape = [shape_of(BF16, steps, 2 * rows, width)] * 2
    out_shape += [shape_of(BF16, 2 * depth, group // 2, columns)] * 2
    out_shape += [shape_of(F32, 1, steps * step), shape_of(F32, tokens, width)]
    if last:
        out_specs += [whole_ref()] * 2
        out_shape += [shape_of(F32, 2, half, width), shape_of(BF16, half, width)]
    else:
        out_specs += [whole_ref()]
        out_shape += [shape_of(F32, tokens, width)]
    scratch = [
        pltpu.VMEM((tokens, width), BF16),
        pltpu.VMEM((tokens, width), BF16),
        pltpu.VMEM((half, width), BF16),
        pltpu.VMEM((tokens, width), F32),
        pltpu.VMEM((tokens, width), F32),
        pltpu.VMEM((half, width), BF16),
        pltpu.VMEM((2, depth, 2, 2, 2, group // 4, step), BF16),
        pltpu.VMEM((2, 2, 2, rows, width), BF16),
        pltpu.SemaphoreType.DMA((2, 8)),
        pltpu.SemaphoreType.DMA((2, 2)),
        pltpu.SemaphoreType.DMA((2, 4 * beside)),
        pltpu.SemaphoreType.DMA((8,)),
        pltpu.VMEM((2, 2 * rows, width), BF16),
        pltpu.VMEM((2 * depth, 2, group // 2, step), BF16),
    ]
    args = (place, up_bias, normed, grad_low, far) + tuple(state) + tuple(up_parts) + tuple(down_parts)
    alias = {len(args) + i: 2 + i for i in range(len(before))}
    return call(
        body,
        "feed_forward",
        (steps,),
        [pl.BlockSpec((1, step), lambda i, _: (0, 2 * first + i))]
        + [whole_ref()] * (5 + 8 + 2 * depth + len(before)),
        out_specs,
        out_shape,
        args + tuple(before),
        scratch=scratch,
        vmem=56,
        alias=alias,
    )


def middle_back(place, grad_normed, middle, gain, grad_out, far, right):
    half, width = far.shape
    step = 256
    parts = half // step

    def body(place_ref, grad_ref, middle_ref, gain_ref, own_ref, far_ref, *refs):
        right_refs = refs[:8]
        total_ref, low_ref, mixed_ref = refs[8:11]
        sums = refs[11:14]
        weight, sems = refs[14:]
        at = pl.program_id(0)

        def copies():
            return parts_copies(place_ref, right_refs, weight, sems, width, width, 0, 0)

        @pl.when(at == 0)
        def _():
            for copy in copies():
                copy.start()
            for ref in sums:
                ref[...] = jnp.zeros_like(ref)

        grad_normed = grad_ref[...]
        unit, scale = norm_parts(middle_ref[...])
        out_grad = jnp.where(at < parts, own_ref[0], far_ref[...].astype(F32))
        total = out_grad + norm_back(unit, scale, gain_ref[...], grad_normed)
        total_ref[...] = total
        low = total.astype(BF16)
        low_ref[...] = low
        sums[0][...] += column(grad_normed * unit)
        sums[1][...] += column(grad_normed)
        sums[2][...] += column(low.astype(F32))

        @pl.when(at == 0)
        def _():
            for copy in copies():
                copy.wait()

        mixed_ref[...] = contract(low, flat(weight[...]), 1, 1).astype(BF16)

    here = pl.BlockSpec((step, width), lambda i, _: (i, 0))
    vector = pl.BlockSpec((1, width), lambda i, _: (0, 0))
    tokens = 2 * half
    return call(
        body,
        "middle_back",
        (2 * parts,),
        [here, here, held(1, width), own_spec(step, width, parts), far_spec(step, width, parts)]
        + [whole_ref()] * 8,
        [here, here, here, vector, vector, vector],
        [shape_of(F32, tokens, width), shape_of(BF16, tokens, width), shape_of(BF16, tokens, width)]
        + [shape_of(F32, 1, width)] * 3,
        (place, grad_normed, middle, gain, grad_out, far) + tuple(right),
        scratch=[weight_scratch(right[0], width), pltpu.SemaphoreType.DMA((1, 8))],
        vmem=56,
    )


def input_back(place, grads, left, right, inputs, far, gain, middle_grad, far_grad):
    half, width = far.shape
    step = 256
    parts = half // step

    def body(
        place_ref, query_ref, key_ref, value_ref, own_ref, far_ref, gain_ref, middle_ref, far_grad_ref, *refs
    ):
        left_refs, right_refs = refs[:8], refs[8:16]
        out_ref, delta_ref = refs[16:18]
        sums = refs[18:22]
        gain_sum_ref, shift_sum_ref, query_sum_ref, value_sum_ref = sums
        weight, sems = refs[22:]
        at = pl.program_id(0)

        def copies():
            result = []
            for chunk, part_refs in enumerate((left_refs, left_refs, right_refs)):
                result += parts_copies(
                    place_ref, part_refs, weight, sems, (chunk % 2) * width, width, chunk * width, chunk
                )
            return result

        @pl.when(at == 0)
        def _():
            for copy in copies():
                copy.start()
            for ref in sums:
                ref[...] = jnp.zeros_like(ref)

        @pl.when(at == 0)
        def _():
            for copy in copies():
                copy.wait()

        def part(chunk):
            return flat(weight[:, :, :, :, :, chunk * width : (chunk + 1) * width])

        grad_normed = contract(query_ref[...], part(0), 1, 1)
        grad_normed += contract(key_ref[...], part(1), 1, 1)
        grad_normed += contract(value_ref[...], part(2), 1, 1)
        rows = jnp.where(at < parts, own_ref[0], far_ref[...].astype(F32))
        unit, scale = norm_parts(rows)
        gain_sum_ref[...] += column(grad_normed * unit)
        shift_sum_ref[...] += column(grad_normed)
        query_sum_ref[...] += column(query_ref[...].astype(F32))
        value_sum_ref[...] += column(value_ref[...].astype(F32))
        result = middle_ref[...] + norm_back(unit, scale, gain_ref[...], grad_normed)

        @pl.when(at < parts)
        def _():
            out_ref[0] = result

        @pl.when(at >= parts)
        def _():
            delta_ref[...] = (result - far_grad_ref[...].astype(F32)).astype(BF16)

    here = pl.BlockSpec((step, width), lambda i, _: (i, 0))
    vector = pl.BlockSpec((1, width), lambda i, _: (0, 0))
    return call(
        body,
        "input_back",
        (2 * parts,),
        [
            here,
            here,
            here,
            own_spec(step, width, parts),
            far_spec(step, width, parts),
            held(1, width),
            here,
            far_spec(step, width, parts),
        ]
        + [whole_ref()] * 16,
        [own_spec(step, width, parts), far_spec(step, width, parts), vector, vector, vector, vector],
        [shape_of(F32, 2, half, width), shape_of(BF16, half, width)] + [shape_of(F32, 1, width)] * 4,
        (place,) + tuple(grads) + (inputs, far, gain, middle_grad, far_grad) + tuple(left) + tuple(right),
        scratch=[weight_scratch(left[0], 3 * width), pltpu.SemaphoreType.DMA((3, 8))],
        vmem=56,
    )


def split_add(place, mine, came, spot):
    groups, _, rows, columns = mine.shape

    def body(place_ref, mine_ref, came_ref, sent_ref, kept_ref):
        for ref, at in ((sent_ref, 1 - place_ref[spot]), (kept_ref, place_ref[spot])):
            ref[0] = (mine_ref[0, at].astype(F32) + came_ref[0, at].astype(F32)).astype(BF16)

    block = pl.BlockSpec((1, 2, rows, columns), lambda i, _: (i, 0, 0, 0))
    out = pl.BlockSpec((1, rows, columns), lambda i, _: (i, 0, 0))
    return call(
        body,
        "split_add",
        (groups,),
        [block, block],
        [out, out],
        [shape_of(BF16, groups, rows, columns)] * 2,
        (place, mine, came),
        vmem=8,
    )


def split_depth(place, pairs, rows):
    depth = pairs[0][0].shape[0]
    layout = [(which, part) for which, (mine, _) in enumerate(pairs) for part in range(mine.shape[1] // rows)]
    total = sum(pairs[which][0].shape[2] for which, _ in layout)

    def body(place_ref, *refs):
        outs = refs[2 * len(pairs) :]
        for step, ref in enumerate(outs):
            at = lax.rem(place_ref[0] + step, depth)
            start = 0
            for which, part in layout:
                width = pairs[which][0].shape[2]
                cut = pl.ds(part * rows, rows)
                value = refs[2 * which][at, cut].astype(F32) + refs[2 * which + 1][at, cut].astype(F32)
                ref[:, start : start + width] = value.astype(ref.dtype)
                start += width

    return call(
        body,
        "split_depth",
        (1,),
        [held(*mine.shape) for mine, _ in pairs for _ in range(2)],
        [held(rows, total)] * depth,
        [shape_of(F32, rows, total)] + [shape_of(BF16, rows, total)] * (depth - 1),
        (place,) + tuple(value for pair in pairs for value in pair),
        vmem=12,
    )


def last_add(place, own, came, shapes):
    rows, total = own.shape
    layout = [(which, part) for which, shape in enumerate(shapes) for part in range(shape[0] // rows)]

    def body(place_ref, own_ref, *refs):
        outs = refs[len(came) :]
        start = 0
        for which, part in layout:
            width = shapes[which][1]
            value = own_ref[:, start : start + width]
            for ref in refs[: len(came)]:
                value = value + ref[:, start : start + width].astype(F32)
            outs[which][part * rows : (part + 1) * rows] = value
            start += width

    return call(
        body,
        "last_add",
        (1,),
        [held(rows, total)] * (1 + len(came)),
        [held(*shape) for shape in shapes],
        [shape_of(F32, *shape) for shape in shapes],
        (place, own) + tuple(came),
        vmem=12,
    )


def spread_rows(count, per, size, row):
    span = size * per
    lane = lax.broadcasted_iota(jnp.int32, (per, count * span), 1)
    line = lax.broadcasted_iota(jnp.int32, (per, count * span), 0)
    return jnp.where(lane % span == row * per + line, 1.0, 0.0)


def chosen_rows(count, span):
    lane = lax.broadcasted_iota(jnp.int32, (count, count * span), 1)
    line = lax.broadcasted_iota(jnp.int32, (count, count * span), 0)
    return lane // span == line


def small_vectors(place, right, start, sizes, per):
    depth, rows, _ = right[0].shape
    count = depth * 8

    def body(place_ref, *refs):
        part_refs, outs, held_rows = refs[:8], refs[8:-1], refs[-1]
        for at, (dx, dc, dy) in enumerate(NEAR):
            x, c, y = flip(place_ref[1], dx), flip(place_ref[2], dc), flip(place_ref[3], dy)
            held_rows[:, x, c, y] = part_refs[at][...].astype(F32)
        table = held_rows[...].reshape(count, rows, PAIR)
        at = 0
        for ref, size in zip(outs, sizes):
            chosen = chosen_rows(count, size * per)
            line = jnp.zeros((1, count * size * per), F32)
            for row in range(size):
                spread = spread_rows(count, per, size, row).astype(BF16)
                wide = contract(table[:, at + row, :per].astype(BF16), spread, 1, 0)
                line += column(jnp.where(chosen, wide, 0.0))
            at += size
            ref[...] = line

    return call(
        body,
        "small_vectors",
        (1,),
        [pl.BlockSpec((depth, rows, PAIR), lambda i, _: (0, 0, start // PAIR))] * 8,
        [held(1, count * size * per) for size in sizes],
        [shape_of(F32, 1, count * size * per) for size in sizes],
        (place,) + tuple(right),
        scratch=[pltpu.VMEM((depth, 2, 2, 2, rows, PAIR), F32)],
        vmem=12,
    )


def merge_add(place, mine, came, spot):
    counts = [part.shape[0] for part in mine]
    _, _, rows, columns = mine[0].shape

    def body(place_ref, *refs):
        sent_ref, kept_ref = refs[2 * len(mine) :]
        start = 0
        for which, count in enumerate(counts):
            for ref, at in ((sent_ref, 1 - place_ref[spot]), (kept_ref, place_ref[spot])):
                total = refs[which][:, at].astype(F32) + refs[len(mine) + which][:, at].astype(F32)
                ref[start : start + count] = total.astype(BF16)
            start += count

    shape = (sum(counts), rows, columns)
    return call(
        body,
        "merge_add",
        (1,),
        [held(*part.shape) for part in mine + came],
        [held(*shape)] * 2,
        [shape_of(BF16, *shape)] * 2,
        (place,) + tuple(mine) + tuple(came),
        vmem=12,
    )


def beside_add(place, mine, came, spot):
    groups, _, rows, _ = mine[0].shape
    widths = [part.shape[-1] for part in mine]

    def body(place_ref, *refs):
        sent_ref, kept_ref = refs[2 * len(mine) :]
        for ref, at in ((sent_ref, 1 - place_ref[spot]), (kept_ref, place_ref[spot])):
            start = 0
            for which, width in enumerate(widths):
                total = refs[which][:, at].astype(F32) + refs[len(mine) + which][:, at].astype(F32)
                ref[:, :, start : start + width] = total.astype(BF16)
                start += width

    shape = (groups, rows, sum(widths))
    return call(
        body,
        "beside_add",
        (1,),
        [held(*part.shape) for part in mine + came],
        [held(*shape)] * 2,
        [shape_of(BF16, *shape)] * 2,
        (place,) + tuple(mine) + tuple(came),
        vmem=12,
    )


def attn_forward_kernel(q_ref, k_ref, v_ref, bias_ref, prob_ref, mixed_ref, total_ref):
    tokens, lanes = q_ref.shape
    half = lanes // 2
    lane = lax.broadcasted_iota(jnp.int32, (tokens, lanes), 1)
    block = lax.broadcasted_iota(jnp.int32, (tokens, lanes), 0) // BLOCK
    scale = half ** -0.5
    q = q_ref[...].astype(jnp.float32) * scale
    k = k_ref[...].astype(jnp.float32)
    v = v_ref[...].astype(jnp.float32)
    sides = []
    for head in range(2):
        own = (lane >= half) if head else (lane < half)
        first = 0 if head else half
        bias = jnp.broadcast_to(bias_ref[head][:, None, :], (tokens // BLOCK, BLOCK, lanes)).reshape(tokens, lanes)
        q_ext = jnp.where(own, q, jnp.where(lane - first == block, 1.0, 0.0)).astype(jnp.bfloat16)
        k_ext = jnp.where(own, k, bias).astype(jnp.bfloat16)
        v_ext = jnp.where(own, v, 1.0).astype(jnp.bfloat16)
        sides.append((q_ext, k_ext, v_ext))
    rows = min(512, tokens)
    low_lane = lax.broadcasted_iota(jnp.int32, (rows, lanes), 1) < half
    for start in range(0, tokens, rows):
        sums = []
        for head, (q_ext, k_ext, v_ext) in enumerate(sides):
            scores = contract(q_ext[start:start + rows], k_ext, 1, 1)
            top = jnp.max(scores, axis=1, keepdims=True)
            prob = jnp.exp(scores - top).astype(jnp.bfloat16)
            prob_ref[head, start:start + rows, :] = prob
            sums.append(contract(prob, v_ext, 1, 0))
        result = jnp.where(low_lane, sums[0], sums[1])
        totals = pltpu.roll(jnp.where(low_lane, sums[1], sums[0]), half, 1)
        mixed_ref[start:start + rows, :] = (result / totals).astype(jnp.bfloat16)
        total_ref[start:start + rows, :] = totals

def attn_backward_kernel(q_ref, k_ref, v_ref, prob_ref, mixed_ref, total_ref, grad_ref, dq_ref, dk_ref, dv_ref):
    tokens, lanes = q_ref.shape
    half = lanes // 2
    scale = half ** -0.5
    lane = lax.broadcasted_iota(jnp.int32, (tokens, lanes), 1)
    grad = grad_ref[...].astype(jnp.float32) / total_ref[...]
    inner = grad * mixed_ref[...].astype(jnp.float32)
    grad_low = grad.astype(jnp.bfloat16)
    q_turned = q_ref[...].T
    grad_turned = grad_low.T
    v = v_ref[...].astype(jnp.float32)
    k = k_ref[...]
    rows = 256
    low_lane = lax.broadcasted_iota(jnp.int32, (rows, lanes), 1) < half
    dq = [[None, None] for _ in range(tokens // rows)]
    dk, dv = [], []
    for head in range(2):
        own = (lane >= half) if head else (lane < half)
        first = 0 if head else half
        minus = -jnp.sum(jnp.where(own, inner, 0.0), axis=1, keepdims=True)
        high = minus.astype(jnp.bfloat16).astype(jnp.float32)
        grad_ext = jnp.where(own, grad, jnp.where(lane == first, high, jnp.where(lane == first + 1, minus - high, 0.0))).astype(jnp.bfloat16)
        v_ext = jnp.where(own, v, jnp.where(lane - first < 2, 1.0, 0.0)).astype(jnp.bfloat16)
        dk_sum = dv_sum = None
        for index in range(tokens // rows):
            part = slice(index * rows, (index + 1) * rows)
            prob = prob_ref[head, part, :]
            spread = contract(grad_ext[part], v_ext, 1, 1)
            grad_scores = (prob.astype(jnp.float32) * spread).astype(jnp.bfloat16)
            dq[index][head] = contract(grad_scores, k, 1, 0)
            rows_of = slice(head * half, (head + 1) * half)
            dk_part = contract(q_turned[rows_of, part], grad_scores, 1, 0)
            dv_part = contract(grad_turned[rows_of, part], prob, 1, 0)
            dk_sum = dk_part if dk_sum is None else dk_sum + dk_part
            dv_sum = dv_part if dv_sum is None else dv_sum + dv_part
        dk.append(dk_sum)
        dv.append(dv_sum)
    for index, pair in enumerate(dq):
        dq_ref[index * rows:(index + 1) * rows, :] = (jnp.where(low_lane, pair[0], pair[1]) * scale).astype(jnp.bfloat16)
    dk_ref[...] = (jnp.concatenate(dk, axis=0) * scale).T.astype(jnp.bfloat16)
    dv_ref[...] = jnp.concatenate(dv, axis=0).T.astype(jnp.bfloat16)


def attn_forward(place, qkv, bias, first, count, before=()):
    tokens, width = qkv.shape[0], qkv.shape[1] // 3
    pairs = width // PAIR

    def at(part):
        return pl.BlockSpec((tokens, PAIR), lambda i, _: (0, part * pairs + first + i))

    def body(place_ref, *refs):
        attn_forward_kernel(*refs[:4], *refs[4 + len(before) :])

    return call(
        body,
        "attn_forward",
        (count,),
        [at(0), at(1), at(2), pl.BlockSpec((2, tokens // BLOCK, PAIR), lambda i, _: (first + i, 0, 0))]
        + [whole_ref()] * len(before),
        [pl.BlockSpec((2, tokens, tokens), lambda i, _: (first + i, 0, 0)), at(0), at(0)],
        [
            shape_of(BF16, 2 * pairs, tokens, tokens),
            shape_of(BF16, tokens, width),
            shape_of(F32, tokens, width),
        ],
        (place, qkv, qkv, qkv, bias) + tuple(before),
        vmem=28,
        alias={5 + i: i for i in range(len(before))},
    )


def attn_backward(place, qkv, prob, mixed, total, grad, first, count, before=()):
    tokens, width = qkv.shape[0], qkv.shape[1] // 3
    pairs = width // PAIR

    def at(part):
        return pl.BlockSpec((tokens, PAIR), lambda i, _: (0, part * pairs + first + i))

    def body(place_ref, *refs):
        attn_backward_kernel(*refs[:7], *refs[7 + len(before) :])

    return call(
        body,
        "attn_backward",
        (count,),
        [at(0), at(1), at(2), pl.BlockSpec((2, tokens, tokens), lambda i, _: (first + i, 0, 0))]
        + [at(0)] * 3
        + [whole_ref()] * len(before),
        [at(0)] * 3,
        [shape_of(BF16, tokens, width)] * 3,
        (place, qkv, qkv, qkv, prob, mixed, total, grad) + tuple(before),
        vmem=28,
        alias={8 + i: i for i in range(len(before))},
    )


def key_bias(random_ids, block_ids):
    heads, blocks, _ = random_ids.shape
    row, col = block_ids[:, None], block_ids[None, :]
    last = blocks - 1
    fixed = (row == 0) | (row == last) | (col == 0) | (col == last) | (jnp.abs(row - col) <= 1)
    drawn = jnp.any(random_ids[:, :, :, None] == block_ids, axis=2)
    bias = jnp.where(fixed[None] | drawn, 0.0, -1e30)
    bias = bias.transpose(0, 2, 1).reshape(heads // 2, 2, blocks, blocks)
    lanes = 128
    even = jnp.pad(bias[:, 0], ((0, 0), (0, 0), (lanes // 2, lanes // 2 - blocks)))
    odd = jnp.pad(bias[:, 1], ((0, 0), (0, 0), (0, lanes - blocks)))
    return jnp.stack([even, odd], axis=1).reshape(heads, blocks, lanes)


def pair_swap(value, axis, bit):
    size = lax.axis_size(axis)
    return lax.ppermute(value, axis, [(i, i ^ bit) for i in range(size)])


def pick(value, index, axis):
    return lax.dynamic_index_in_dim(value, index, axis, keepdims=False)


def swap_x(value):
    return pair_swap(value, "dp", 2)


def swap_core(value):
    return pair_swap(value, "dp", 1)


def swap_y(value):
    return pair_swap(value, "seq", 1)


def ring_z(value, step):
    size = lax.axis_size("dp")
    return lax.ppermute(value, "dp", [(i, (i + 4 * step) % size) for i in range(size)])


def tie(*values):
    return lax.optimization_barrier(values)


def swap_core_sum(values):
    return values + swap_core(values)


def sum_depth(values):
    total = values
    for step in range(1, lax.axis_size("dp") // 4):
        total = total + ring_z(values, step)
    return total


class Reduce:
    def __init__(self, place, rows, x_first):
        self.place, self.rows, self.x_first = place, rows, x_first

    def begin(self, mine, other):
        self.mine, self.came = mine, swap_core(other)

    def first(self):
        groups, tall, columns = self.mine.shape
        if self.x_first:
            shape = (groups // 2, 2, tall, columns)
        else:
            shape = (groups, 2, self.rows, columns)
        spot, swap = (1, swap_x) if self.x_first else (3, swap_y)
        sent, kept = split_add(self.place, self.mine.reshape(shape), self.came.reshape(shape), spot)
        self.mine, self.came = kept, swap(sent)

    def second(self, *others, beside=False):
        spot, swap = (3, swap_y) if self.x_first else (1, swap_x)
        mine, came = [], []
        for part in (self,) + others:
            shape = (-1, 2, self.rows, part.mine.shape[-1])
            mine.append(part.mine.reshape(shape))
            came.append(part.came.reshape(shape))
        if beside:
            sent, kept = beside_add(self.place, mine, came, spot)
        elif others:
            sent, kept = merge_add(self.place, mine, came, spot)
        else:
            sent, kept = split_add(self.place, mine[0], came[0], spot)
        self.mine, self.came = kept, swap(sent)

    def third(self, *others):
        parts = (self,) + others
        rows = min(part.rows for part in parts)
        own, *sent = split_depth(self.place, [(part.mine, part.came) for part in parts], rows)
        self.mine = own
        self.came = [ring_z(block, step + 1) for step, block in enumerate(sent)]

    def last(self, *shapes):
        return last_add(self.place, self.mine, self.came, shapes)

    def hold(self, *others):
        self.mine, self.came, others = tie(self.mine, self.came, others)
        return others


def split_depth_spot(place_ref, step, depth):
    return lax.rem(place_ref[0] + depth - step, depth)


def join_depth(place, blocks, cuts, name):
    depth = len(blocks)
    rows = blocks[0].shape[0]
    moves = []
    for step in range(depth):
        for j, (start, stop) in enumerate(cuts):
            cut = (slice(None), slice(start, stop))
            moves.append((step, cut, j, lambda p, step=step: split_depth_spot(p, step, depth)))
    return join(place, blocks, moves, [(depth, rows, stop - start) for start, stop in cuts], name)


def join_plane(place, blocks):
    moves = []
    for at, (dx, dy) in enumerate(((0, 0), (1, 0), (0, 1), (1, 1))):
        moves.append(
            (at, (), 0, lambda p, dx=dx, dy=dy: (flip(p[1], dx), flip(p[3], dy)))
        )
    return join(place, blocks, moves, [(2, 2) + blocks[0].shape], "join_plane")[0]


def near_parts(own, by_x, by_y, by_xy, cores):
    blocks = {(0, 0): own, (1, 0): by_x, (0, 1): by_y, (1, 1): by_xy}
    return [cores[dx, dy] if dc else blocks[dx, dy] for dx, dc, dy in NEAR]


def paired(inputs, grad_out, random_blocks, *shards):
    depth = lax.axis_size("dp") // 4
    dp, y = lax.axis_index("dp"), lax.axis_index("seq")
    z, x, c = dp // 4, (dp // 2) % 2, dp % 2
    spots = (z, x, c, y)
    place = jnp.stack(spots).astype(jnp.int32)
    w_query, w_key, w_value, w_out, w_up, w_down = shards[:6]
    vectors = shards[6:]
    half, width = inputs.shape[1:]
    rows, tall_rows, hidden_width = w_up.shape[0], w_down.shape[0], w_up.shape[1]
    pairs = width // PAIR
    ring = range(1, depth)

    sizes = [vector.shape[0] // rows for vector in vectors]
    small = jnp.concatenate([vector.reshape(-1, rows) for vector in vectors])
    small = jnp.pad(small, ((0, rows - small.shape[0]), (0, PAIR - rows)))
    shard = join_beside(place, [w_query, w_key, w_value, w_out, small])
    turned = [shard] + [ring_z(shard, step) for step in ring]
    tall_half = tall_rows // 2
    down_near, down_own = w_down[tall_half:], w_down[:tall_half]
    down_x = swap_x(down_own)
    far_rows = swap_y(cast_far(place, inputs))
    up_shard = join_beside(
        place, [w_up] + [down_near[start : start + rows] for start in range(0, tall_half, rows)]
    )
    turned, down_x, far_rows, up_shard, down_own, random_blocks, grad_out = tie(
        turned, down_x, far_rows, up_shard, down_own, random_blocks, grad_out
    )
    cut = 2 * width
    left, right = join_depth(place, turned, [(0, cut), (cut, shard.shape[1])], "join_first")
    left_y, right_x = swap_y(left), swap_x(right)
    up_turned = {1: ring_z(up_shard, 1), depth - 1: ring_z(up_shard, depth - 1)}
    down_y, down_xy = swap_y(down_own), swap_y(down_x)
    random_far = swap_y(pick(random_blocks, 1 - y, 0))
    far_grad_low = cast_far(place, grad_out)
    left_y, right_x, up_turned, down_own, down_x, down_y, down_xy, far_grad_low, random_far = tie(
        left_y, right_x, up_turned, down_own, down_x, down_y, down_xy, far_grad_low, random_far
    )
    left_x, left_xy = swap_x(left), swap_x(left_y)
    right_y, right_xy = swap_y(right), swap_y(right_x)
    for step in ring:
        if step not in up_turned:
            up_turned[step] = ring_z(up_shard, step)
    plane = join_plane(place, [down_own, down_x, down_y, down_xy])
    local_blocks = half // BLOCK
    ids = jnp.arange(2 * local_blocks, dtype=jnp.int32)
    block_ids = (ids + y * local_blocks) % (2 * local_blocks)
    random_ids = jnp.concatenate([pick(random_blocks, y, 0), random_far], axis=1)
    bias = key_bias(random_ids, block_ids)
    left_x, left_xy, right_y, right_xy, up_turned, left_y, right_x, plane, bias = tie(
        left_x, left_xy, right_y, right_xy, up_turned, left_y, right_x, plane, bias
    )
    (up_own,) = join_depth(
        place, [up_shard] + [up_turned[step] for step in ring], [(0, up_shard.shape[1])], "join_up"
    )
    left_core = {
        (0, 0): swap_core(left), (0, 1): swap_core(left_y),
        (1, 0): swap_core(left_x), (1, 1): swap_core(left_xy),
    }
    right_core = {
        (0, 0): swap_core(right), (0, 1): swap_core(right_y),
        (1, 0): swap_core(right_x), (1, 1): swap_core(right_xy),
    }
    left_parts = near_parts(left, left_x, left_y, left_xy, left_core)
    right_parts = near_parts(right, right_x, right_y, right_xy, right_core)
    left_parts, right_parts, plane, up_own = tie(left_parts, right_parts, plane, up_own)

    up_y, up_x = swap_y(up_own), swap_x(up_own)
    planes = {0: plane, 1: ring_z(plane, 1), depth - 1: ring_z(plane, depth - 1)}
    up_core = {(0, 0): swap_core(up_own)}
    spans = small_vectors(place, right_parts, cut, sizes, rows)
    (
        ln1_gain,
        ln1_bias,
        query_bias,
        value_bias,
        out_bias,
        ln2_gain,
        ln2_bias,
        up_bias,
        down_bias,
    ) = spans
    qkv_bias = jnp.concatenate([query_bias, jnp.zeros_like(query_bias), value_bias], axis=1)
    normed_low, qkv = norm_project(
        place, inputs, far_rows, ln1_gain, ln1_bias, left_parts, right_parts, qkv_bias
    )
    attended = attn_forward(place, qkv, bias, 0, pairs // 2)
    attended, up_y, up_x, planes, up_core, far_grad_low = tie(
        attended, up_y, up_x, planes, up_core, far_grad_low
    )
    up_xy = swap_x(up_y)
    up_core[0, 1] = swap_core(up_y)
    up_core[1, 0] = swap_core(up_x)
    far_grad = swap_y(far_grad_low)
    for step in ring:
        if step not in planes:
            planes[step] = ring_z(planes[0], step)
    prob, mixed_low, totals = attn_forward(
        place, qkv, bias, pairs // 2, pairs - pairs // 2, attended
    )
    mixed_low, far_grad, planes, up_core = tie(mixed_low, far_grad, planes, up_core)
    plane_core = {0: swap_core(planes[0])}
    for step in ring:
        plane_core[step] = swap_core(planes[step])
    grad_ff_low, grad_down_bias = join_low(place, grad_out, far_grad)
    mixed_low, grad_ff_low = tie(mixed_low, grad_ff_low)
    middle, normed_two_low, start_out = out_norm(
        place, mixed_low, right_parts, out_bias, inputs, far_rows, ln2_gain, ln2_bias, down_bias
    )
    normed_two_low, up_xy, plane_core = tie(normed_two_low, up_xy, plane_core)
    up_core[1, 1] = swap_core(up_xy)
    up_parts = near_parts(up_own, up_x, up_y, up_xy, up_core)
    down_parts = [part for step in range(depth) for part in (planes[step], plane_core[step])]

    down_sums = [Reduce(place, tall_rows, True) for _ in range(3)]
    near_sum = Reduce(place, rows, False)
    wide_sum = Reduce(place, rows, True)
    out_sum = Reduce(place, rows, True)
    left_sum = Reduce(place, rows, True)
    right_sum = Reduce(place, rows, False)

    def feed(first, count, state, wide):
        return feed_forward(
            place, first, count, depth, normed_two_low, grad_ff_low, up_parts, down_parts, up_bias,
            far_rows, state, wide,
        )

    near = depth // 2
    near_width = hidden_width // 2
    each = hidden_width // depth
    mine, other, up_mine, up_other, bias_0, back, total = feed(
        0, near, (start_out, start_out), (near_width, 0, ())
    )
    down_sums[0].begin(mine, other)
    near_sum.begin(up_mine, up_other)
    mine, other, up_mine, up_other, bias_1, back, total = feed(
        near, depth - 1 - near, (total, back), (near_width, 0, ())
    )
    (back,) = down_sums[0].hold(back)
    (back,) = near_sum.hold(back)
    down_sums[1].begin(mine, other)
    down_sums[0].first()
    near_sum.first()
    down_sums[0].mine, near_sum.mine, back = tie(down_sums[0].mine, near_sum.mine, back)
    mine, other, up_mine, up_other, bias_2, back, out_part, out_delta = feed(
        depth - 1, 1, (total, back), (near_width, (depth - 1 - near) * each, (up_mine, up_other))
    )
    (back,) = down_sums[0].hold(back)
    (back,) = near_sum.hold(back)
    (back,) = down_sums[1].hold(back)
    down_sums[2].begin(mine, other)
    wide_sum.begin(up_mine, up_other)
    down_sums[1].first()
    down_sums[1].mine, back = tie(down_sums[1].mine, back)
    grad_up_bias = jnp.concatenate([bias_0, bias_1, bias_2], axis=1)
    grad_middle, grad_attn_low, grad_mixed_low, grad_ln2_gain, grad_ln2_bias, grad_out_bias = middle_back(
        place, back, middle, ln2_gain, grad_out, far_grad, right_parts
    )
    out_sum.begin(*grad_wide(place, mixed_low, (grad_attn_low,), rows, 1))
    out_sum.mine, grad_mixed_low = tie(out_sum.mine, grad_mixed_low)
    (grad_mixed_low,) = down_sums[1].hold(grad_mixed_low)
    (grad_mixed_low,) = down_sums[2].hold(grad_mixed_low)
    (grad_mixed_low,) = wide_sum.hold(grad_mixed_low)
    down_sums[2].first()
    near_sum.second()
    down_sums[2].mine, near_sum.mine, grad_mixed_low, out_delta = tie(
        down_sums[2].mine, near_sum.mine, grad_mixed_low, out_delta
    )
    out_far = swap_y(out_delta)
    grads = attn_backward(place, qkv, prob, mixed_low, totals, grad_mixed_low, 0, pairs // 2)
    grads, out_far = tie(grads, out_far)
    (grads,) = near_sum.hold(grads)
    (grads,) = down_sums[2].hold(grads)
    (grads,) = out_sum.hold(grads)
    wide_sum.first()
    out_sum.first()
    near_sum.third()
    down_sums[0].second(*down_sums[1:])
    down_sum = down_sums[0]
    down_sum.mine, near_sum.mine, wide_sum.mine, out_sum.mine, grads = tie(
        down_sum.mine, near_sum.mine, wide_sum.mine, out_sum.mine, grads
    )
    grads = attn_backward(
        place, qkv, prob, mixed_low, totals, grad_mixed_low, pairs // 2, pairs - pairs // 2, grads
    )
    (grads,) = near_sum.hold(grads)
    (grads,) = wide_sum.hold(grads)
    (grads,) = down_sum.hold(grads)
    wide_sum.second()
    wide_sum.mine, grads = tie(wide_sum.mine, grads)
    wide = grad_wide(place, normed_low, grads, rows, 2)
    (wide,) = wide_sum.hold(wide)
    (wide,) = out_sum.hold(wide)
    out_sum.second()
    out_sum.mine, wide = tie(out_sum.mine, wide)
    left_sum.begin(*wide[:2])
    right_sum.begin(*wide[2:])
    (grad_up_near,) = near_sum.last((rows, near_width))
    left_sum.mine, grads, grad_up_near = tie(left_sum.mine, grads, grad_up_near)
    (grads,) = out_sum.hold(grads)
    (grads,) = left_sum.hold(grads)
    left_sum.first()
    (grads,) = right_sum.hold(grads)
    right_sum.first()
    down_sum.third()
    left_sum.mine, right_sum.mine, down_sum.mine, grads = tie(
        left_sum.mine, right_sum.mine, down_sum.mine, grads
    )
    in_part, in_delta, grad_ln1_gain, grad_ln1_bias, grad_query_bias, grad_value_bias = input_back(
        place, grads, left_parts, right_parts, inputs, far_rows, ln1_gain, grad_middle, far_grad
    )
    (in_delta,) = down_sum.hold(in_delta)
    (in_delta,) = left_sum.hold(in_delta)
    left_sum.second()
    (in_delta,) = right_sum.hold(in_delta)
    right_sum.second()
    wide_sum.third(out_sum)
    left_sum.mine, right_sum.mine, wide_sum.mine, in_delta, grad_ln1_gain = tie(
        left_sum.mine, right_sum.mine, wide_sum.mine, in_delta, grad_ln1_gain
    )
    grad_vectors = (
        grad_ln1_gain,
        grad_ln1_bias,
        grad_query_bias,
        grad_value_bias,
        grad_out_bias,
        grad_ln2_gain,
        grad_ln2_bias,
        grad_up_bias,
        grad_down_bias,
    )
    packed = jnp.concatenate(grad_vectors, axis=1)
    in_far = swap_y(in_delta)
    packed = swap_core_sum(packed.reshape(-1, PAIR))
    (packed,) = wide_sum.hold(packed)
    (packed,) = left_sum.hold(packed)
    (packed,) = right_sum.hold(packed)
    packed = sum_depth(packed)
    left_sum.third(right_sum)
    left_sum.mine, packed = tie(left_sum.mine, packed)
    packed = packed + swap_x(packed)
    packed = (packed + swap_y(packed)).reshape(-1)
    (grad_w_down,) = down_sum.last(w_down.shape)
    grad_up_far, grad_w_out = wide_sum.last((rows, near_width), w_out.shape)
    packed, out_far, grad_w_down, grad_up_far, in_far = tie(
        packed, out_far, grad_w_down, grad_up_far, in_far
    )
    left_sum.came, in_far, out_far = tie(left_sum.came, in_far, out_far)
    result = fill_far(place, out_part, inputs, out_far)
    grad_in = fill_far(place, in_part, grad_out, in_far)
    grad_w_up = jnp.concatenate([grad_up_near, grad_up_far], axis=1)
    square, part = (rows, width), (rows, width // 2)
    grad_left_q, grad_left_k, grad_right_k, grad_right_v = left_sum.last(square, part, part, square)
    out_vectors = []
    at = 0
    for vector in vectors:
        count = vector.shape[0]
        out_vectors.append(lax.dynamic_slice_in_dim(packed, at + (dp * 2 + y) * count, count))
        at += count * depth * 8
    grad_w_key = jnp.concatenate([grad_left_k, grad_right_k], axis=1)
    return (
        (result, grad_in, grad_left_q, grad_w_key, grad_right_v, grad_w_out, grad_w_up, grad_w_down)
        + tuple(out_vectors)
    )


def solution(mesh):
    tokens, table, matrix, vector = P("dp", "seq", None), P("dp", None, "seq", None), P(BOTH, None), P(BOTH)
    in_specs = (tokens, tokens, table) + (matrix,) * 6 + (vector,) * 9
    out_specs = (tokens, tokens) + (matrix,) * 6 + (vector,) * 9
    paired_fits = mesh.shape["seq"] == 2 and mesh.shape["dp"] % 4 == 0

    def body(inputs, *rest):
        whole = paired if paired_fits and inputs.shape[0] == 2 else on_device
        return whole(inputs, *rest)

    return jax.shard_map(
        body, mesh=mesh, in_specs=in_specs, out_specs=out_specs, check_vma=False
    )
```

```python
import jax
import jax.numpy as jnp
from jax import lax
from jax.experimental import pallas as pl
from jax.experimental.pallas import tpu as pltpu
from jax.sharding import PartitionSpec as P

HEADS = 16
BLOCK = 64
BOTH = ("dp", "seq")


eps_norm = 1e-05
neg_fill = -1e30


def layer_norm(values, norm_gain, norm_shift):
    centre = values - jnp.mean(values, axis=-1, keepdims=True)
    spread = jnp.mean(centre * centre, axis=-1, keepdims=True)
    return centre * lax.rsqrt(spread + eps_norm) * norm_gain + norm_shift


def gelu_tanh(values):
    return jax.nn.gelu(values, approximate=True)


def project(left, right):
    return jnp.dot(left, right, preferred_element_type=jnp.float32)


def project_back(grad_rows, weight):
    return lax.dot_general(
        grad_rows, weight, (((1,), (1,)), ((), ())), preferred_element_type=jnp.float32
    )


def weight_grad(left, grad_rows):
    return lax.dot_general(
        left, grad_rows, (((0,), (0,)), ((), ())), preferred_element_type=jnp.float32
    )


def column_sum(grad_rows):
    return jnp.sum(grad_rows, axis=0, dtype=jnp.float32)


def to_table(block_rows):
    block_count = block_rows.shape[0] // BLOCK
    head_dim = block_rows.shape[1] // HEADS
    shaped = block_rows.reshape(block_count, BLOCK, HEADS, head_dim)
    return shaped.transpose(2, 0, 1, 3).reshape(HEADS, block_count, BLOCK * head_dim)


def from_table(table):
    block_count = table.shape[1]
    head_dim = table.shape[2] // BLOCK
    shaped = table.reshape(HEADS, block_count, BLOCK, head_dim)
    return shaped.transpose(1, 2, 0, 3).reshape(block_count * BLOCK, HEADS * head_dim)


def key_layout(first_block, local_blocks, all_blocks, random_ids):
    query_ids = first_block + jnp.arange(local_blocks, dtype=jnp.int32)
    window = jnp.stack([query_ids - 1, query_ids, query_ids + 1], axis=1)
    inside = (window >= 1) & (window <= all_blocks - 2)
    window = jnp.clip(window, 0, all_blocks - 1)
    end_blocks = jnp.broadcast_to(jnp.array([0, all_blocks - 1], jnp.int32), (local_blocks, 2))
    fixed_slots = jnp.concatenate([end_blocks, window], axis=1)
    key_slots = jnp.concatenate(
        [jnp.broadcast_to(fixed_slots[None], (HEADS, local_blocks, 5)), random_ids], axis=2
    )
    key_valid = jnp.concatenate(
        [
            jnp.ones((local_blocks, 2), jnp.bool_),
            inside,
            jnp.ones((local_blocks, random_ids.shape[2]), jnp.bool_),
        ],
        axis=1,
    )
    return (key_slots, jnp.repeat(key_valid, BLOCK, axis=1))


def pick_blocks(table, key_slots):
    head_index = jnp.arange(HEADS)[:, None, None]
    picked = table[head_index, key_slots]
    head_dim = table.shape[2] // BLOCK
    return picked.reshape(HEADS, key_slots.shape[1], key_slots.shape[2] * BLOCK, head_dim)


def sparse_scores(query_heads, key_picked, key_valid, score_scale):
    raw_scores = jnp.einsum(
        "hqid,hqkd->hqik", query_heads, key_picked, preferred_element_type=jnp.float32
    )
    return jnp.where(key_valid[None, :, None, :], raw_scores * score_scale, neg_fill)


def dense_scores(query_block, key_flat, score_scale):
    return (
        jnp.einsum("hid,hkd->hik", query_block, key_flat, preferred_element_type=jnp.float32)
        * score_scale
    )


def dense_forward(query_block, key_flat, value_flat, score_scale):
    scores = dense_scores(query_block, key_flat, score_scale)
    top_score = jnp.max(scores, axis=-1, keepdims=True)
    expos = jnp.exp(scores - top_score)
    totals = jnp.sum(expos, axis=-1, keepdims=True)
    attn_prob = (expos / totals).astype(jnp.bfloat16)
    result = jnp.einsum("hik,hkd->ihd", attn_prob, value_flat, preferred_element_type=jnp.float32)
    return (result, (top_score + jnp.log(totals))[..., 0])


def softmax_back(attn_prob, grad_prob, score_scale):
    inner = jnp.sum(attn_prob * grad_prob, axis=-1, keepdims=True)
    return (attn_prob * (grad_prob - inner) * score_scale).astype(jnp.bfloat16)


def dense_backward(query_block, key_flat, value_flat, grad_block, log_total, score_scale):
    attn_prob = jnp.exp(dense_scores(query_block, key_flat, score_scale) - log_total[..., None])
    grad_prob = jnp.einsum(
        "ihd,hkd->hik", grad_block, value_flat, preferred_element_type=jnp.float32
    )
    grad_value = jnp.einsum(
        "hik,ihd->hkd",
        attn_prob.astype(jnp.bfloat16),
        grad_block,
        preferred_element_type=jnp.float32,
    )
    grad_scores = softmax_back(attn_prob, grad_prob, score_scale)
    grad_query = jnp.einsum(
        "hik,hkd->ihd", grad_scores, key_flat, preferred_element_type=jnp.float32
    )
    grad_key = jnp.einsum(
        "hik,hid->hkd", grad_scores, query_block, preferred_element_type=jnp.float32
    )
    return (grad_query, grad_key, grad_value)


def run_forward(weights, in_rows, random_ids):
    (
        w_query,
        w_key,
        w_value,
        w_out,
        w_up,
        w_down,
        ln1_gain,
        ln1_bias,
        query_bias,
        value_bias,
        out_bias,
        ln2_gain,
        ln2_bias,
        up_bias,
        down_bias,
    ) = weights
    normed, pull_first = jax.vjp(
        layer_norm, in_rows, ln1_gain.astype(jnp.float32), ln1_bias.astype(jnp.float32)
    )
    normed_low = normed.astype(jnp.bfloat16)
    queries = (project(normed_low, w_query) + query_bias.astype(jnp.float32)).astype(jnp.bfloat16)
    key_rows = project(normed_low, w_key).astype(jnp.bfloat16)
    value_rows = (project(normed_low, w_value) + value_bias.astype(jnp.float32)).astype(
        jnp.bfloat16
    )
    key_all, value_all = (
        lax.all_gather(key_rows, "seq", axis=0, tiled=True),
        lax.all_gather(value_rows, "seq", axis=0, tiled=True),
    )
    place = lax.axis_index("seq")
    ranks = lax.axis_size("seq")
    local_blocks = in_rows.shape[0] // BLOCK
    all_blocks = key_all.shape[0] // BLOCK
    head_dim = queries.shape[1] // HEADS
    score_scale = head_dim ** (-0.5)
    key_slots, key_valid = key_layout(place * local_blocks, local_blocks, all_blocks, random_ids)
    key_table = to_table(key_all)
    value_table = to_table(value_all)
    key_picked = pick_blocks(key_table, key_slots)
    value_picked = pick_blocks(value_table, key_slots)
    query_heads = to_table(queries).reshape(HEADS, local_blocks, BLOCK, head_dim)
    scores = sparse_scores(query_heads, key_picked, key_valid, score_scale)
    top_score = jnp.max(scores, axis=-1, keepdims=True)
    expos = jnp.exp(scores - top_score)
    totals = jnp.sum(expos, axis=-1, keepdims=True)
    prob_low = (expos / totals).astype(jnp.bfloat16)
    log_sparse = (top_score + jnp.log(totals))[..., 0]
    sparse_out = jnp.einsum(
        "hqik,hqkd->qihd", prob_low, value_picked, preferred_element_type=jnp.float32
    )
    is_edge = (place == 0) | (place == ranks - 1)
    edge_slot = jnp.where(place == 0, 0, local_blocks - 1)
    key_flat = key_table.reshape(HEADS, all_blocks * BLOCK, head_dim)
    value_flat = value_table.reshape(HEADS, all_blocks * BLOCK, head_dim)
    query_edge = lax.dynamic_index_in_dim(query_heads, edge_slot, 1, keepdims=False)
    edge_out, log_edge = lax.cond(
        is_edge,
        lambda: dense_forward(query_edge, key_flat, value_flat, score_scale),
        lambda: (
            jnp.zeros((BLOCK, HEADS, head_dim), jnp.float32),
            jnp.zeros((HEADS, BLOCK), jnp.float32),
        ),
    )
    current = lax.dynamic_index_in_dim(sparse_out, edge_slot, 0, keepdims=False)
    mixed_heads = lax.dynamic_update_index_in_dim(
        sparse_out, jnp.where(is_edge, edge_out, current), edge_slot, 0
    )
    mixed_low = mixed_heads.reshape(in_rows.shape[0], queries.shape[1]).astype(jnp.bfloat16)
    middle = in_rows + (project(mixed_low, w_out) + out_bias.astype(jnp.float32))
    normed_two, pull_second = jax.vjp(
        layer_norm, middle, ln2_gain.astype(jnp.float32), ln2_bias.astype(jnp.float32)
    )
    normed_two_low = normed_two.astype(jnp.bfloat16)
    hidden_pre = project(normed_two_low, w_up) + up_bias.astype(jnp.float32)
    hidden, pull_gelu = jax.vjp(gelu_tanh, hidden_pre)
    hidden_low = hidden.astype(jnp.bfloat16)
    result = middle + (project(hidden_low, w_down) + down_bias.astype(jnp.float32))
    saved = {
        "pull_first": pull_first,
        "pull_second": pull_second,
        "pull_gelu": pull_gelu,
        "normed_low": normed_low,
        "normed_two_low": normed_two_low,
        "hidden_low": hidden_low,
        "mixed_low": mixed_low,
        "query_heads": query_heads,
        "query_edge": query_edge,
        "key_picked": key_picked,
        "value_picked": value_picked,
        "key_flat": key_flat,
        "value_flat": value_flat,
        "key_slots": key_slots,
        "key_valid": key_valid,
        "log_sparse": log_sparse,
        "log_edge": log_edge,
        "is_edge": is_edge,
        "edge_slot": edge_slot,
    }
    return (saved, result)


def run_backward(weights, saved, grad_rows):
    (
        w_query,
        w_key,
        w_value,
        w_out,
        w_up,
        w_down,
        ln1_gain,
        ln1_bias,
        query_bias,
        value_bias,
        out_bias,
        ln2_gain,
        ln2_bias,
        up_bias,
        down_bias,
    ) = weights
    query_heads = saved["query_heads"]
    key_picked = saved["key_picked"]
    value_picked = saved["value_picked"]
    key_slots = saved["key_slots"]
    is_edge = saved["is_edge"]
    edge_slot = saved["edge_slot"]
    local_blocks = query_heads.shape[1]
    head_dim = query_heads.shape[3]
    all_blocks = saved["key_flat"].shape[1] // BLOCK
    score_scale = head_dim ** (-0.5)
    token_count = grad_rows.shape[0]
    grad_ff_low = grad_rows.astype(jnp.bfloat16)
    grad_w_down = weight_grad(saved["hidden_low"], grad_ff_low)
    grad_down_bias = column_sum(grad_ff_low)
    (grad_pre,) = saved["pull_gelu"](project_back(grad_ff_low, w_down))
    grad_pre_low = grad_pre.astype(jnp.bfloat16)
    grad_w_up = weight_grad(saved["normed_two_low"], grad_pre_low)
    grad_up_bias = column_sum(grad_pre_low)
    grad_normed_two = project_back(grad_pre_low, w_up)
    grad_middle, grad_ln2_gain, grad_ln2_bias = saved["pull_second"](grad_normed_two)
    grad_middle = grad_middle + grad_rows
    grad_attn_low = grad_middle.astype(jnp.bfloat16)
    grad_w_out = weight_grad(saved["mixed_low"], grad_attn_low)
    grad_out_bias = column_sum(grad_attn_low)
    grad_mixed = (
        project_back(grad_attn_low, w_out)
        .astype(jnp.bfloat16)
        .reshape(local_blocks, BLOCK, HEADS, head_dim)
    )
    block_ids = jnp.arange(local_blocks, dtype=jnp.int32)
    keep_sparse = jnp.where(is_edge & (block_ids == edge_slot), 0.0, 1.0).astype(jnp.bfloat16)
    grad_sparse = grad_mixed * keep_sparse[:, None, None, None]
    scores = sparse_scores(query_heads, key_picked, saved["key_valid"], score_scale)
    attn_prob = jnp.exp(scores - saved["log_sparse"][..., None])
    grad_prob = jnp.einsum(
        "qihd,hqkd->hqik", grad_sparse, value_picked, preferred_element_type=jnp.float32
    )
    grad_value_picked = jnp.einsum(
        "hqik,qihd->hqkd",
        attn_prob.astype(jnp.bfloat16),
        grad_sparse,
        preferred_element_type=jnp.float32,
    )
    grad_scores = softmax_back(attn_prob, grad_prob, score_scale)
    grad_query_sparse = jnp.einsum(
        "hqik,hqkd->qihd", grad_scores, key_picked, preferred_element_type=jnp.float32
    )
    grad_key_picked = jnp.einsum(
        "hqik,hqid->hqkd", grad_scores, query_heads, preferred_element_type=jnp.float32
    )
    head_index = jnp.arange(HEADS)[:, None, None]
    slot_count = key_slots.shape[2]
    table_shape = (HEADS, all_blocks, BLOCK * head_dim)
    grad_key_table = (
        jnp.zeros(table_shape, jnp.float32)
        .at[head_index, key_slots]
        .add(grad_key_picked.reshape(HEADS, local_blocks, slot_count, BLOCK * head_dim))
    )
    grad_value_table = (
        jnp.zeros(table_shape, jnp.float32)
        .at[head_index, key_slots]
        .add(grad_value_picked.reshape(HEADS, local_blocks, slot_count, BLOCK * head_dim))
    )
    grad_edge_block = lax.dynamic_index_in_dim(grad_mixed, edge_slot, 0, keepdims=False)
    flat_shape = (HEADS, all_blocks * BLOCK, head_dim)
    grad_query_edge, grad_key_edge, grad_value_edge = lax.cond(
        is_edge,
        lambda: dense_backward(
            saved["query_edge"],
            saved["key_flat"],
            saved["value_flat"],
            grad_edge_block,
            saved["log_edge"],
            score_scale,
        ),
        lambda: (
            jnp.zeros((BLOCK, HEADS, head_dim), jnp.float32),
            jnp.zeros(flat_shape, jnp.float32),
            jnp.zeros(flat_shape, jnp.float32),
        ),
    )
    grad_key_table = grad_key_table + grad_key_edge.reshape(table_shape)
    grad_value_table = grad_value_table + grad_value_edge.reshape(table_shape)
    grad_key_own, grad_value_own = (
        lax.psum_scatter(
            from_table(grad_key_table).astype(jnp.bfloat16), "seq", scatter_dimension=0, tiled=True
        ).astype(jnp.float32),
        lax.psum_scatter(
            from_table(grad_value_table).astype(jnp.bfloat16),
            "seq",
            scatter_dimension=0,
            tiled=True,
        ).astype(jnp.float32),
    )
    current = lax.dynamic_index_in_dim(grad_query_sparse, edge_slot, 0, keepdims=False)
    grad_query_all = lax.dynamic_update_index_in_dim(
        grad_query_sparse, current + grad_query_edge, edge_slot, 0
    )
    grad_query_low = grad_query_all.reshape(token_count, HEADS * head_dim).astype(jnp.bfloat16)
    grad_key_low = grad_key_own.astype(jnp.bfloat16)
    grad_value_low = grad_value_own.astype(jnp.bfloat16)
    normed_low = saved["normed_low"]
    grad_w_query = weight_grad(normed_low, grad_query_low)
    grad_w_key = weight_grad(normed_low, grad_key_low)
    grad_w_value = weight_grad(normed_low, grad_value_low)
    grad_query_bias = column_sum(grad_query_low)
    grad_value_bias = column_sum(grad_value_low)
    grad_normed = (
        project_back(grad_query_low, w_query)
        + project_back(grad_key_low, w_key)
        + project_back(grad_value_low, w_value)
    )
    grad_inputs, grad_ln1_gain, grad_ln1_bias = saved["pull_first"](grad_normed)
    grad_inputs = grad_inputs + grad_middle
    grads = (
        grad_w_query,
        grad_w_key,
        grad_w_value,
        grad_w_out,
        grad_w_up,
        grad_w_down,
        grad_ln1_gain,
        grad_ln1_bias,
        grad_query_bias,
        grad_value_bias,
        grad_out_bias,
        grad_ln2_gain,
        grad_ln2_bias,
        grad_up_bias,
        grad_down_bias,
    )
    return (grad_inputs, grads)


def on_device(inputs, grad_out, random_blocks, *shards):
    weights = tuple(lax.all_gather(part, BOTH, axis=0, tiled=True) for part in shards)

    def micro_step(totals, sequence):
        in_rows, grad_rows, random_ids = sequence
        saved, result = run_forward(weights, in_rows, random_ids)
        grad_in, grads = run_backward(weights, saved, grad_rows)
        return (tuple(left + right for left, right in zip(totals, grads)), (result, grad_in))

    initial = tuple(jnp.zeros(weight.shape, jnp.float32) for weight in weights)
    totals, (results, grads_in) = lax.scan(micro_step, initial, (inputs, grad_out, random_blocks))
    summed = tuple(
        lax.psum_scatter(total, BOTH, scatter_dimension=0, tiled=True) for total in totals
    )
    return (results, grads_in) + summed


F32, BF16 = jnp.float32, jnp.bfloat16
PAIR = 128
TIMES = dict(
    cast_far=1,
    join_first=2,
    join_beside=1,
    join_up=2,
    join_plane=2,
    small_vectors=2,
    norm_project=0.3,
    attn_forward=0.5,
    out_norm=0.3,
    join_low=0.3,
    feed_forward=9,
    split_add=0.1,
    merge_add=0.3,
    beside_add=0.3,
    middle_back=12,
    grad_wide=1.8,
    attn_backward=5,
    split_depth=0.3,
    input_back=0.25,
    pack_vectors=0.3,
    fill_far=0.05,
    last_add=0.05,
)
COST = 0.3 * 1e9
NEAR = tuple((dx, dc, dy) for dx in range(2) for dc in range(2) for dy in range(2))


def contract(left, right, left_dim, right_dim):
    return lax.dot_general(
        left, right, (((left_dim,), (right_dim,)), ((), ())), preferred_element_type=F32
    )


def held(*shape):
    zeros = (0,) * len(shape)
    return pl.BlockSpec(shape, lambda *_: zeros, pipeline_mode=pl.Buffered(1))


def whole_ref():
    return pl.BlockSpec(memory_space=pltpu.HBM)


def call(body, name, grid, in_specs, out_specs, out_shape, args, scratch=(), vmem=24, alias=None):
    spec = pltpu.PrefetchScalarGridSpec(
        num_scalar_prefetch=1,
        grid=grid,
        in_specs=in_specs,
        out_specs=out_specs,
        scratch_shapes=scratch,
    )
    return pl.pallas_call(
        body,
        grid_spec=spec,
        out_shape=out_shape,
        name=name,
        input_output_aliases=alias or {},
        compiler_params=pltpu.CompilerParams(vmem_limit_bytes=vmem << 20),
        cost_estimate=pl.CostEstimate(
            flops=int(TIMES[name] * grid[0] * COST), bytes_accessed=1, transcendentals=1
        ),
    )(*args)


def shape_of(kind, *shape):
    return jax.ShapeDtypeStruct(shape, kind)


def norm_parts(values):
    mean = jnp.mean(values, axis=-1, keepdims=True)
    centre = values - mean
    spread = jnp.mean(centre * centre, axis=-1, keepdims=True)
    scale = lax.rsqrt(spread + eps_norm)
    return centre * scale, scale


def norm_back(unit, scale, gain, grad):
    inner = grad * gain
    first = jnp.mean(inner, axis=-1, keepdims=True)
    second = jnp.mean(inner * unit, axis=-1, keepdims=True)
    return scale * (inner - first - unit * second)


def column(values):
    return jnp.sum(values, axis=0, keepdims=True)


def gelu_both(values):
    root = 2 * 0.7978845608028654
    cubic = root * 0.044715
    turn = -1.4426950408889634
    square = values * values
    power = jnp.exp2(jnp.minimum(values * (turn * root + (turn * cubic) * square), 126.0))
    part = pl.reciprocal(1.0 + power, approx=True)
    hidden = values * part
    return hidden, part + (hidden - hidden * part) * (root + (3 * cubic) * square)


def flip(value, bit):
    return 1 - value if bit else value


def parts_copies(place_ref, part_refs, weight, sems, start, size, into, chunk):
    copies = []
    for at, (dx, dc, dy) in enumerate(NEAR):
        spot = (slice(None), flip(place_ref[1], dx), flip(place_ref[2], dc), flip(place_ref[3], dy))
        copies.append(
            pltpu.make_async_copy(
                part_refs[at].at[:, :, pl.ds(start, size)],
                weight.at[spot + (slice(None), pl.ds(into, size))],
                sems.at[chunk, at],
            )
        )
    return copies


def weight_scratch(part, columns):
    depth, rows, _ = part.shape
    return pltpu.VMEM((depth, 2, 2, 2, rows, columns), BF16)


def flat(value):
    return value.reshape(-1, value.shape[-1])


def depth_copies(place_ref, part_refs, weight, sems):
    depth = weight.shape[0]
    copies = []
    for step in range(depth):
        there = lax.rem(place_ref[0] + depth - step, depth)
        for dc in range(2):
            core = flip(place_ref[2], dc)
            copies.append(
                pltpu.make_async_copy(
                    part_refs[2 * step + dc], weight.at[there, :, core], sems.at[there, dc]
                )
            )
    return copies


def depth_wait(place_ref, part_refs, weight, sems, at):
    for dc in range(2):
        core = flip(place_ref[2], dc)
        pltpu.make_async_copy(part_refs[dc], weight.at[at, :, core], sems.at[at, dc]).wait()


def own_spec(step, width, parts):
    return pl.BlockSpec((1, step, width), lambda i, p: (p[3], jnp.minimum(i, parts - 1), 0))


def far_spec(step, width, parts):
    return pl.BlockSpec((step, width), lambda i, _: (jnp.maximum(i - parts, 0), 0))


def join(place, blocks, moves, shapes, name):
    def body(place_ref, *refs):
        ins, outs = refs[: len(blocks)], refs[len(blocks) :]
        for i, cut, j, spot in moves:
            outs[j][spot(place_ref)] = ins[i][cut]

    return call(
        body,
        name,
        (1,),
        [held(*block.shape) for block in blocks],
        [held(*shape) for shape in shapes],
        [shape_of(BF16, *shape) for shape in shapes],
        (place,) + tuple(blocks),
        vmem=10,
    )


def join_beside(place, blocks):
    rows = blocks[0].shape[0]
    widths = [block.shape[1] for block in blocks]

    def body(place_ref, *refs):
        start = 0
        for ref, width in zip(refs, widths):
            refs[-1][:, start : start + width] = ref[...]
            start += width

    return call(
        body,
        "join_beside",
        (1,),
        [held(*block.shape) for block in blocks],
        held(rows, sum(widths)),
        shape_of(BF16, rows, sum(widths)),
        (place,) + tuple(blocks),
        vmem=4,
    )


def join_low(place, grad_out, far):
    half, width = far.shape

    def body(place_ref, own_ref, far_ref, low_ref, sum_ref):
        low = own_ref[0].astype(BF16)
        low_ref[:half] = low
        low_ref[half:] = far_ref[...]
        sum_ref[...] = column(low.astype(F32)) + column(far_ref[...].astype(F32))

    return call(
        body,
        "join_low",
        (1,),
        [
            pl.BlockSpec((1, half, width), lambda i, p: (p[3], 0, 0), pipeline_mode=pl.Buffered(1)),
            held(half, width),
        ],
        [held(2 * half, width), held(1, width)],
        [shape_of(BF16, 2 * half, width), shape_of(F32, 1, width)],
        (place, grad_out, far),
        vmem=12,
    )


def cast_far(place, values):
    _, half, width = values.shape
    step = half // 2

    def body(place_ref, values_ref, out_ref):
        out_ref[...] = values_ref[0].astype(BF16)

    return call(
        body,
        "cast_far",
        (half // step,),
        [pl.BlockSpec((1, step, width), lambda i, p: (1 - p[3], i, 0))],
        pl.BlockSpec((step, width), lambda i, _: (i, 0)),
        shape_of(BF16, half, width),
        (place, values),
        vmem=6,
    )


def norm_project(place, inputs, far, gain, shift, left, right, bias):
    half, width = far.shape
    columns = bias.shape[1]
    step = 512
    left_steps = left[0].shape[-1] // step
    steps = columns // step
    sub = 256

    def body(place_ref, own_ref, far_ref, gain_ref, shift_ref, bias_ref, *refs):
        left_refs, right_refs = refs[:8], refs[8:16]
        normed_ref, out_ref, weight, sems = refs[16:]
        at = pl.program_id(0)

        def copies(chunk):
            refs, start = (left_refs, chunk) if chunk < left_steps else (right_refs, chunk - left_steps)
            return parts_copies(place_ref, refs, weight, sems, start * step, step, chunk * step, chunk)

        @pl.when(at == 0)
        def _():
            for chunk in range(steps):
                for copy in copies(chunk):
                    copy.start()
            for start, rows in ((0, own_ref[0]), (half, far_ref[...])):
                unit, _ = norm_parts(rows.astype(F32))
                normed_ref[start : start + half, :] = (
                    unit * gain_ref[...] + shift_ref[...]
                ).astype(BF16)

        for chunk in range(steps):
            @pl.when(at == chunk)
            def _():
                for copy in copies(chunk):
                    copy.wait()

        cut = pl.ds(pl.multiple_of(at * step, step), step)
        part = flat(weight[:, :, :, :, :, cut])
        for start in range(0, 2 * half, sub):
            result = contract(normed_ref[start : start + sub], part, 1, 0) + bias_ref[...]
            out_ref[start : start + sub] = result.astype(BF16)

    return call(
        body,
        "norm_project",
        (steps,),
        [
            pl.BlockSpec((1, half, width), lambda i, p: (p[3], 0, 0), pipeline_mode=pl.Buffered(1)),
            held(half, width),
            held(1, width),
            held(1, width),
            pl.BlockSpec((1, step), lambda i, _: (0, i)),
        ]
        + [whole_ref()] * 16,
        [
            pl.BlockSpec((2 * half, width), lambda i, _: (0, 0)),
            pl.BlockSpec((2 * half, step), lambda i, _: (0, i)),
        ],
        [shape_of(BF16, 2 * half, width), shape_of(BF16, 2 * half, columns)],
        (place, inputs, far, gain, shift, bias) + tuple(left) + tuple(right),
        scratch=[weight_scratch(left[0], columns), pltpu.SemaphoreType.DMA((steps, 8))],
        vmem=56,
    )


def out_norm(place, mixed, up_parts, at_out, bias, inputs, far, gain, shift, down_bias):
    half, width = far.shape
    step = 256
    parts = half // step

    def body(place_ref, mixed_ref, bias_ref, own_ref, far_ref, gain_ref, shift_ref, down_ref, *refs):
        right_refs = refs[:8]
        middle_ref, normed_ref, start_ref, weight, sems = refs[8:]

        @pl.when(pl.program_id(0) == 0)
        def _():
            copies = parts_copies(place_ref, right_refs, weight, sems, at_out, width, 0, 0)
            for copy in copies:
                copy.start()
            for copy in copies:
                copy.wait()

        near = pl.program_id(0) < parts
        rows = jnp.where(near, own_ref[0], far_ref[...].astype(F32))
        middle = rows + (contract(mixed_ref[...], flat(weight[...]), 1, 0) + bias_ref[...])
        middle_ref[...] = middle
        start_ref[...] = middle + down_ref[...]
        unit, _ = norm_parts(middle)
        normed_ref[...] = (unit * gain_ref[...] + shift_ref[...]).astype(BF16)

    here = pl.BlockSpec((step, width), lambda i, _: (i, 0))
    return call(
        body,
        "out_norm",
        (2 * parts,),
        [
            here,
            held(1, width),
            own_spec(step, width, parts),
            far_spec(step, width, parts),
            held(1, width),
            held(1, width),
            held(1, width),
        ]
        + [whole_ref()] * 8,
        [here, here, here],
        [shape_of(F32, 2 * half, width), shape_of(BF16, 2 * half, width), shape_of(F32, 2 * half, width)],
        (place, mixed, bias, inputs, far, gain, shift, down_bias) + tuple(up_parts),
        scratch=[weight_scratch(up_parts[0], width), pltpu.SemaphoreType.DMA((1, 8))],
        vmem=56,
    )


def fill_far(place, partial, base, delta):
    _, half, width = base.shape
    step = 256

    def body(place_ref, partial_ref, base_ref, delta_ref, out_ref):
        out_ref[0] = base_ref[0] + delta_ref[...].astype(F32)

    there = pl.BlockSpec((1, step, width), lambda i, p: (1 - p[3], i, 0))
    return call(
        body,
        "fill_far",
        (half // step,),
        [whole_ref(), there, pl.BlockSpec((step, width), lambda i, _: (i, 0))],
        there,
        shape_of(F32, 2, half, width),
        (place, partial, base, delta),
        alias={1: 0},
        vmem=8,
    )


def grad_wide(place, left, rights, rows, span, pieces=1):
    tokens, tall = left.shape
    width = rights[0].shape[1]
    step = 512
    each = width // step
    first, stop = span
    steps = stop - first
    per = steps // pieces
    group = 4 * rows
    used = sorted({at // each for at in range(first, stop)})

    def body(place_ref, left_ref, *refs):
        right_refs = refs[: len(used)]
        outs, sums = refs[len(used) : -1], refs[-1]
        at = pl.program_id(0)
        for which, right_ref in zip(used, right_refs):
            @pl.when((at + first) // each == which)
            def _():
                result = contract(left_ref[...], right_ref[...], 0, 0).astype(BF16)
                sums[...] = result.reshape(tall // group, 2, group // 2, step)

        for piece in range(pieces):
            @pl.when(at // per == piece)
            def _():
                outs[2 * piece][...] = sums[:, place_ref[2]]
                outs[2 * piece + 1][...] = sums[:, 1 - place_ref[2]]

    def right_at(which):
        low, high = max(first - which * each, 0), min(stop - which * each, each) - 1
        return lambda i, _: (0, jnp.clip(i + first - which * each, low, high))

    def out_at(piece):
        return lambda i, _: (0, 0, jnp.clip(i - piece * per, 0, per - 1))

    return call(
        body,
        "grad_wide",
        (steps,),
        [held(tokens, tall)] + [pl.BlockSpec((tokens, step), right_at(which)) for which in used],
        [
            pl.BlockSpec((tall // group, group // 2, step), out_at(piece))
            for piece in range(pieces)
            for _ in range(2)
        ],
        [shape_of(BF16, tall // group, group // 2, per * step)] * (2 * pieces),
        (place, left) + tuple(rights[which] for which in used),
        scratch=[pltpu.VMEM((tall // group, 2, group // 2, step), BF16)],
        vmem=20,
    )


def feed_forward(place, first, count, depth, normed, grad_low, up_parts, down_parts, up_bias, far, state, wide):
    tokens, width = normed.shape
    half = tokens // 2
    hidden_width = up_bias.shape[1]
    step = hidden_width // (2 * depth)
    steps = 2 * count
    rows = down_parts[0].shape[-2]
    group = width // (2 * depth)
    last = first + count == depth
    columns, offset, before = wide
    offset = offset // step
    lines = up_parts[0].shape[1]
    beside = (up_parts[0].shape[-1] - hidden_width) // width
    rows = rows + beside * lines

    def body(place_ref, bias_ref, normed_in, grad_in, far_in, out_in, back_in, *refs):
        up_refs, down_refs = refs[:8], refs[8 : 8 + 2 * depth]
        refs = refs[8 + 2 * depth + len(before) :]
        tall_mine, tall_other, wide_mine, wide_other, sum_ref, back_out = refs[:6]
        outs = refs[6:8] if last else refs[6:7]
        refs = refs[6 + len(outs) :]
        normed_ref, grad_ref, far_ref, total, back, delta = refs[:6]
        up, down, up_sems, down_sems, beside_sems, state_sems, tall_sums, wide_sums = refs[6:]
        at = pl.program_id(0)
        slot = lax.rem(at, 2)

        def up_copies(index, into):
            start = pl.multiple_of((2 * first + index) * step, step)
            copies = []
            for which, (dx, dc, dy) in enumerate(NEAR):
                x, c, y = flip(place_ref[1], dx), flip(place_ref[2], dc), flip(place_ref[3], dy)
                copies.append(
                    pltpu.make_async_copy(
                        up_refs[which].at[:, :, pl.ds(start, step)],
                        up.at[into, :, x, c, y],
                        up_sems.at[into, which],
                    )
                )
            return copies

        def down_copies(index, into, turn):
            x = lax.rem(index, 2)
            return [
                pltpu.make_async_copy(
                    down_refs[2 * turn + dc].at[x],
                    down.at[into, flip(place_ref[2], dc), :, pl.ds(0, rows - beside * lines)],
                    down_sems.at[into, dc],
                )
                for dc in range(2)
            ]

        def beside_copies(index, into, dx):
            copies = []
            for dc in range(2):
                for dy in range(2):
                    which = NEAR.index((dx, dc, dy))
                    c, y = flip(place_ref[2], dc), flip(place_ref[3], dy)
                    for part in range(beside):
                        copies.append(
                            pltpu.make_async_copy(
                                up_refs[which].at[
                                    first + index // 2, :, pl.ds(hidden_width + part * width, width)
                                ],
                                down.at[into, c, y, pl.ds(rows - (beside - part) * lines, lines)],
                                beside_sems.at[into, len(copies)],
                            )
                        )
            return copies

        def begin(index, into):
            for copy in up_copies(index, into):
                copy.start()
            away = lax.rem(place_ref[0] + depth - first - index // 2, depth)
            for turn in range(depth):
                @pl.when(away == turn)
                def _():
                    for copy in down_copies(index, into, turn):
                        copy.start()
            for dx in range(2):
                @pl.when(flip(place_ref[1], dx) == lax.rem(index, 2))
                def _():
                    for copy in beside_copies(index, into, dx):
                        copy.start()

        normed_copy = pltpu.make_async_copy(normed_in, normed_ref, state_sems.at[0])
        grad_copy = pltpu.make_async_copy(grad_in, grad_ref, state_sems.at[1])
        out_copy = pltpu.make_async_copy(out_in, total, state_sems.at[2])
        if first:
            back_copy = pltpu.make_async_copy(back_in, back, state_sems.at[3])
        back_away = pltpu.make_async_copy(back, back_out, state_sems.at[5])
        if last:
            far_copy = pltpu.make_async_copy(far_in, far_ref, state_sems.at[4])
            away = [
                pltpu.make_async_copy(
                    total.at[pl.ds(0, half)], outs[0].at[place_ref[3]], state_sems.at[6]
                ),
                pltpu.make_async_copy(delta, outs[1], state_sems.at[7]),
            ]
        else:
            away = [pltpu.make_async_copy(total, outs[0], state_sems.at[6])]

        @pl.when(at == 0)
        def _():
            normed_copy.start()
            begin(0, 0)
            grad_copy.start()
            out_copy.start()
            if first:
                back_copy.start()
            else:
                back[...] = jnp.zeros((tokens, width), F32)
            if last:
                far_copy.start()
            normed_copy.wait()

        @pl.when(at + 1 < steps)
        def _():
            begin(at + 1, 1 - slot)

        for copy in up_copies(at, slot):
            copy.wait()
        up_part = flat(up[slot])
        before_gelu = contract(normed_ref[...], up_part, 1, 0) + bias_ref[...]
        hidden, slope = gelu_both(before_gelu)
        hidden = hidden.astype(BF16)

        @pl.when(at == 0)
        def _():
            grad_copy.wait()

        tall = contract(hidden, grad_ref[...], 0, 0).astype(BF16)
        tall_sums[...] = tall.reshape(tall_sums.shape)
        tall_mine[0] = tall_sums[place_ref[2]]
        tall_other[0] = tall_sums[1 - place_ref[2]]

        for copy in down_copies(at, slot, 0) + beside_copies(at, slot, 0):
            copy.wait()

        @pl.when(at == 0)
        def _():
            out_copy.wait()
            if first:
                back_copy.wait()
            if last:
                far_copy.wait()

        down_part = flat(down[slot])
        total[...] += contract(hidden, down_part, 1, 0)

        @pl.when(at == steps - 1)
        def _():
            if last:
                delta[...] = (total[half:] - far_ref[...].astype(F32)).astype(BF16)
            for copy in away:
                copy.start()

        low = (contract(grad_ref[...], down_part, 1, 1) * slope).astype(BF16)
        back[...] += contract(low, up_part, 1, 1)

        @pl.when(at == steps - 1)
        def _():
            back_away.start()

        sum_ref[...] = column(low.astype(F32))
        broad = contract(normed_ref[...], low, 0, 0).astype(BF16)
        wide_sums[...] = broad.reshape(wide_sums.shape)
        wide_mine[...] = wide_sums[:, place_ref[2]]
        wide_other[...] = wide_sums[:, 1 - place_ref[2]]

        @pl.when(at == steps - 1)
        def _():
            for copy in away + [back_away]:
                copy.wait()

    tall_spec = pl.BlockSpec((1, 2 * rows, width), lambda i, _: (i, 0, 0))
    broad_spec = pl.BlockSpec((2 * depth, group // 2, step), lambda i, _: (0, 0, offset + i))
    sum_spec = pl.BlockSpec((1, step), lambda i, _: (0, i))
    out_specs = [tall_spec, tall_spec, broad_spec, broad_spec, sum_spec, whole_ref()]
    out_shape = [shape_of(BF16, steps, 2 * rows, width)] * 2
    out_shape += [shape_of(BF16, 2 * depth, group // 2, columns)] * 2
    out_shape += [shape_of(F32, 1, steps * step), shape_of(F32, tokens, width)]
    if last:
        out_specs += [whole_ref()] * 2
        out_shape += [shape_of(F32, 2, half, width), shape_of(BF16, half, width)]
    else:
        out_specs += [whole_ref()]
        out_shape += [shape_of(F32, tokens, width)]
    scratch = [
        pltpu.VMEM((tokens, width), BF16),
        pltpu.VMEM((tokens, width), BF16),
        pltpu.VMEM((half, width), BF16),
        pltpu.VMEM((tokens, width), F32),
        pltpu.VMEM((tokens, width), F32),
        pltpu.VMEM((half, width), BF16),
        pltpu.VMEM((2, depth, 2, 2, 2, group // 4, step), BF16),
        pltpu.VMEM((2, 2, 2, rows, width), BF16),
        pltpu.SemaphoreType.DMA((2, 8)),
        pltpu.SemaphoreType.DMA((2, 2)),
        pltpu.SemaphoreType.DMA((2, 4 * beside)),
        pltpu.SemaphoreType.DMA((8,)),
        pltpu.VMEM((2, 2 * rows, width), BF16),
        pltpu.VMEM((2 * depth, 2, group // 2, step), BF16),
    ]
    args = (place, up_bias, normed, grad_low, far) + tuple(state) + tuple(up_parts) + tuple(down_parts)
    alias = {len(args) + i: 2 + i for i in range(len(before))}
    return call(
        body,
        "feed_forward",
        (steps,),
        [pl.BlockSpec((1, step), lambda i, _: (0, 2 * first + i))]
        + [whole_ref()] * (5 + 8 + 2 * depth + len(before)),
        out_specs,
        out_shape,
        args + tuple(before),
        scratch=scratch,
        vmem=56,
        alias=alias,
    )


def middle_back(place, grad_normed, middle, gain, grad_out, far, up_parts, at_out):
    half, width = far.shape
    step = 256
    parts = half // step

    def body(place_ref, grad_ref, middle_ref, gain_ref, own_ref, far_ref, *refs):
        right_refs = refs[:8]
        total_ref, low_ref, mixed_ref = refs[8:11]
        sums = refs[11:14]
        weight, sems = refs[14:]
        at = pl.program_id(0)

        def copies():
            return parts_copies(place_ref, right_refs, weight, sems, at_out, width, 0, 0)

        @pl.when(at == 0)
        def _():
            for copy in copies():
                copy.start()
            for ref in sums:
                ref[...] = jnp.zeros_like(ref)

        grad_normed = grad_ref[...]
        unit, scale = norm_parts(middle_ref[...])
        out_grad = jnp.where(at < parts, own_ref[0], far_ref[...].astype(F32))
        total = out_grad + norm_back(unit, scale, gain_ref[...], grad_normed)
        total_ref[...] = total
        low = total.astype(BF16)
        low_ref[...] = low
        sums[0][...] += column(grad_normed * unit)
        sums[1][...] += column(grad_normed)
        sums[2][...] += column(low.astype(F32))

        @pl.when(at == 0)
        def _():
            for copy in copies():
                copy.wait()

        mixed_ref[...] = contract(low, flat(weight[...]), 1, 1).astype(BF16)

    here = pl.BlockSpec((step, width), lambda i, _: (i, 0))
    vector = pl.BlockSpec((1, width), lambda i, _: (0, 0))
    tokens = 2 * half
    return call(
        body,
        "middle_back",
        (2 * parts,),
        [here, here, held(1, width), own_spec(step, width, parts), far_spec(step, width, parts)]
        + [whole_ref()] * 8,
        [here, here, here, vector, vector, vector],
        [shape_of(F32, tokens, width), shape_of(BF16, tokens, width), shape_of(BF16, tokens, width)]
        + [shape_of(F32, 1, width)] * 3,
        (place, grad_normed, middle, gain, grad_out, far) + tuple(up_parts),
        scratch=[weight_scratch(up_parts[0], width), pltpu.SemaphoreType.DMA((1, 8))],
        vmem=56,
    )


def input_back(place, grads, left, right, inputs, far, gain, middle_grad, far_grad):
    half, width = far.shape
    cut = left[0].shape[-1]
    step = 256
    parts = half // step

    def body(
        place_ref, query_ref, key_ref, value_ref, own_ref, far_ref, gain_ref, middle_ref, far_grad_ref, *refs
    ):
        left_refs, right_refs = refs[:8], refs[8:16]
        out_ref, delta_ref = refs[16:18]
        sums = refs[18:22]
        gain_sum_ref, shift_sum_ref, query_sum_ref, value_sum_ref = sums
        weight, sems = refs[22:]
        at = pl.program_id(0)

        def copies():
            result = []
            for chunk, part_refs in enumerate((left_refs, right_refs)):
                size = (cut, 3 * width - cut)[chunk]
                result += parts_copies(
                    place_ref, part_refs, weight, sems, 0, size, chunk * cut, chunk
                )
            return result

        @pl.when(at == 0)
        def _():
            for copy in copies():
                copy.start()
            for ref in sums:
                ref[...] = jnp.zeros_like(ref)

        @pl.when(at == 0)
        def _():
            for copy in copies():
                copy.wait()

        def part(chunk):
            return flat(weight[:, :, :, :, :, chunk * width : (chunk + 1) * width])

        grad_normed = contract(query_ref[...], part(0), 1, 1)
        grad_normed += contract(key_ref[...], part(1), 1, 1)
        grad_normed += contract(value_ref[...], part(2), 1, 1)
        rows = jnp.where(at < parts, own_ref[0], far_ref[...].astype(F32))
        unit, scale = norm_parts(rows)
        gain_sum_ref[...] += column(grad_normed * unit)
        shift_sum_ref[...] += column(grad_normed)
        query_sum_ref[...] += column(query_ref[...].astype(F32))
        value_sum_ref[...] += column(value_ref[...].astype(F32))
        result = middle_ref[...] + norm_back(unit, scale, gain_ref[...], grad_normed)

        @pl.when(at < parts)
        def _():
            out_ref[0] = result

        @pl.when(at >= parts)
        def _():
            delta_ref[...] = (result - far_grad_ref[...].astype(F32)).astype(BF16)

    here = pl.BlockSpec((step, width), lambda i, _: (i, 0))
    vector = pl.BlockSpec((1, width), lambda i, _: (0, 0))
    return call(
        body,
        "input_back",
        (2 * parts,),
        [
            here,
            here,
            here,
            own_spec(step, width, parts),
            far_spec(step, width, parts),
            held(1, width),
            here,
            far_spec(step, width, parts),
        ]
        + [whole_ref()] * 16,
        [own_spec(step, width, parts), far_spec(step, width, parts), vector, vector, vector, vector],
        [shape_of(F32, 2, half, width), shape_of(BF16, half, width)] + [shape_of(F32, 1, width)] * 4,
        (place,) + tuple(grads) + (inputs, far, gain, middle_grad, far_grad) + tuple(left) + tuple(right),
        scratch=[weight_scratch(left[0], 3 * width), pltpu.SemaphoreType.DMA((2, 8))],
        vmem=56,
    )


def split_add(place, mine, came, spot):
    groups, _, rows, columns = mine.shape

    def body(place_ref, mine_ref, came_ref, sent_ref, kept_ref):
        for ref, at in ((sent_ref, 1 - place_ref[spot]), (kept_ref, place_ref[spot])):
            ref[0] = (mine_ref[0, at].astype(F32) + came_ref[0, at].astype(F32)).astype(BF16)

    block = pl.BlockSpec((1, 2, rows, columns), lambda i, _: (i, 0, 0, 0))
    out = pl.BlockSpec((1, rows, columns), lambda i, _: (i, 0, 0))
    return call(
        body,
        "split_add",
        (groups,),
        [block, block],
        [out, out],
        [shape_of(BF16, groups, rows, columns)] * 2,
        (place, mine, came),
        vmem=8,
    )


def split_depth(place, pairs, rows, vectors=None, sizes=()):
    depth = pairs[0][0].shape[0]
    layout = [(which, part) for which, (mine, _) in enumerate(pairs) for part in range(mine.shape[1] // rows)]
    total = sum(pairs[which][0].shape[2] for which, _ in layout)
    extra = () if vectors is None else (vectors,)
    wide = total + PAIR * len(extra)
    count = depth * 8

    def body(place_ref, *refs):
        outs = refs[2 * len(pairs) + len(extra) :]
        for step, ref in enumerate(outs):
            at = lax.rem(place_ref[0] + step, depth)
            start = 0
            for which, part in layout:
                width = pairs[which][0].shape[2]
                cut = pl.ds(part * rows, rows)
                value = refs[2 * which][at, cut].astype(F32) + refs[2 * which + 1][at, cut].astype(F32)
                ref[:, start : start + width] = value.astype(ref.dtype)
                start += width
            if extra:
                device = ((at * 2 + place_ref[1]) * 2 + place_ref[2]) * 2 + place_ref[3]
                line = lax.broadcasted_iota(jnp.int32, (rows, PAIR), 0)
                block = jnp.zeros((rows, PAIR), F32)
                base = 0
                for index, size in enumerate(sizes):
                    values = refs[2 * len(pairs)][pl.ds(base + device * size * rows // PAIR, 1), :]
                    block = jnp.where(line == index, values, block)
                    base += count * size * rows // PAIR
                ref[:, total:] = block.astype(ref.dtype)

    return call(
        body,
        "split_depth",
        (1,),
        [held(*mine.shape) for mine, _ in pairs for _ in range(2)] + [held(*value.shape) for value in extra],
        [held(rows, wide)] * depth,
        [shape_of(F32, rows, wide)] + [shape_of(BF16, rows, wide)] * (depth - 1),
        (place,) + tuple(value for pair in pairs for value in pair) + extra,
        vmem=12,
    )


def last_add(place, own, came, shapes):
    rows, total = own.shape
    layout = [(which, part) for which, shape in enumerate(shapes) for part in range(shape[0] // rows)]

    def body(place_ref, own_ref, *refs):
        outs = refs[len(came) :]
        start = 0
        for which, part in layout:
            width = shapes[which][1]
            value = own_ref[:, start : start + width]
            for ref in refs[: len(came)]:
                value = value + ref[:, start : start + width].astype(F32)
            outs[which][part * rows : (part + 1) * rows] = value
            start += width

    return call(
        body,
        "last_add",
        (1,),
        [held(rows, total)] * (1 + len(came)),
        [held(*shape) for shape in shapes],
        [shape_of(F32, *shape) for shape in shapes],
        (place, own) + tuple(came),
        vmem=12,
    )


def spread_rows(count, per, size, row):
    span = size * per
    lane = lax.broadcasted_iota(jnp.int32, (per, count * span), 1)
    line = lax.broadcasted_iota(jnp.int32, (per, count * span), 0)
    return jnp.where(lane % span == row * per + line, 1.0, 0.0)


def chosen_rows(count, span):
    lane = lax.broadcasted_iota(jnp.int32, (count, count * span), 1)
    line = lax.broadcasted_iota(jnp.int32, (count, count * span), 0)
    return lane // span == line


def small_vectors(place, right, start, sizes, per):
    depth, rows, _ = right[0].shape
    count = depth * 8

    def body(place_ref, *refs):
        part_refs, outs, held_rows = refs[:8], refs[8:-1], refs[-1]
        for at, (dx, dc, dy) in enumerate(NEAR):
            x, c, y = flip(place_ref[1], dx), flip(place_ref[2], dc), flip(place_ref[3], dy)
            held_rows[:, x, c, y] = part_refs[at][...].astype(F32)
        table = held_rows[...].reshape(count, rows, PAIR)
        at = 0
        for ref, size in zip(outs, sizes):
            chosen = chosen_rows(count, size * per)
            line = jnp.zeros((1, count * size * per), F32)
            for row in range(size):
                spread = spread_rows(count, per, size, row).astype(BF16)
                wide = contract(table[:, at + row, :per].astype(BF16), spread, 1, 0)
                line += column(jnp.where(chosen, wide, 0.0))
            at += size
            ref[...] = line

    return call(
        body,
        "small_vectors",
        (1,),
        [pl.BlockSpec((depth, rows, PAIR), lambda i, _: (0, 0, start // PAIR))] * 8,
        [held(1, count * size * per) for size in sizes],
        [shape_of(F32, 1, count * size * per) for size in sizes],
        (place,) + tuple(right),
        scratch=[pltpu.VMEM((depth, 2, 2, 2, rows, PAIR), F32)],
        vmem=12,
    )


def merge_add(place, mine, came, spot):
    counts = [part.shape[0] for part in mine]
    _, _, rows, columns = mine[0].shape

    def body(place_ref, *refs):
        sent_ref, kept_ref = refs[2 * len(mine) :]
        start = 0
        for which, count in enumerate(counts):
            for ref, at in ((sent_ref, 1 - place_ref[spot]), (kept_ref, place_ref[spot])):
                total = refs[which][:, at].astype(F32) + refs[len(mine) + which][:, at].astype(F32)
                ref[start : start + count] = total.astype(BF16)
            start += count

    shape = (sum(counts), rows, columns)
    return call(
        body,
        "merge_add",
        (1,),
        [held(*part.shape) for part in mine + came],
        [held(*shape)] * 2,
        [shape_of(BF16, *shape)] * 2,
        (place,) + tuple(mine) + tuple(came),
        vmem=12,
    )


def beside_add(place, mine, came, spot):
    groups, _, rows, _ = mine[0].shape
    widths = [part.shape[-1] for part in mine]

    def body(place_ref, *refs):
        sent_ref, kept_ref = refs[2 * len(mine) :]
        for ref, at in ((sent_ref, 1 - place_ref[spot]), (kept_ref, place_ref[spot])):
            start = 0
            for which, width in enumerate(widths):
                total = refs[which][:, at].astype(F32) + refs[len(mine) + which][:, at].astype(F32)
                ref[:, :, start : start + width] = total.astype(BF16)
                start += width

    shape = (groups, rows, sum(widths))
    return call(
        body,
        "beside_add",
        (1,),
        [held(*part.shape) for part in mine + came],
        [held(*shape)] * 2,
        [shape_of(BF16, *shape)] * 2,
        (place,) + tuple(mine) + tuple(came),
        vmem=12,
    )


def attn_forward_kernel(q_ref, k_ref, v_ref, bias_ref, prob_ref, mixed_ref, total_ref):
    tokens, lanes = q_ref.shape
    half = lanes // 2
    lane = lax.broadcasted_iota(jnp.int32, (tokens, lanes), 1)
    block = lax.broadcasted_iota(jnp.int32, (tokens, lanes), 0) // BLOCK
    scale = half ** -0.5
    q = q_ref[...].astype(jnp.float32) * scale
    k = k_ref[...].astype(jnp.float32)
    v = v_ref[...].astype(jnp.float32)
    sides = []
    for head in range(2):
        own = (lane >= half) if head else (lane < half)
        first = 0 if head else half
        bias = jnp.broadcast_to(bias_ref[head][:, None, :], (tokens // BLOCK, BLOCK, lanes)).reshape(tokens, lanes)
        q_ext = jnp.where(own, q, jnp.where(lane - first == block, 1.0, 0.0)).astype(jnp.bfloat16)
        k_ext = jnp.where(own, k, bias).astype(jnp.bfloat16)
        v_ext = jnp.where(own, v, 1.0).astype(jnp.bfloat16)
        sides.append((q_ext, k_ext, v_ext))
    rows = min(512, tokens)
    low_lane = lax.broadcasted_iota(jnp.int32, (rows, lanes), 1) < half
    for start in range(0, tokens, rows):
        sums = []
        for head, (q_ext, k_ext, v_ext) in enumerate(sides):
            scores = contract(q_ext[start:start + rows], k_ext, 1, 1)
            top = jnp.max(scores, axis=1, keepdims=True)
            prob = jnp.exp(scores - top).astype(jnp.bfloat16)
            prob_ref[head, start:start + rows, :] = prob
            sums.append(contract(prob, v_ext, 1, 0))
        result = jnp.where(low_lane, sums[0], sums[1])
        totals = pltpu.roll(jnp.where(low_lane, sums[1], sums[0]), half, 1)
        mixed_ref[start:start + rows, :] = (result / totals).astype(jnp.bfloat16)
        total_ref[start:start + rows, :] = totals

def attn_backward_kernel(q_ref, k_ref, v_ref, prob_ref, mixed_ref, total_ref, grad_ref, dq_ref, dk_ref, dv_ref):
    tokens, lanes = q_ref.shape
    half = lanes // 2
    scale = half ** -0.5
    lane = lax.broadcasted_iota(jnp.int32, (tokens, lanes), 1)
    grad = grad_ref[...].astype(jnp.float32) / total_ref[...]
    inner = grad * mixed_ref[...].astype(jnp.float32)
    grad_low = grad.astype(jnp.bfloat16)
    q_turned = q_ref[...].T
    grad_turned = grad_low.T
    v = v_ref[...].astype(jnp.float32)
    k = k_ref[...]
    rows = 256
    low_lane = lax.broadcasted_iota(jnp.int32, (rows, lanes), 1) < half
    dq = [[None, None] for _ in range(tokens // rows)]
    dk, dv = [], []
    for head in range(2):
        own = (lane >= half) if head else (lane < half)
        first = 0 if head else half
        minus = -jnp.sum(jnp.where(own, inner, 0.0), axis=1, keepdims=True)
        high = minus.astype(jnp.bfloat16).astype(jnp.float32)
        grad_ext = jnp.where(own, grad, jnp.where(lane == first, high, jnp.where(lane == first + 1, minus - high, 0.0))).astype(jnp.bfloat16)
        v_ext = jnp.where(own, v, jnp.where(lane - first < 2, 1.0, 0.0)).astype(jnp.bfloat16)
        dk_sum = dv_sum = None
        for index in range(tokens // rows):
            part = slice(index * rows, (index + 1) * rows)
            prob = prob_ref[head, part, :]
            spread = contract(grad_ext[part], v_ext, 1, 1)
            grad_scores = (prob.astype(jnp.float32) * spread).astype(jnp.bfloat16)
            dq[index][head] = contract(grad_scores, k, 1, 0)
            rows_of = slice(head * half, (head + 1) * half)
            dk_part = contract(q_turned[rows_of, part], grad_scores, 1, 0)
            dv_part = contract(grad_turned[rows_of, part], prob, 1, 0)
            dk_sum = dk_part if dk_sum is None else dk_sum + dk_part
            dv_sum = dv_part if dv_sum is None else dv_sum + dv_part
        dk.append(dk_sum)
        dv.append(dv_sum)
    for index, pair in enumerate(dq):
        dq_ref[index * rows:(index + 1) * rows, :] = (jnp.where(low_lane, pair[0], pair[1]) * scale).astype(jnp.bfloat16)
    dk_ref[...] = (jnp.concatenate(dk, axis=0) * scale).T.astype(jnp.bfloat16)
    dv_ref[...] = jnp.concatenate(dv, axis=0).T.astype(jnp.bfloat16)


def attn_forward(place, qkv, bias, first, count, before=()):
    tokens, width = qkv.shape[0], qkv.shape[1] // 3
    pairs = width // PAIR

    def at(part):
        return pl.BlockSpec((tokens, PAIR), lambda i, _: (0, part * pairs + first + i))

    def body(place_ref, *refs):
        attn_forward_kernel(*refs[:4], *refs[4 + len(before) :])

    return call(
        body,
        "attn_forward",
        (count,),
        [at(0), at(1), at(2), pl.BlockSpec((2, tokens // BLOCK, PAIR), lambda i, _: (first + i, 0, 0))]
        + [whole_ref()] * len(before),
        [pl.BlockSpec((2, tokens, tokens), lambda i, _: (first + i, 0, 0)), at(0), at(0)],
        [
            shape_of(BF16, 2 * pairs, tokens, tokens),
            shape_of(BF16, tokens, width),
            shape_of(F32, tokens, width),
        ],
        (place, qkv, qkv, qkv, bias) + tuple(before),
        vmem=28,
        alias={5 + i: i for i in range(len(before))},
    )


def attn_backward(place, qkv, prob, mixed, total, grad, first, count, before=()):
    tokens, width = qkv.shape[0], qkv.shape[1] // 3
    pairs = width // PAIR

    def at(part):
        return pl.BlockSpec((tokens, PAIR), lambda i, _: (0, part * pairs + first + i))

    def body(place_ref, *refs):
        attn_backward_kernel(*refs[:7], *refs[7 + len(before) :])

    return call(
        body,
        "attn_backward",
        (count,),
        [at(0), at(1), at(2), pl.BlockSpec((2, tokens, tokens), lambda i, _: (first + i, 0, 0))]
        + [at(0)] * 3
        + [whole_ref()] * len(before),
        [at(0)] * 3,
        [shape_of(BF16, tokens, width)] * 3,
        (place, qkv, qkv, qkv, prob, mixed, total, grad) + tuple(before),
        vmem=28,
        alias={8 + i: i for i in range(len(before))},
    )


def key_bias(random_ids, block_ids):
    heads, blocks, _ = random_ids.shape
    row, col = block_ids[:, None], block_ids[None, :]
    last = blocks - 1
    fixed = (row == 0) | (row == last) | (col == 0) | (col == last) | (jnp.abs(row - col) <= 1)
    drawn = jnp.any(random_ids[:, :, :, None] == block_ids, axis=2)
    bias = jnp.where(fixed[None] | drawn, 0.0, -1e30)
    bias = bias.transpose(0, 2, 1).reshape(heads // 2, 2, blocks, blocks)
    lanes = 128
    even = jnp.pad(bias[:, 0], ((0, 0), (0, 0), (lanes // 2, lanes // 2 - blocks)))
    odd = jnp.pad(bias[:, 1], ((0, 0), (0, 0), (0, lanes - blocks)))
    return jnp.stack([even, odd], axis=1).reshape(heads, blocks, lanes)


def pair_swap(value, axis, bit):
    size = lax.axis_size(axis)
    return lax.ppermute(value, axis, [(i, i ^ bit) for i in range(size)])


def pick(value, index, axis):
    return lax.dynamic_index_in_dim(value, index, axis, keepdims=False)


def swap_x(value):
    return pair_swap(value, "dp", 2)


def swap_core(value):
    return pair_swap(value, "dp", 1)


def swap_y(value):
    return pair_swap(value, "seq", 1)


def swap_xy(value):
    pairs = 2 * lax.axis_size("dp")
    return lax.ppermute(value, BOTH, [(i, i ^ 5) for i in range(pairs)])


def ring_z(value, step):
    size = lax.axis_size("dp")
    return lax.ppermute(value, "dp", [(i, (i + 4 * step) % size) for i in range(size)])


def tie(*values):
    return lax.optimization_barrier(values)


class Reduce:
    def __init__(self, place, rows, x_first):
        self.place, self.rows, self.x_first = place, rows, x_first

    def begin(self, mine, other):
        self.mine, self.came = mine, swap_core(other)

    def first(self):
        groups, tall, columns = self.mine.shape
        if self.x_first:
            shape = (groups // 2, 2, tall, columns)
        else:
            shape = (groups, 2, self.rows, columns)
        spot, swap = (1, swap_x) if self.x_first else (3, swap_y)
        sent, kept = split_add(self.place, self.mine.reshape(shape), self.came.reshape(shape), spot)
        self.mine, self.came = kept, swap(sent)

    def second(self, *others, beside=False):
        spot, swap = (3, swap_y) if self.x_first else (1, swap_x)
        mine, came = [], []
        for part in (self,) + others:
            shape = (-1, 2, self.rows, part.mine.shape[-1])
            mine.append(part.mine.reshape(shape))
            came.append(part.came.reshape(shape))
        if beside:
            sent, kept = beside_add(self.place, mine, came, spot)
        elif others:
            sent, kept = merge_add(self.place, mine, came, spot)
        else:
            sent, kept = split_add(self.place, mine[0], came[0], spot)
        self.mine, self.came = kept, swap(sent)

    def third(self, *others, vectors=None, sizes=()):
        parts = (self,) + others
        rows = min(part.rows for part in parts)
        pairs = [(part.mine, part.came) for part in parts]
        own, *sent = split_depth(self.place, pairs, rows, vectors, sizes)
        self.mine = own
        self.came = [ring_z(block, step + 1) for step, block in enumerate(sent)]

    def last(self, *shapes):
        return last_add(self.place, self.mine, self.came, shapes)

    def hold(self, *others):
        self.mine, self.came, others = tie(self.mine, self.came, others)
        return others


def split_depth_spot(place_ref, step, depth):
    return lax.rem(place_ref[0] + depth - step, depth)


def join_depth(place, blocks, cuts, name):
    depth = len(blocks)
    rows = blocks[0].shape[0]
    moves = []
    for step in range(depth):
        for j, (start, stop) in enumerate(cuts):
            cut = (slice(None), slice(start, stop))
            moves.append((step, cut, j, lambda p, step=step: split_depth_spot(p, step, depth)))
    return join(place, blocks, moves, [(depth, rows, stop - start) for start, stop in cuts], name)


def join_plane(place, blocks):
    moves = []
    for at, (dx, dy) in enumerate(((0, 0), (1, 0), (0, 1), (1, 1))):
        moves.append(
            (at, (), 0, lambda p, dx=dx, dy=dy: (flip(p[1], dx), flip(p[3], dy)))
        )
    return join(place, blocks, moves, [(2, 2) + blocks[0].shape], "join_plane")[0]


def near_parts(own, by_x, by_y, by_xy, cores):
    blocks = {(0, 0): own, (1, 0): by_x, (0, 1): by_y, (1, 1): by_xy}
    return [cores[dx, dy] if dc else blocks[dx, dy] for dx, dc, dy in NEAR]


def paired(inputs, grad_out, random_blocks, *shards):
    depth = lax.axis_size("dp") // 4
    dp, y = lax.axis_index("dp"), lax.axis_index("seq")
    z, x, c = dp // 4, (dp // 2) % 2, dp % 2
    spots = (z, x, c, y)
    place = jnp.stack(spots).astype(jnp.int32)
    w_query, w_key, w_value, w_out, w_up, w_down = shards[:6]
    vectors = shards[6:]
    half, width = inputs.shape[1:]
    rows, tall_rows, hidden_width = w_up.shape[0], w_down.shape[0], w_up.shape[1]
    pairs = width // PAIR
    ring = range(1, depth)

    sizes = [vector.shape[0] // rows for vector in vectors]
    small = jnp.concatenate([vector.reshape(-1, rows) for vector in vectors])
    small = jnp.pad(small, ((0, rows - small.shape[0]), (0, PAIR - rows)))
    shard = join_beside(place, [w_query, w_key, w_value, w_out, small])
    turned = [shard] + [ring_z(shard, step) for step in ring]
    tall_cut = tall_rows // 2
    down_near, down_own = w_down[tall_cut:], w_down[:tall_cut]
    down_x = swap_x(down_own)
    random_far = swap_y(pick(random_blocks, 1 - y, 0))
    random_far, far_rows = tie(random_far, cast_far(place, inputs))
    far_rows = swap_y(far_rows)
    up_shard = join_beside(
        place, [w_up] + [down_near[start : start + rows] for start in range(0, tall_cut, rows)]
    )
    at_out = width
    turned, down_x, far_rows, up_shard, down_own, random_far, grad_out = tie(
        turned, down_x, far_rows, up_shard, down_own, random_far, grad_out
    )
    cut = 2 * width
    left, right = join_depth(place, turned, [(0, cut), (cut, shard.shape[1])], "join_first")
    left_y, right_x = swap_y(left), swap_x(right)
    up_turned = {1: ring_z(up_shard, 1), depth - 1: ring_z(up_shard, depth - 1)}
    down_y, down_xy = swap_y(down_own), swap_y(down_x)
    far_grad_low = cast_far(place, grad_out)
    left_y, right_x, up_turned, down_own, down_x, down_y, down_xy, far_grad_low, random_far = tie(
        left_y, right_x, up_turned, down_own, down_x, down_y, down_xy, far_grad_low, random_far
    )
    left_x, left_xy = swap_x(left), swap_x(left_y)
    right_y, right_xy = swap_y(right), swap_y(right_x)
    for step in ring:
        if step not in up_turned:
            up_turned[step] = ring_z(up_shard, step)
    plane = join_plane(place, [down_own, down_x, down_y, down_xy])
    local_blocks = half // BLOCK
    ids = jnp.arange(2 * local_blocks, dtype=jnp.int32)
    block_ids = (ids + y * local_blocks) % (2 * local_blocks)
    random_ids = jnp.concatenate([pick(random_blocks, y, 0), random_far], axis=1)
    bias = key_bias(random_ids, block_ids)
    left_x, left_xy, right_y, right_xy, up_turned, left_y, right_x, plane, bias = tie(
        left_x, left_xy, right_y, right_xy, up_turned, left_y, right_x, plane, bias
    )
    (up_own,) = join_depth(
        place, [up_shard] + [up_turned[step] for step in ring], [(0, up_shard.shape[1])], "join_up"
    )
    up_own, left, left_x, left_y, left_xy, right, right_x, right_y, right_xy = tie(
        up_own, left, left_x, left_y, left_xy, right, right_x, right_y, right_xy
    )
    up_y, up_x = swap_y(up_own), swap_x(up_own)
    left_core = {
        (0, 0): swap_core(left), (0, 1): swap_core(left_y),
        (1, 0): swap_core(left_x), (1, 1): swap_core(left_xy),
    }
    right_core = {
        (0, 0): swap_core(right), (0, 1): swap_core(right_y),
        (1, 0): swap_core(right_x), (1, 1): swap_core(right_xy),
    }
    left_parts = near_parts(left, left_x, left_y, left_xy, left_core)
    right_parts = near_parts(right, right_x, right_y, right_xy, right_core)
    left_parts, right_parts, up_own = tie(left_parts, right_parts, up_own)

    planes = {0: plane, 1: ring_z(plane, 1), depth - 1: ring_z(plane, depth - 1)}
    spans = small_vectors(place, right_parts, cut, sizes, rows)
    (
        ln1_gain,
        ln1_bias,
        query_bias,
        value_bias,
        out_bias,
        ln2_gain,
        ln2_bias,
        up_bias,
        down_bias,
    ) = spans
    qkv_bias = jnp.concatenate([query_bias, jnp.zeros_like(query_bias), value_bias], axis=1)
    normed_low, qkv = norm_project(
        place, inputs, far_rows, ln1_gain, ln1_bias, left_parts, right_parts, qkv_bias
    )
    near_pairs = 3 * pairs // 8
    attended = attn_forward(place, qkv, bias, 0, near_pairs)
    attended, up_y, up_x, planes, far_grad_low = tie(attended, up_y, up_x, planes, far_grad_low)
    up_xy = swap_x(up_y)
    up_core = {(0, 0): swap_core(up_own), (0, 1): swap_core(up_y)}
    far_grad = swap_y(far_grad_low)
    for step in ring:
        if step not in planes:
            planes[step] = ring_z(planes[0], step)
    prob, mixed_low, totals = attn_forward(
        place, qkv, bias, near_pairs, pairs - near_pairs, attended
    )
    mixed_low, far_grad, up_core, up_x, planes = tie(mixed_low, far_grad, up_core, up_x, planes)
    up_core[1, 0] = swap_core(up_x)
    plane_core = {step: swap_core(planes[step]) for step in (0, 1, depth - 1)}
    grad_ff_low, grad_down_bias = join_low(place, grad_out, far_grad)
    mixed_low, grad_ff_low = tie(mixed_low, grad_ff_low)
    middle, normed_two_low, start_out = out_norm(
        place, mixed_low, right_parts, at_out, out_bias, inputs, far_rows, ln2_gain, ln2_bias, down_bias
    )
    normed_two_low, up_xy, plane_core, up_core, planes = tie(
        normed_two_low, up_xy, plane_core, up_core, planes
    )
    up_core[1, 1] = swap_core(up_xy)
    for step in ring:
        if step not in plane_core:
            plane_core[step] = swap_core(planes[step])
    up_parts = near_parts(up_own, up_x, up_y, up_xy, up_core)
    down_parts = [part for step in range(depth) for part in (planes[step], plane_core[step])]

    down_sums = [Reduce(place, tall_rows, True) for _ in range(3)]
    near_sum = Reduce(place, rows, False)
    wide_sum = Reduce(place, rows, True)
    out_sum = Reduce(place, rows, True)
    left_sum = Reduce(place, rows, True)
    right_sum = Reduce(place, rows, False)

    def feed(first, count, state, wide):
        return feed_forward(
            place, first, count, depth, normed_two_low, grad_ff_low, up_parts, down_parts, up_bias,
            far_rows, state, wide,
        )

    near = depth // 2
    near_width = hidden_width // 2
    each = hidden_width // depth
    mine, other, up_mine, up_other, bias_0, back, total = feed(
        0, near, (start_out, start_out), (near_width, 0, ())
    )
    down_sums[0].begin(mine, other)
    near_sum.begin(up_mine, up_other)
    mine, other, up_mine, up_other, bias_1, back, total = feed(
        near, depth - 1 - near, (total, back), (near_width, 0, ())
    )
    (back,) = down_sums[0].hold(back)
    (back,) = near_sum.hold(back)
    down_sums[1].begin(mine, other)
    down_sums[0].first()
    near_sum.first()
    down_sums[0].mine, near_sum.mine, back = tie(down_sums[0].mine, near_sum.mine, back)
    mine, other, up_mine, up_other, bias_2, back, out_part, out_delta = feed(
        depth - 1, 1, (total, back), (near_width, (depth - 1 - near) * each, (up_mine, up_other))
    )
    (back,) = down_sums[0].hold(back)
    (back,) = near_sum.hold(back)
    (back,) = down_sums[1].hold(back)
    down_sums[2].begin(mine, other)
    wide_sum.begin(up_mine, up_other)
    down_sums[1].first()
    down_sums[1].mine, back = tie(down_sums[1].mine, back)
    grad_up_bias = jnp.concatenate([bias_0, bias_1, bias_2], axis=1)
    grad_middle, grad_attn_low, grad_mixed_low, grad_ln2_gain, grad_ln2_bias, grad_out_bias = middle_back(
        place, back, middle, ln2_gain, grad_out, far_grad, right_parts, at_out
    )
    out_sum.begin(*grad_wide(place, mixed_low, (grad_attn_low,), rows, (0, 2)))
    out_sum.mine, grad_mixed_low = tie(out_sum.mine, grad_mixed_low)
    (grad_mixed_low,) = down_sums[1].hold(grad_mixed_low)
    (grad_mixed_low,) = down_sums[2].hold(grad_mixed_low)
    (grad_mixed_low,) = wide_sum.hold(grad_mixed_low)
    down_sums[2].first()
    near_sum.second()
    down_sums[2].mine, near_sum.mine, grad_mixed_low, out_delta = tie(
        down_sums[2].mine, near_sum.mine, grad_mixed_low, out_delta
    )
    out_far = swap_y(out_delta)
    grads = attn_backward(place, qkv, prob, mixed_low, totals, grad_mixed_low, 0, pairs // 2)
    grads, out_far = tie(grads, out_far)
    (grads,) = near_sum.hold(grads)
    (grads,) = down_sums[2].hold(grads)
    (grads,) = out_sum.hold(grads)
    wide_sum.first()
    out_sum.first()
    near_sum.third()
    down_sums[0].second(*down_sums[1:])
    down_sum = down_sums[0]
    down_sum.mine, near_sum.mine, wide_sum.mine, out_sum.mine, grads = tie(
        down_sum.mine, near_sum.mine, wide_sum.mine, out_sum.mine, grads
    )
    grads = attn_backward(
        place, qkv, prob, mixed_low, totals, grad_mixed_low, pairs // 2, pairs - pairs // 2, grads
    )
    (grads,) = near_sum.hold(grads)
    (grads,) = wide_sum.hold(grads)
    (grads,) = down_sum.hold(grads)
    wide_sum.second()
    wide_sum.mine, grads = tie(wide_sum.mine, grads)
    wide = grad_wide(place, normed_low, grads, rows, (0, 6), 2)
    (wide,) = wide_sum.hold(wide)
    (wide,) = out_sum.hold(wide)
    out_sum.second()
    out_sum.mine, wide = tie(out_sum.mine, wide)
    left_sum.begin(*wide[:2])
    right_sum.begin(*wide[2:])
    (grad_up_near,) = near_sum.last((rows, near_width))
    left_sum.mine, grads, grad_up_near = tie(left_sum.mine, grads, grad_up_near)
    (grads,) = out_sum.hold(grads)
    (grads,) = left_sum.hold(grads)
    left_sum.first()
    (grads,) = right_sum.hold(grads)
    right_sum.first()
    down_sum.third(wide_sum, out_sum)
    left_sum.mine, right_sum.mine, down_sum.mine, grads = tie(
        left_sum.mine, right_sum.mine, down_sum.mine, grads
    )
    in_part, in_delta, grad_ln1_gain, grad_ln1_bias, grad_query_bias, grad_value_bias = input_back(
        place, grads, left_parts, right_parts, inputs, far_rows, ln1_gain, grad_middle, far_grad
    )
    (in_delta,) = left_sum.hold(in_delta)
    left_sum.second()
    (in_delta,) = right_sum.hold(in_delta)
    right_sum.second()
    left_sum.mine, right_sum.mine, in_delta, grad_ln1_gain = tie(
        left_sum.mine, right_sum.mine, in_delta, grad_ln1_gain
    )
    grad_vectors = (
        grad_ln1_gain,
        grad_ln1_bias,
        grad_query_bias,
        grad_value_bias,
        grad_out_bias,
        grad_ln2_gain,
        grad_ln2_bias,
        grad_up_bias,
        grad_down_bias,
    )
    packed = jnp.concatenate(grad_vectors, axis=1).reshape(-1, PAIR)
    packed = packed + swap_core(packed)
    packed = packed + swap_x(packed) + swap_y(packed) + swap_xy(packed)
    (in_delta,) = down_sum.hold(in_delta)
    (in_delta,) = left_sum.hold(in_delta)
    (in_delta,) = right_sum.hold(in_delta)
    packed, in_delta = tie(packed, in_delta)
    in_far = swap_y(in_delta)
    left_sum.third(right_sum, vectors=packed, sizes=sizes)
    left_sum.mine, out_far, down_sum.mine = tie(left_sum.mine, out_far, down_sum.mine)
    grad_w_down, grad_up_far, grad_w_out = down_sum.last(w_down.shape, (rows, near_width), w_out.shape)
    result = fill_far(place, out_part, inputs, out_far)
    result, in_far, grad_up_far = tie(result, in_far, grad_up_far)
    grad_in = fill_far(place, in_part, grad_out, in_far)
    left_sum.came, grad_in = tie(left_sum.came, grad_in)
    grad_w_up = jnp.concatenate([grad_up_near, grad_up_far], axis=1)
    square, part = (rows, width), (rows, width // 2)
    grad_left_q, grad_left_k, grad_right_k, grad_right_v, packed = left_sum.last(
        square, part, part, square, (rows, PAIR)
    )
    packed = packed.reshape(-1)
    out_vectors = []
    for index, size in enumerate(sizes):
        count = size * rows
        lane = (dp * 2 + y) * count % PAIR
        out_vectors.append(lax.dynamic_slice_in_dim(packed, index * PAIR + lane, count))
    grad_w_key = jnp.concatenate([grad_left_k, grad_right_k], axis=1)
    return (
        (result, grad_in, grad_left_q, grad_w_key, grad_right_v, grad_w_out, grad_w_up, grad_w_down)
        + tuple(out_vectors)
    )


def solution(mesh):
    tokens, table, matrix, vector = P("dp", "seq", None), P("dp", None, "seq", None), P(BOTH, None), P(BOTH)
    in_specs = (tokens, tokens, table) + (matrix,) * 6 + (vector,) * 9
    out_specs = (tokens, tokens) + (matrix,) * 6 + (vector,) * 9
    paired_fits = mesh.shape["seq"] == 2 and mesh.shape["dp"] % 4 == 0

    def body(inputs, *rest):
        whole = paired if paired_fits and inputs.shape[0] == 2 else on_device
        return whole(inputs, *rest)

    return jax.shard_map(
        body, mesh=mesh, in_specs=in_specs, out_specs=out_specs, check_vma=False
    )
```

```python
import jax
import jax.numpy as jnp
from jax import lax
from jax.experimental import pallas as pl
from jax.experimental.pallas import tpu as pltpu
from jax.sharding import PartitionSpec as P

HEADS = 16
BLOCK = 64
BOTH = ("dp", "seq")


eps_norm = 1e-05
neg_fill = -1e30


def layer_norm(values, norm_gain, norm_shift):
    centre = values - jnp.mean(values, axis=-1, keepdims=True)
    spread = jnp.mean(centre * centre, axis=-1, keepdims=True)
    return centre * lax.rsqrt(spread + eps_norm) * norm_gain + norm_shift


def gelu_tanh(values):
    return jax.nn.gelu(values, approximate=True)


def project(left, right):
    return jnp.dot(left, right, preferred_element_type=jnp.float32)


def project_back(grad_rows, weight):
    return lax.dot_general(
        grad_rows, weight, (((1,), (1,)), ((), ())), preferred_element_type=jnp.float32
    )


def weight_grad(left, grad_rows):
    return lax.dot_general(
        left, grad_rows, (((0,), (0,)), ((), ())), preferred_element_type=jnp.float32
    )


def column_sum(grad_rows):
    return jnp.sum(grad_rows, axis=0, dtype=jnp.float32)


def to_table(block_rows):
    block_count = block_rows.shape[0] // BLOCK
    head_dim = block_rows.shape[1] // HEADS
    shaped = block_rows.reshape(block_count, BLOCK, HEADS, head_dim)
    return shaped.transpose(2, 0, 1, 3).reshape(HEADS, block_count, BLOCK * head_dim)


def from_table(table):
    block_count = table.shape[1]
    head_dim = table.shape[2] // BLOCK
    shaped = table.reshape(HEADS, block_count, BLOCK, head_dim)
    return shaped.transpose(1, 2, 0, 3).reshape(block_count * BLOCK, HEADS * head_dim)


def key_layout(first_block, local_blocks, all_blocks, random_ids):
    query_ids = first_block + jnp.arange(local_blocks, dtype=jnp.int32)
    window = jnp.stack([query_ids - 1, query_ids, query_ids + 1], axis=1)
    inside = (window >= 1) & (window <= all_blocks - 2)
    window = jnp.clip(window, 0, all_blocks - 1)
    end_blocks = jnp.broadcast_to(jnp.array([0, all_blocks - 1], jnp.int32), (local_blocks, 2))
    fixed_slots = jnp.concatenate([end_blocks, window], axis=1)
    key_slots = jnp.concatenate(
        [jnp.broadcast_to(fixed_slots[None], (HEADS, local_blocks, 5)), random_ids], axis=2
    )
    key_valid = jnp.concatenate(
        [
            jnp.ones((local_blocks, 2), jnp.bool_),
            inside,
            jnp.ones((local_blocks, random_ids.shape[2]), jnp.bool_),
        ],
        axis=1,
    )
    return (key_slots, jnp.repeat(key_valid, BLOCK, axis=1))


def pick_blocks(table, key_slots):
    head_index = jnp.arange(HEADS)[:, None, None]
    picked = table[head_index, key_slots]
    head_dim = table.shape[2] // BLOCK
    return picked.reshape(HEADS, key_slots.shape[1], key_slots.shape[2] * BLOCK, head_dim)


def sparse_scores(query_heads, key_picked, key_valid, score_scale):
    raw_scores = jnp.einsum(
        "hqid,hqkd->hqik", query_heads, key_picked, preferred_element_type=jnp.float32
    )
    return jnp.where(key_valid[None, :, None, :], raw_scores * score_scale, neg_fill)


def dense_scores(query_block, key_flat, score_scale):
    return (
        jnp.einsum("hid,hkd->hik", query_block, key_flat, preferred_element_type=jnp.float32)
        * score_scale
    )


def dense_forward(query_block, key_flat, value_flat, score_scale):
    scores = dense_scores(query_block, key_flat, score_scale)
    top_score = jnp.max(scores, axis=-1, keepdims=True)
    expos = jnp.exp(scores - top_score)
    totals = jnp.sum(expos, axis=-1, keepdims=True)
    attn_prob = (expos / totals).astype(jnp.bfloat16)
    result = jnp.einsum("hik,hkd->ihd", attn_prob, value_flat, preferred_element_type=jnp.float32)
    return (result, (top_score + jnp.log(totals))[..., 0])


def softmax_back(attn_prob, grad_prob, score_scale):
    inner = jnp.sum(attn_prob * grad_prob, axis=-1, keepdims=True)
    return (attn_prob * (grad_prob - inner) * score_scale).astype(jnp.bfloat16)


def dense_backward(query_block, key_flat, value_flat, grad_block, log_total, score_scale):
    attn_prob = jnp.exp(dense_scores(query_block, key_flat, score_scale) - log_total[..., None])
    grad_prob = jnp.einsum(
        "ihd,hkd->hik", grad_block, value_flat, preferred_element_type=jnp.float32
    )
    grad_value = jnp.einsum(
        "hik,ihd->hkd",
        attn_prob.astype(jnp.bfloat16),
        grad_block,
        preferred_element_type=jnp.float32,
    )
    grad_scores = softmax_back(attn_prob, grad_prob, score_scale)
    grad_query = jnp.einsum(
        "hik,hkd->ihd", grad_scores, key_flat, preferred_element_type=jnp.float32
    )
    grad_key = jnp.einsum(
        "hik,hid->hkd", grad_scores, query_block, preferred_element_type=jnp.float32
    )
    return (grad_query, grad_key, grad_value)


def run_forward(weights, in_rows, random_ids):
    (
        w_query,
        w_key,
        w_value,
        w_out,
        w_up,
        w_down,
        ln1_gain,
        ln1_bias,
        query_bias,
        value_bias,
        out_bias,
        ln2_gain,
        ln2_bias,
        up_bias,
        down_bias,
    ) = weights
    normed, pull_first = jax.vjp(
        layer_norm, in_rows, ln1_gain.astype(jnp.float32), ln1_bias.astype(jnp.float32)
    )
    normed_low = normed.astype(jnp.bfloat16)
    queries = (project(normed_low, w_query) + query_bias.astype(jnp.float32)).astype(jnp.bfloat16)
    key_rows = project(normed_low, w_key).astype(jnp.bfloat16)
    value_rows = (project(normed_low, w_value) + value_bias.astype(jnp.float32)).astype(
        jnp.bfloat16
    )
    key_all, value_all = (
        lax.all_gather(key_rows, "seq", axis=0, tiled=True),
        lax.all_gather(value_rows, "seq", axis=0, tiled=True),
    )
    place = lax.axis_index("seq")
    ranks = lax.axis_size("seq")
    local_blocks = in_rows.shape[0] // BLOCK
    all_blocks = key_all.shape[0] // BLOCK
    head_dim = queries.shape[1] // HEADS
    score_scale = head_dim ** (-0.5)
    key_slots, key_valid = key_layout(place * local_blocks, local_blocks, all_blocks, random_ids)
    key_table = to_table(key_all)
    value_table = to_table(value_all)
    key_picked = pick_blocks(key_table, key_slots)
    value_picked = pick_blocks(value_table, key_slots)
    query_heads = to_table(queries).reshape(HEADS, local_blocks, BLOCK, head_dim)
    scores = sparse_scores(query_heads, key_picked, key_valid, score_scale)
    top_score = jnp.max(scores, axis=-1, keepdims=True)
    expos = jnp.exp(scores - top_score)
    totals = jnp.sum(expos, axis=-1, keepdims=True)
    prob_low = (expos / totals).astype(jnp.bfloat16)
    log_sparse = (top_score + jnp.log(totals))[..., 0]
    sparse_out = jnp.einsum(
        "hqik,hqkd->qihd", prob_low, value_picked, preferred_element_type=jnp.float32
    )
    is_edge = (place == 0) | (place == ranks - 1)
    edge_slot = jnp.where(place == 0, 0, local_blocks - 1)
    key_flat = key_table.reshape(HEADS, all_blocks * BLOCK, head_dim)
    value_flat = value_table.reshape(HEADS, all_blocks * BLOCK, head_dim)
    query_edge = lax.dynamic_index_in_dim(query_heads, edge_slot, 1, keepdims=False)
    edge_out, log_edge = lax.cond(
        is_edge,
        lambda: dense_forward(query_edge, key_flat, value_flat, score_scale),
        lambda: (
            jnp.zeros((BLOCK, HEADS, head_dim), jnp.float32),
            jnp.zeros((HEADS, BLOCK), jnp.float32),
        ),
    )
    current = lax.dynamic_index_in_dim(sparse_out, edge_slot, 0, keepdims=False)
    mixed_heads = lax.dynamic_update_index_in_dim(
        sparse_out, jnp.where(is_edge, edge_out, current), edge_slot, 0
    )
    mixed_low = mixed_heads.reshape(in_rows.shape[0], queries.shape[1]).astype(jnp.bfloat16)
    middle = in_rows + (project(mixed_low, w_out) + out_bias.astype(jnp.float32))
    normed_two, pull_second = jax.vjp(
        layer_norm, middle, ln2_gain.astype(jnp.float32), ln2_bias.astype(jnp.float32)
    )
    normed_two_low = normed_two.astype(jnp.bfloat16)
    hidden_pre = project(normed_two_low, w_up) + up_bias.astype(jnp.float32)
    hidden, pull_gelu = jax.vjp(gelu_tanh, hidden_pre)
    hidden_low = hidden.astype(jnp.bfloat16)
    result = middle + (project(hidden_low, w_down) + down_bias.astype(jnp.float32))
    saved = {
        "pull_first": pull_first,
        "pull_second": pull_second,
        "pull_gelu": pull_gelu,
        "normed_low": normed_low,
        "normed_two_low": normed_two_low,
        "hidden_low": hidden_low,
        "mixed_low": mixed_low,
        "query_heads": query_heads,
        "query_edge": query_edge,
        "key_picked": key_picked,
        "value_picked": value_picked,
        "key_flat": key_flat,
        "value_flat": value_flat,
        "key_slots": key_slots,
        "key_valid": key_valid,
        "log_sparse": log_sparse,
        "log_edge": log_edge,
        "is_edge": is_edge,
        "edge_slot": edge_slot,
    }
    return (saved, result)


def run_backward(weights, saved, grad_rows):
    (
        w_query,
        w_key,
        w_value,
        w_out,
        w_up,
        w_down,
        ln1_gain,
        ln1_bias,
        query_bias,
        value_bias,
        out_bias,
        ln2_gain,
        ln2_bias,
        up_bias,
        down_bias,
    ) = weights
    query_heads = saved["query_heads"]
    key_picked = saved["key_picked"]
    value_picked = saved["value_picked"]
    key_slots = saved["key_slots"]
    is_edge = saved["is_edge"]
    edge_slot = saved["edge_slot"]
    local_blocks = query_heads.shape[1]
    head_dim = query_heads.shape[3]
    all_blocks = saved["key_flat"].shape[1] // BLOCK
    score_scale = head_dim ** (-0.5)
    token_count = grad_rows.shape[0]
    grad_ff_low = grad_rows.astype(jnp.bfloat16)
    grad_w_down = weight_grad(saved["hidden_low"], grad_ff_low)
    grad_down_bias = column_sum(grad_ff_low)
    (grad_pre,) = saved["pull_gelu"](project_back(grad_ff_low, w_down))
    grad_pre_low = grad_pre.astype(jnp.bfloat16)
    grad_w_up = weight_grad(saved["normed_two_low"], grad_pre_low)
    grad_up_bias = column_sum(grad_pre_low)
    grad_normed_two = project_back(grad_pre_low, w_up)
    grad_middle, grad_ln2_gain, grad_ln2_bias = saved["pull_second"](grad_normed_two)
    grad_middle = grad_middle + grad_rows
    grad_attn_low = grad_middle.astype(jnp.bfloat16)
    grad_w_out = weight_grad(saved["mixed_low"], grad_attn_low)
    grad_out_bias = column_sum(grad_attn_low)
    grad_mixed = (
        project_back(grad_attn_low, w_out)
        .astype(jnp.bfloat16)
        .reshape(local_blocks, BLOCK, HEADS, head_dim)
    )
    block_ids = jnp.arange(local_blocks, dtype=jnp.int32)
    keep_sparse = jnp.where(is_edge & (block_ids == edge_slot), 0.0, 1.0).astype(jnp.bfloat16)
    grad_sparse = grad_mixed * keep_sparse[:, None, None, None]
    scores = sparse_scores(query_heads, key_picked, saved["key_valid"], score_scale)
    attn_prob = jnp.exp(scores - saved["log_sparse"][..., None])
    grad_prob = jnp.einsum(
        "qihd,hqkd->hqik", grad_sparse, value_picked, preferred_element_type=jnp.float32
    )
    grad_value_picked = jnp.einsum(
        "hqik,qihd->hqkd",
        attn_prob.astype(jnp.bfloat16),
        grad_sparse,
        preferred_element_type=jnp.float32,
    )
    grad_scores = softmax_back(attn_prob, grad_prob, score_scale)
    grad_query_sparse = jnp.einsum(
        "hqik,hqkd->qihd", grad_scores, key_picked, preferred_element_type=jnp.float32
    )
    grad_key_picked = jnp.einsum(
        "hqik,hqid->hqkd", grad_scores, query_heads, preferred_element_type=jnp.float32
    )
    head_index = jnp.arange(HEADS)[:, None, None]
    slot_count = key_slots.shape[2]
    table_shape = (HEADS, all_blocks, BLOCK * head_dim)
    grad_key_table = (
        jnp.zeros(table_shape, jnp.float32)
        .at[head_index, key_slots]
        .add(grad_key_picked.reshape(HEADS, local_blocks, slot_count, BLOCK * head_dim))
    )
    grad_value_table = (
        jnp.zeros(table_shape, jnp.float32)
        .at[head_index, key_slots]
        .add(grad_value_picked.reshape(HEADS, local_blocks, slot_count, BLOCK * head_dim))
    )
    grad_edge_block = lax.dynamic_index_in_dim(grad_mixed, edge_slot, 0, keepdims=False)
    flat_shape = (HEADS, all_blocks * BLOCK, head_dim)
    grad_query_edge, grad_key_edge, grad_value_edge = lax.cond(
        is_edge,
        lambda: dense_backward(
            saved["query_edge"],
            saved["key_flat"],
            saved["value_flat"],
            grad_edge_block,
            saved["log_edge"],
            score_scale,
        ),
        lambda: (
            jnp.zeros((BLOCK, HEADS, head_dim), jnp.float32),
            jnp.zeros(flat_shape, jnp.float32),
            jnp.zeros(flat_shape, jnp.float32),
        ),
    )
    grad_key_table = grad_key_table + grad_key_edge.reshape(table_shape)
    grad_value_table = grad_value_table + grad_value_edge.reshape(table_shape)
    grad_key_own, grad_value_own = (
        lax.psum_scatter(
            from_table(grad_key_table).astype(jnp.bfloat16), "seq", scatter_dimension=0, tiled=True
        ).astype(jnp.float32),
        lax.psum_scatter(
            from_table(grad_value_table).astype(jnp.bfloat16),
            "seq",
            scatter_dimension=0,
            tiled=True,
        ).astype(jnp.float32),
    )
    current = lax.dynamic_index_in_dim(grad_query_sparse, edge_slot, 0, keepdims=False)
    grad_query_all = lax.dynamic_update_index_in_dim(
        grad_query_sparse, current + grad_query_edge, edge_slot, 0
    )
    grad_query_low = grad_query_all.reshape(token_count, HEADS * head_dim).astype(jnp.bfloat16)
    grad_key_low = grad_key_own.astype(jnp.bfloat16)
    grad_value_low = grad_value_own.astype(jnp.bfloat16)
    normed_low = saved["normed_low"]
    grad_w_query = weight_grad(normed_low, grad_query_low)
    grad_w_key = weight_grad(normed_low, grad_key_low)
    grad_w_value = weight_grad(normed_low, grad_value_low)
    grad_query_bias = column_sum(grad_query_low)
    grad_value_bias = column_sum(grad_value_low)
    grad_normed = (
        project_back(grad_query_low, w_query)
        + project_back(grad_key_low, w_key)
        + project_back(grad_value_low, w_value)
    )
    grad_inputs, grad_ln1_gain, grad_ln1_bias = saved["pull_first"](grad_normed)
    grad_inputs = grad_inputs + grad_middle
    grads = (
        grad_w_query,
        grad_w_key,
        grad_w_value,
        grad_w_out,
        grad_w_up,
        grad_w_down,
        grad_ln1_gain,
        grad_ln1_bias,
        grad_query_bias,
        grad_value_bias,
        grad_out_bias,
        grad_ln2_gain,
        grad_ln2_bias,
        grad_up_bias,
        grad_down_bias,
    )
    return (grad_inputs, grads)


def on_device(inputs, grad_out, random_blocks, *shards):
    weights = tuple(lax.all_gather(part, BOTH, axis=0, tiled=True) for part in shards)

    def micro_step(totals, sequence):
        in_rows, grad_rows, random_ids = sequence
        saved, result = run_forward(weights, in_rows, random_ids)
        grad_in, grads = run_backward(weights, saved, grad_rows)
        return (tuple(left + right for left, right in zip(totals, grads)), (result, grad_in))

    initial = tuple(jnp.zeros(weight.shape, jnp.float32) for weight in weights)
    totals, (results, grads_in) = lax.scan(micro_step, initial, (inputs, grad_out, random_blocks))
    summed = tuple(
        lax.psum_scatter(total, BOTH, scatter_dimension=0, tiled=True) for total in totals
    )
    return (results, grads_in) + summed


F32, BF16 = jnp.float32, jnp.bfloat16
PAIR = 128
TIMES = dict(
    cast_far=1,
    join_first=2,
    join_beside=1,
    join_up=2,
    join_plane=2,
    small_vectors=2,
    norm_project=4,
    attn_forward=0.5,
    out_norm=1,
    join_low=0.3,
    feed_forward=9,
    split_add=0.1,
    merge_add=0.3,
    beside_add=0.3,
    middle_back=40,
    grad_wide=1.8,
    attn_backward=5,
    split_depth=0.3,
    input_back=1,
    pack_vectors=0.3,
    fill_far=0.05,
    last_add=0.05,
)
COST = 0.3 * 1e9
NEAR = tuple((dx, dc, dy) for dx in range(2) for dc in range(2) for dy in range(2))


def contract(left, right, left_dim, right_dim):
    return lax.dot_general(
        left, right, (((left_dim,), (right_dim,)), ((), ())), preferred_element_type=F32
    )


def held(*shape):
    zeros = (0,) * len(shape)
    return pl.BlockSpec(shape, lambda *_: zeros, pipeline_mode=pl.Buffered(1))


def whole_ref():
    return pl.BlockSpec(memory_space=pltpu.HBM)


def call(body, name, grid, in_specs, out_specs, out_shape, args, scratch=(), vmem=24, alias=None):
    spec = pltpu.PrefetchScalarGridSpec(
        num_scalar_prefetch=1,
        grid=grid,
        in_specs=in_specs,
        out_specs=out_specs,
        scratch_shapes=scratch,
    )
    return pl.pallas_call(
        body,
        grid_spec=spec,
        out_shape=out_shape,
        name=name,
        input_output_aliases=alias or {},
        compiler_params=pltpu.CompilerParams(vmem_limit_bytes=vmem << 20),
        cost_estimate=pl.CostEstimate(
            flops=int(TIMES[name] * grid[0] * COST), bytes_accessed=1, transcendentals=1
        ),
    )(*args)


def shape_of(kind, *shape):
    return jax.ShapeDtypeStruct(shape, kind)


def norm_parts(values):
    mean = jnp.mean(values, axis=-1, keepdims=True)
    centre = values - mean
    spread = jnp.mean(centre * centre, axis=-1, keepdims=True)
    scale = lax.rsqrt(spread + eps_norm)
    return centre * scale, scale


def norm_back(unit, scale, gain, grad):
    inner = grad * gain
    first = jnp.mean(inner, axis=-1, keepdims=True)
    second = jnp.mean(inner * unit, axis=-1, keepdims=True)
    return scale * (inner - first - unit * second)


def column(values):
    return jnp.sum(values, axis=0, keepdims=True)


def gelu_both(values):
    root = 2 * 0.7978845608028654
    cubic = root * 0.044715
    turn = -1.4426950408889634
    square = values * values
    power = jnp.exp2(jnp.minimum(values * (turn * root + (turn * cubic) * square), 126.0))
    part = pl.reciprocal(1.0 + power, approx=True)
    hidden = values * part
    return hidden, part + (hidden - hidden * part) * (root + (3 * cubic) * square)


def flip(value, bit):
    return 1 - value if bit else value


def parts_copies(place_ref, part_refs, weight, sems, start, size, into, chunk):
    copies = []
    for at, (dx, dc, dy) in enumerate(NEAR):
        spot = (slice(None), flip(place_ref[1], dx), flip(place_ref[2], dc), flip(place_ref[3], dy))
        copies.append(
            pltpu.make_async_copy(
                part_refs[at].at[:, :, pl.ds(start, size)],
                weight.at[spot + (slice(None), pl.ds(into, size))],
                sems.at[chunk, at],
            )
        )
    return copies


def weight_scratch(part, columns):
    depth, rows, _ = part.shape
    return pltpu.VMEM((depth, 2, 2, 2, rows, columns), BF16)


def flat(value):
    return value.reshape(-1, value.shape[-1])


def depth_copies(place_ref, part_refs, weight, sems):
    depth = weight.shape[0]
    copies = []
    for step in range(depth):
        there = lax.rem(place_ref[0] + depth - step, depth)
        for dc in range(2):
            core = flip(place_ref[2], dc)
            copies.append(
                pltpu.make_async_copy(
                    part_refs[2 * step + dc], weight.at[there, :, core], sems.at[there, dc]
                )
            )
    return copies


def depth_wait(place_ref, part_refs, weight, sems, at):
    for dc in range(2):
        core = flip(place_ref[2], dc)
        pltpu.make_async_copy(part_refs[dc], weight.at[at, :, core], sems.at[at, dc]).wait()


def own_spec(step, width, parts):
    return pl.BlockSpec((1, step, width), lambda i, p: (p[3], jnp.minimum(i, parts - 1), 0))


def far_spec(step, width, parts):
    return pl.BlockSpec((step, width), lambda i, _: (jnp.maximum(i - parts, 0), 0))


def join(place, blocks, moves, shapes, name):
    def body(place_ref, *refs):
        ins, outs = refs[: len(blocks)], refs[len(blocks) :]
        for i, cut, j, spot in moves:
            outs[j][spot(place_ref)] = ins[i][cut]

    return call(
        body,
        name,
        (1,),
        [held(*block.shape) for block in blocks],
        [held(*shape) for shape in shapes],
        [shape_of(BF16, *shape) for shape in shapes],
        (place,) + tuple(blocks),
        vmem=10,
    )


def join_beside(place, blocks):
    rows = blocks[0].shape[0]
    widths = [block.shape[1] for block in blocks]

    def body(place_ref, *refs):
        start = 0
        for ref, width in zip(refs, widths):
            refs[-1][:, start : start + width] = ref[...]
            start += width

    return call(
        body,
        "join_beside",
        (1,),
        [held(*block.shape) for block in blocks],
        held(rows, sum(widths)),
        shape_of(BF16, rows, sum(widths)),
        (place,) + tuple(blocks),
        vmem=4,
    )


def join_low(place, grad_out, far):
    half, width = far.shape

    def body(place_ref, own_ref, far_ref, low_ref, sum_ref):
        low = own_ref[0].astype(BF16)
        low_ref[:half] = low
        low_ref[half:] = far_ref[...]
        sum_ref[...] = column(low.astype(F32)) + column(far_ref[...].astype(F32))

    return call(
        body,
        "join_low",
        (1,),
        [
            pl.BlockSpec((1, half, width), lambda i, p: (p[3], 0, 0), pipeline_mode=pl.Buffered(1)),
            held(half, width),
        ],
        [held(2 * half, width), held(1, width)],
        [shape_of(BF16, 2 * half, width), shape_of(F32, 1, width)],
        (place, grad_out, far),
        vmem=12,
    )


def cast_far(place, values):
    _, half, width = values.shape
    step = half // 2

    def body(place_ref, values_ref, out_ref):
        out_ref[...] = values_ref[0].astype(BF16)

    return call(
        body,
        "cast_far",
        (half // step,),
        [pl.BlockSpec((1, step, width), lambda i, p: (1 - p[3], i, 0))],
        pl.BlockSpec((step, width), lambda i, _: (i, 0)),
        shape_of(BF16, half, width),
        (place, values),
        vmem=6,
    )


class Transfers:
    def __init__(self, sems):
        self.sems, self.count = sems, 0

    def start(self, source, target):
        copy = pltpu.make_async_copy(source, target, self.sems.at[self.count])
        self.count += 1
        copy.start()
        return copy


def wait_all(copies):
    for copy in copies:
        copy.wait()


def start_parts(moves, place_ref, part_refs, weight, start, size, into):
    copies = []
    for part_ref, (dx, dc, dy) in zip(part_refs, NEAR):
        x, c, y = flip(place_ref[1], dx), flip(place_ref[2], dc), flip(place_ref[3], dy)
        copies.append(
            moves.start(
                part_ref.at[:, :, pl.ds(start, size)],
                weight.at[:, x, c, y, :, pl.ds(into, size)],
            )
        )
    return copies


def start_rows(moves, place_ref, whole_in, far_in, own, far, cuts):
    half = own.shape[0]
    copies = []
    for cut in cuts:
        if cut.start < half:
            copies.append(moves.start(whole_in.at[place_ref[3], cut], own.at[cut]))
        else:
            back = pl.ds(cut.start - half, cut.size)
            copies.append(moves.start(far_in.at[back], far.at[back]))
    return copies


def rows_at(own, far, cut):
    half = own.shape[0]
    if cut.start < half:
        return own[cut]
    return far[pl.ds(cut.start - half, cut.size)].astype(F32)


def row_cuts(tokens, step):
    return [pl.ds(start, step) for start in range(0, tokens, step)]


def norm_project(place, inputs, far, gain, shift, left, right, bias):
    half, width = far.shape
    tokens = 2 * half
    columns = bias.shape[1]
    step = 512
    left_steps = left[0].shape[-1] // step
    steps = columns // step
    cuts = row_cuts(tokens, 256)

    def body(place_ref, gain_ref, shift_ref, bias_ref, inputs_in, far_in, *refs):
        left_refs, right_refs = refs[:8], refs[8:16]
        normed_out, out_ref, own, far_rows, normed, weight, result, sems = refs[16:]
        moves = Transfers(sems)

        def weights(chunk):
            refs, start = (left_refs, chunk) if chunk < left_steps else (right_refs, chunk - left_steps)
            return start_parts(moves, place_ref, refs, weight, start * step, step, chunk * step)

        rows = start_rows(moves, place_ref, inputs_in, far_in, own, far_rows, cuts)
        parts = [weights(chunk) for chunk in range(steps)]
        away = []
        wait_all(rows)
        for chunk in range(steps):
            span = pl.ds(chunk * step, step)
            wait_all(parts[chunk])
            part = flat(weight[:, :, :, :, :, span])
            for cut in cuts:
                if chunk == 0:
                    unit, _ = norm_parts(rows_at(own, far_rows, cut))
                    low = (unit * gain_ref[...] + shift_ref[...]).astype(BF16)
                    normed[cut] = low
                else:
                    low = normed[cut]
                value = contract(low, part, 1, 0) + bias_ref[:, span]
                result[chunk, cut] = value.astype(BF16)
            if chunk == 0:
                away.append(moves.start(normed, normed_out))
            away.append(moves.start(result.at[chunk], out_ref.at[:, span]))
        wait_all(away)

    return call(
        body,
        "norm_project",
        (1,),
        [held(1, width), held(1, width), held(1, columns)] + [whole_ref()] * 18,
        [whole_ref(), whole_ref()],
        [shape_of(BF16, tokens, width), shape_of(BF16, tokens, columns)],
        (place, gain, shift, bias, inputs, far) + tuple(left) + tuple(right),
        scratch=[
            pltpu.VMEM((half, width), F32),
            pltpu.VMEM((half, width), BF16),
            pltpu.VMEM((tokens, width), BF16),
            weight_scratch(left[0], columns),
            pltpu.VMEM((steps, tokens, step), BF16),
            pltpu.SemaphoreType.DMA((2 * len(cuts) + 9 * steps,)),
        ],
        vmem=56,
    )


def out_norm(place, mixed, up_parts, at_out, bias, inputs, far, gain, shift):
    half, width = far.shape
    tokens = 2 * half
    cuts = row_cuts(tokens, 256)

    def body(place_ref, bias_ref, gain_ref, shift_ref, mixed_in, inputs_in, far_in, *refs):
        part_refs = refs[:8]
        middle_out, normed_out, mixed_rows, own, far_rows, middle, normed, weight, sems = refs[8:]
        moves = Transfers(sems)
        parts = start_parts(moves, place_ref, part_refs, weight, at_out, width, 0)
        mixes = [moves.start(mixed_in.at[cut], mixed_rows.at[cut]) for cut in cuts]
        rows = start_rows(moves, place_ref, inputs_in, far_in, own, far_rows, cuts)
        wait_all(parts)
        away = []
        for at, cut in enumerate(cuts):
            mixes[at].wait()
            product = contract(mixed_rows[cut], flat(weight[...]), 1, 0) + bias_ref[...]
            rows[at].wait()
            value = rows_at(own, far_rows, cut) + product
            middle[cut] = value
            away.append(moves.start(middle.at[cut], middle_out.at[cut]))
            unit, _ = norm_parts(value)
            normed[cut] = (unit * gain_ref[...] + shift_ref[...]).astype(BF16)
            away.append(moves.start(normed.at[cut], normed_out.at[cut]))
        wait_all(away)

    return call(
        body,
        "out_norm",
        (1,),
        [held(1, width)] * 3 + [whole_ref()] * 11,
        [whole_ref(), whole_ref()],
        [shape_of(F32, tokens, width), shape_of(BF16, tokens, width)],
        (place, bias, gain, shift, mixed, inputs, far) + tuple(up_parts),
        scratch=[
            pltpu.VMEM((tokens, width), BF16),
            pltpu.VMEM((half, width), F32),
            pltpu.VMEM((half, width), BF16),
            pltpu.VMEM((tokens, width), F32),
            pltpu.VMEM((tokens, width), BF16),
            weight_scratch(up_parts[0], width),
            pltpu.SemaphoreType.DMA((8 + 4 * len(cuts),)),
        ],
        vmem=56,
    )


def fill_far(place, partial, base, delta):
    _, half, width = base.shape
    step = 256

    def body(place_ref, partial_ref, base_ref, delta_ref, out_ref):
        out_ref[0] = base_ref[0] + delta_ref[...].astype(F32)

    there = pl.BlockSpec((1, step, width), lambda i, p: (1 - p[3], i, 0))
    return call(
        body,
        "fill_far",
        (half // step,),
        [whole_ref(), there, pl.BlockSpec((step, width), lambda i, _: (i, 0))],
        there,
        shape_of(F32, 2, half, width),
        (place, partial, base, delta),
        alias={1: 0},
        vmem=8,
    )


def grad_wide(place, left, rights, rows, span, pieces=1):
    tokens, tall = left.shape
    width = rights[0].shape[1]
    step = 512
    each = width // step
    first, stop = span
    steps = stop - first
    per = steps // pieces
    group = 4 * rows
    used = sorted({at // each for at in range(first, stop)})

    def body(place_ref, left_ref, *refs):
        right_refs = refs[: len(used)]
        outs, sums = refs[len(used) : -1], refs[-1]
        at = pl.program_id(0)
        for which, right_ref in zip(used, right_refs):
            @pl.when((at + first) // each == which)
            def _():
                result = contract(left_ref[...], right_ref[...], 0, 0).astype(BF16)
                sums[...] = result.reshape(tall // group, 2, group // 2, step)

        for piece in range(pieces):
            @pl.when(at // per == piece)
            def _():
                outs[2 * piece][...] = sums[:, place_ref[2]]
                outs[2 * piece + 1][...] = sums[:, 1 - place_ref[2]]

    def right_at(which):
        low, high = max(first - which * each, 0), min(stop - which * each, each) - 1
        return lambda i, _: (0, jnp.clip(i + first - which * each, low, high))

    def out_at(piece):
        return lambda i, _: (0, 0, jnp.clip(i - piece * per, 0, per - 1))

    return call(
        body,
        "grad_wide",
        (steps,),
        [held(tokens, tall)] + [pl.BlockSpec((tokens, step), right_at(which)) for which in used],
        [
            pl.BlockSpec((tall // group, group // 2, step), out_at(piece))
            for piece in range(pieces)
            for _ in range(2)
        ],
        [shape_of(BF16, tall // group, group // 2, per * step)] * (2 * pieces),
        (place, left) + tuple(rights[which] for which in used),
        scratch=[pltpu.VMEM((tall // group, 2, group // 2, step), BF16)],
        vmem=20,
    )


def feed_forward(place, first, count, depth, normed, grad_low, up_parts, down_parts, up_bias, down_bias, far, state, wide):
    tokens, width = normed.shape
    half = tokens // 2
    hidden_width = up_bias.shape[1]
    step = hidden_width // (2 * depth)
    steps = 2 * count
    rows = down_parts[0].shape[-2]
    group = width // (2 * depth)
    last = first + count == depth
    columns, offset, before = wide
    offset = offset // step
    lines = up_parts[0].shape[1]
    beside = (up_parts[0].shape[-1] - hidden_width) // width
    rows = rows + beside * lines

    def body(place_ref, bias_ref, down_ref, normed_in, grad_in, far_in, out_in, back_in, *refs):
        up_refs, down_refs = refs[:8], refs[8 : 8 + 2 * depth]
        refs = refs[8 + 2 * depth + len(before) :]
        tall_mine, tall_other, wide_mine, wide_other, sum_ref, back_out = refs[:6]
        outs = refs[6:8] if last else refs[6:7]
        refs = refs[6 + len(outs) :]
        normed_ref, grad_ref, far_ref, total, back, delta = refs[:6]
        up, down, up_sems, down_sems, beside_sems, state_sems, tall_sums, wide_sums = refs[6:]
        at = pl.program_id(0)
        slot = lax.rem(at, 2)

        def up_copies(index, into):
            start = pl.multiple_of((2 * first + index) * step, step)
            copies = []
            for which, (dx, dc, dy) in enumerate(NEAR):
                x, c, y = flip(place_ref[1], dx), flip(place_ref[2], dc), flip(place_ref[3], dy)
                copies.append(
                    pltpu.make_async_copy(
                        up_refs[which].at[:, :, pl.ds(start, step)],
                        up.at[into, :, x, c, y],
                        up_sems.at[into, which],
                    )
                )
            return copies

        def down_copies(index, into, turn):
            x = lax.rem(index, 2)
            return [
                pltpu.make_async_copy(
                    down_refs[2 * turn + dc].at[x],
                    down.at[into, flip(place_ref[2], dc), :, pl.ds(0, rows - beside * lines)],
                    down_sems.at[into, dc],
                )
                for dc in range(2)
            ]

        def beside_copies(index, into, dx):
            copies = []
            for dc in range(2):
                for dy in range(2):
                    which = NEAR.index((dx, dc, dy))
                    c, y = flip(place_ref[2], dc), flip(place_ref[3], dy)
                    for part in range(beside):
                        copies.append(
                            pltpu.make_async_copy(
                                up_refs[which].at[
                                    first + index // 2, :, pl.ds(hidden_width + part * width, width)
                                ],
                                down.at[into, c, y, pl.ds(rows - (beside - part) * lines, lines)],
                                beside_sems.at[into, len(copies)],
                            )
                        )
            return copies

        def begin(index, into):
            for copy in up_copies(index, into):
                copy.start()
            away = lax.rem(place_ref[0] + depth - first - index // 2, depth)
            for turn in range(depth):
                @pl.when(away == turn)
                def _():
                    for copy in down_copies(index, into, turn):
                        copy.start()
            for dx in range(2):
                @pl.when(flip(place_ref[1], dx) == lax.rem(index, 2))
                def _():
                    for copy in beside_copies(index, into, dx):
                        copy.start()

        normed_copy = pltpu.make_async_copy(normed_in, normed_ref, state_sems.at[0])
        grad_copy = pltpu.make_async_copy(grad_in, grad_ref, state_sems.at[1])
        out_copy = pltpu.make_async_copy(out_in, total, state_sems.at[2])
        if first:
            back_copy = pltpu.make_async_copy(back_in, back, state_sems.at[3])
        back_away = pltpu.make_async_copy(back, back_out, state_sems.at[5])
        if last:
            far_copy = pltpu.make_async_copy(far_in, far_ref, state_sems.at[4])
            away = [
                pltpu.make_async_copy(
                    total.at[pl.ds(0, half)], outs[0].at[place_ref[3]], state_sems.at[6]
                ),
                pltpu.make_async_copy(delta, outs[1], state_sems.at[7]),
            ]
        else:
            away = [pltpu.make_async_copy(total, outs[0], state_sems.at[6])]

        @pl.when(at == 0)
        def _():
            normed_copy.start()
            begin(0, 0)
            grad_copy.start()
            out_copy.start()
            if first:
                back_copy.start()
            else:
                back[...] = jnp.zeros((tokens, width), F32)
            if last:
                far_copy.start()
            normed_copy.wait()

        @pl.when(at + 1 < steps)
        def _():
            begin(at + 1, 1 - slot)

        for copy in up_copies(at, slot):
            copy.wait()
        up_part = flat(up[slot])
        before_gelu = contract(normed_ref[...], up_part, 1, 0) + bias_ref[...]
        hidden, slope = gelu_both(before_gelu)
        hidden = hidden.astype(BF16)

        @pl.when(at == 0)
        def _():
            grad_copy.wait()

        tall = contract(hidden, grad_ref[...], 0, 0).astype(BF16)
        tall_sums[...] = tall.reshape(tall_sums.shape)
        tall_mine[0] = tall_sums[place_ref[2]]
        tall_other[0] = tall_sums[1 - place_ref[2]]

        for copy in down_copies(at, slot, 0) + beside_copies(at, slot, 0):
            copy.wait()

        @pl.when(at == 0)
        def _():
            out_copy.wait()
            if first:
                back_copy.wait()
            if last:
                far_copy.wait()

        down_part = flat(down[slot])
        total[...] += contract(hidden, down_part, 1, 0)

        @pl.when(at == steps - 1)
        def _():
            if last:
                total[...] += down_ref[...]
                delta[...] = (total[half:] - far_ref[...].astype(F32)).astype(BF16)
            for copy in away:
                copy.start()

        low = (contract(grad_ref[...], down_part, 1, 1) * slope).astype(BF16)
        back[...] += contract(low, up_part, 1, 1)

        @pl.when(at == steps - 1)
        def _():
            back_away.start()

        sum_ref[...] = column(low.astype(F32))
        broad = contract(normed_ref[...], low, 0, 0).astype(BF16)
        wide_sums[...] = broad.reshape(wide_sums.shape)
        wide_mine[...] = wide_sums[:, place_ref[2]]
        wide_other[...] = wide_sums[:, 1 - place_ref[2]]

        @pl.when(at == steps - 1)
        def _():
            for copy in away + [back_away]:
                copy.wait()

    tall_spec = pl.BlockSpec((1, 2 * rows, width), lambda i, _: (i, 0, 0))
    broad_spec = pl.BlockSpec((2 * depth, group // 2, step), lambda i, _: (0, 0, offset + i))
    sum_spec = pl.BlockSpec((1, step), lambda i, _: (0, i))
    out_specs = [tall_spec, tall_spec, broad_spec, broad_spec, sum_spec, whole_ref()]
    out_shape = [shape_of(BF16, steps, 2 * rows, width)] * 2
    out_shape += [shape_of(BF16, 2 * depth, group // 2, columns)] * 2
    out_shape += [shape_of(F32, 1, steps * step), shape_of(F32, tokens, width)]
    if last:
        out_specs += [whole_ref()] * 2
        out_shape += [shape_of(F32, 2, half, width), shape_of(BF16, half, width)]
    else:
        out_specs += [whole_ref()]
        out_shape += [shape_of(F32, tokens, width)]
    scratch = [
        pltpu.VMEM((tokens, width), BF16),
        pltpu.VMEM((tokens, width), BF16),
        pltpu.VMEM((half, width), BF16),
        pltpu.VMEM((tokens, width), F32),
        pltpu.VMEM((tokens, width), F32),
        pltpu.VMEM((half, width), BF16),
        pltpu.VMEM((2, depth, 2, 2, 2, group // 4, step), BF16),
        pltpu.VMEM((2, 2, 2, rows, width), BF16),
        pltpu.SemaphoreType.DMA((2, 8)),
        pltpu.SemaphoreType.DMA((2, 2)),
        pltpu.SemaphoreType.DMA((2, 4 * beside)),
        pltpu.SemaphoreType.DMA((8,)),
        pltpu.VMEM((2, 2 * rows, width), BF16),
        pltpu.VMEM((2 * depth, 2, group // 2, step), BF16),
    ]
    args = (place, up_bias, down_bias, normed, grad_low, far) + tuple(state) + tuple(up_parts) + tuple(down_parts)
    alias = {len(args) + i: 2 + i for i in range(len(before))}
    return call(
        body,
        "feed_forward",
        (steps,),
        [pl.BlockSpec((1, step), lambda i, _: (0, 2 * first + i)), held(1, width)]
        + [whole_ref()] * (5 + 8 + 2 * depth + len(before)),
        out_specs,
        out_shape,
        args + tuple(before),
        scratch=scratch,
        vmem=46,
        alias=alias,
    )


def middle_back(place, grad_normed, middle, gain, grad_out, far, up_parts, at_out):
    half, width = far.shape
    tokens = 2 * half
    cuts = row_cuts(tokens, 256)

    def body(place_ref, gain_ref, grad_in, middle_in, grad_out_in, far_in, *refs):
        part_refs = refs[:8]
        total_out, low_out, mixed_out = refs[8:11]
        sum_refs = refs[11:14]
        grads, middles, own, far_rows, total, low, mixed, weight, sems = refs[14:]
        moves = Transfers(sems)
        pairs = []
        for at, cut in enumerate(cuts):
            pairs.append(
                [
                    moves.start(grad_in.at[cut], grads.at[cut]),
                    moves.start(middle_in.at[cut], middles.at[cut]),
                ]
                + start_rows(moves, place_ref, grad_out_in, far_in, own, far_rows, [cut])
            )
            if at == 0:
                parts = start_parts(moves, place_ref, part_refs, weight, at_out, width, 0)
        sums = [jnp.zeros((1, width), F32) for _ in range(3)]
        away = []
        for at, cut in enumerate(cuts):
            wait_all(pairs[at])
            grad = grads[cut]
            unit, scale = norm_parts(middles[cut])
            value = rows_at(own, far_rows, cut) + norm_back(unit, scale, gain_ref[...], grad)
            total[cut] = value
            away.append(moves.start(total.at[cut], total_out.at[cut]))
            value_low = value.astype(BF16)
            low[cut] = value_low
            away.append(moves.start(low.at[cut], low_out.at[cut]))
            sums[0] += column(grad * unit)
            sums[1] += column(grad)
            sums[2] += column(value_low.astype(F32))
            if at == 0:
                wait_all(parts)
            mixed[cut] = contract(value_low, flat(weight[...]), 1, 1).astype(BF16)
            away.append(moves.start(mixed.at[cut], mixed_out.at[cut]))
        for ref, value in zip(sum_refs, sums):
            ref[...] = value
        wait_all(away)

    vector = held(1, width)
    return call(
        body,
        "middle_back",
        (1,),
        [vector] + [whole_ref()] * 12,
        [whole_ref()] * 3 + [vector] * 3,
        [shape_of(F32, tokens, width), shape_of(BF16, tokens, width), shape_of(BF16, tokens, width)]
        + [shape_of(F32, 1, width)] * 3,
        (place, gain, grad_normed, middle, grad_out, far) + tuple(up_parts),
        scratch=[
            pltpu.VMEM((tokens, width), F32),
            pltpu.VMEM((tokens, width), F32),
            pltpu.VMEM((half, width), F32),
            pltpu.VMEM((half, width), BF16),
            pltpu.VMEM((tokens, width), F32),
            pltpu.VMEM((tokens, width), BF16),
            pltpu.VMEM((tokens, width), BF16),
            weight_scratch(up_parts[0], width),
            pltpu.SemaphoreType.DMA((8 + 6 * len(cuts),)),
        ],
        vmem=56,
    )


def input_back(place, grads, left, right, inputs, far, gain, middle_grad, far_grad):
    half, width = far.shape
    tokens = 2 * half
    split = left[0].shape[-1]
    cuts = row_cuts(tokens, 256)

    def body(place_ref, gain_ref, query_in, key_in, value_in, inputs_in, far_in, middle_in, far_grad_in, *refs):
        left_refs, right_refs = refs[:8], refs[8:16]
        out_ref, delta_out = refs[16:18]
        sum_refs = refs[18:22]
        query, key, value, own, far_rows, middle, far_grads, result, delta, weight, sems = refs[22:]
        moves = Transfers(sems)
        first = start_parts(moves, place_ref, left_refs, weight, 0, split, 0)
        pairs, lates = [], []
        for at, cut in enumerate(cuts):
            pairs.append([moves.start(query_in.at[cut], query.at[cut]), moves.start(key_in.at[cut], key.at[cut])])
            late = [moves.start(value_in.at[cut], value.at[cut])]
            if at == 0:
                late += start_parts(moves, place_ref, right_refs, weight, 0, 3 * width - split, split)
            late += start_rows(moves, place_ref, inputs_in, far_in, own, far_rows, [cut])
            late.append(moves.start(middle_in.at[cut], middle.at[cut]))
            if cut.start >= half:
                back = pl.ds(cut.start - half, cut.size)
                late.append(moves.start(far_grad_in.at[back], far_grads.at[back]))
            lates.append(late)

        def part(chunk):
            return flat(weight[:, :, :, :, :, chunk * width : (chunk + 1) * width])

        sums = [jnp.zeros((1, width), F32) for _ in range(4)]
        away = []
        for at, cut in enumerate(cuts):
            wait_all(pairs[at])
            if at == 0:
                wait_all(first)
            grad = contract(query[cut], part(0), 1, 1) + contract(key[cut], part(1), 1, 1)
            wait_all(lates[at])
            grad += contract(value[cut], part(2), 1, 1)
            unit, scale = norm_parts(rows_at(own, far_rows, cut))
            sums[0] += column(grad * unit)
            sums[1] += column(grad)
            sums[2] += column(query[cut].astype(F32))
            sums[3] += column(value[cut].astype(F32))
            total = middle[cut] + norm_back(unit, scale, gain_ref[...], grad)
            if cut.start < half:
                result[cut] = total
                away.append(moves.start(result.at[cut], out_ref.at[place_ref[3], cut]))
            else:
                back = pl.ds(cut.start - half, cut.size)
                delta[back] = (total - far_grads[back].astype(F32)).astype(BF16)
                away.append(moves.start(delta.at[back], delta_out.at[back]))
        for ref, total in zip(sum_refs, sums):
            ref[...] = total
        wait_all(away)

    vector = held(1, width)
    return call(
        body,
        "input_back",
        (1,),
        [vector] + [whole_ref()] * 23,
        [whole_ref()] * 2 + [vector] * 4,
        [shape_of(F32, 2, half, width), shape_of(BF16, half, width)] + [shape_of(F32, 1, width)] * 4,
        (place, gain) + tuple(grads) + (inputs, far, middle_grad, far_grad) + tuple(left) + tuple(right),
        scratch=[pltpu.VMEM((tokens, width), BF16)] * 3
        + [
            pltpu.VMEM((half, width), F32),
            pltpu.VMEM((half, width), BF16),
            pltpu.VMEM((tokens, width), F32),
            pltpu.VMEM((half, width), BF16),
            pltpu.VMEM((half, width), F32),
            pltpu.VMEM((half, width), BF16),
            weight_scratch(left[0], 3 * width),
            pltpu.SemaphoreType.DMA((16 + 8 * len(cuts),)),
        ],
        vmem=34,
    )


def split_add(place, mine, came, spot):
    groups, _, rows, columns = mine.shape

    def body(place_ref, mine_ref, came_ref, sent_ref, kept_ref):
        for ref, at in ((sent_ref, 1 - place_ref[spot]), (kept_ref, place_ref[spot])):
            ref[0] = (mine_ref[0, at].astype(F32) + came_ref[0, at].astype(F32)).astype(BF16)

    block = pl.BlockSpec((1, 2, rows, columns), lambda i, _: (i, 0, 0, 0))
    out = pl.BlockSpec((1, rows, columns), lambda i, _: (i, 0, 0))
    return call(
        body,
        "split_add",
        (groups,),
        [block, block],
        [out, out],
        [shape_of(BF16, groups, rows, columns)] * 2,
        (place, mine, came),
        vmem=8,
    )


def split_depth(place, pairs, rows, vectors=None, sizes=()):
    depth = pairs[0][0].shape[0]
    layout = [(which, part) for which, (mine, _) in enumerate(pairs) for part in range(mine.shape[1] // rows)]
    total = sum(pairs[which][0].shape[2] for which, _ in layout)
    extra = () if vectors is None else (vectors,)
    wide = total + PAIR * len(extra)
    count = depth * 8

    def body(place_ref, *refs):
        outs = refs[2 * len(pairs) + len(extra) :]
        for step, ref in enumerate(outs):
            at = lax.rem(place_ref[0] + step, depth)
            start = 0
            for which, part in layout:
                width = pairs[which][0].shape[2]
                cut = pl.ds(part * rows, rows)
                value = refs[2 * which][at, cut].astype(F32) + refs[2 * which + 1][at, cut].astype(F32)
                ref[:, start : start + width] = value.astype(ref.dtype)
                start += width
            if extra:
                device = ((at * 2 + place_ref[1]) * 2 + place_ref[2]) * 2 + place_ref[3]
                line = lax.broadcasted_iota(jnp.int32, (rows, PAIR), 0)
                block = jnp.zeros((rows, PAIR), F32)
                base = 0
                for index, size in enumerate(sizes):
                    values = refs[2 * len(pairs)][pl.ds(base + device * size * rows // PAIR, 1), :]
                    block = jnp.where(line == index, values, block)
                    base += count * size * rows // PAIR
                ref[:, total:] = block.astype(ref.dtype)

    return call(
        body,
        "split_depth",
        (1,),
        [held(*mine.shape) for mine, _ in pairs for _ in range(2)] + [held(*value.shape) for value in extra],
        [held(rows, wide)] * depth,
        [shape_of(F32, rows, wide)] + [shape_of(BF16, rows, wide)] * (depth - 1),
        (place,) + tuple(value for pair in pairs for value in pair) + extra,
        vmem=12,
    )


def last_add(place, own, came, shapes, before):
    rows, total = own.shape
    layout = [(which, part) for which, shape in enumerate(shapes) for part in range(shape[0] // rows)]
    offsets = [before[which].shape[1] if which in before else 0 for which in range(len(shapes))]
    extra = sorted(before)

    def body(place_ref, own_ref, *refs):
        outs = refs[len(came) + len(extra) :]
        for which, ref in zip(extra, refs[len(came) :]):
            outs[which][:, : offsets[which]] = ref[...]
        start = 0
        for which, part in layout:
            width = shapes[which][1]
            value = own_ref[:, start : start + width]
            for ref in refs[: len(came)]:
                value = value + ref[:, start : start + width].astype(F32)
            first = offsets[which]
            outs[which][part * rows : (part + 1) * rows, first : first + width] = value
            start += width

    wholes = [(shape[0], shape[1] + offset) for shape, offset in zip(shapes, offsets)]
    return call(
        body,
        "last_add",
        (1,),
        [held(rows, total)] * (1 + len(came)) + [held(*before[which].shape) for which in extra],
        [held(*shape) for shape in wholes],
        [shape_of(F32, *shape) for shape in wholes],
        (place, own) + tuple(came) + tuple(before[which] for which in extra),
        vmem=12,
    )


def spread_rows(count, per, size, row):
    span = size * per
    lane = lax.broadcasted_iota(jnp.int32, (per, count * span), 1)
    line = lax.broadcasted_iota(jnp.int32, (per, count * span), 0)
    return jnp.where(lane % span == row * per + line, 1.0, 0.0)


def chosen_rows(count, span):
    lane = lax.broadcasted_iota(jnp.int32, (count, count * span), 1)
    line = lax.broadcasted_iota(jnp.int32, (count, count * span), 0)
    return lane // span == line


def small_vectors(place, right, start, sizes, per):
    depth, rows, _ = right[0].shape
    count = depth * 8

    def body(place_ref, *refs):
        part_refs, outs, held_rows = refs[:8], refs[8:-1], refs[-1]
        for at, (dx, dc, dy) in enumerate(NEAR):
            x, c, y = flip(place_ref[1], dx), flip(place_ref[2], dc), flip(place_ref[3], dy)
            held_rows[:, x, c, y] = part_refs[at][...].astype(F32)
        table = held_rows[...].reshape(count, rows, PAIR)
        at = 0
        for ref, size in zip(outs, sizes):
            chosen = chosen_rows(count, size * per)
            line = jnp.zeros((1, count * size * per), F32)
            for row in range(size):
                spread = spread_rows(count, per, size, row).astype(BF16)
                wide = contract(table[:, at + row, :per].astype(BF16), spread, 1, 0)
                line += column(jnp.where(chosen, wide, 0.0))
            at += size
            ref[...] = line

    return call(
        body,
        "small_vectors",
        (1,),
        [pl.BlockSpec((depth, rows, PAIR), lambda i, _: (0, 0, start // PAIR))] * 8,
        [held(1, count * size * per) for size in sizes],
        [shape_of(F32, 1, count * size * per) for size in sizes],
        (place,) + tuple(right),
        scratch=[pltpu.VMEM((depth, 2, 2, 2, rows, PAIR), F32)],
        vmem=12,
    )


def merge_add(place, mine, came, spot):
    counts = [part.shape[0] for part in mine]
    _, _, rows, columns = mine[0].shape

    def body(place_ref, *refs):
        sent_ref, kept_ref = refs[2 * len(mine) :]
        start = 0
        for which, count in enumerate(counts):
            for ref, at in ((sent_ref, 1 - place_ref[spot]), (kept_ref, place_ref[spot])):
                total = refs[which][:, at].astype(F32) + refs[len(mine) + which][:, at].astype(F32)
                ref[start : start + count] = total.astype(BF16)
            start += count

    shape = (sum(counts), rows, columns)
    return call(
        body,
        "merge_add",
        (1,),
        [held(*part.shape) for part in mine + came],
        [held(*shape)] * 2,
        [shape_of(BF16, *shape)] * 2,
        (place,) + tuple(mine) + tuple(came),
        vmem=12,
    )


def beside_add(place, mine, came, spot):
    groups, _, rows, _ = mine[0].shape
    widths = [part.shape[-1] for part in mine]

    def body(place_ref, *refs):
        sent_ref, kept_ref = refs[2 * len(mine) :]
        for ref, at in ((sent_ref, 1 - place_ref[spot]), (kept_ref, place_ref[spot])):
            start = 0
            for which, width in enumerate(widths):
                total = refs[which][:, at].astype(F32) + refs[len(mine) + which][:, at].astype(F32)
                ref[:, :, start : start + width] = total.astype(BF16)
                start += width

    shape = (groups, rows, sum(widths))
    return call(
        body,
        "beside_add",
        (1,),
        [held(*part.shape) for part in mine + came],
        [held(*shape)] * 2,
        [shape_of(BF16, *shape)] * 2,
        (place,) + tuple(mine) + tuple(came),
        vmem=12,
    )


def attn_forward_kernel(q_ref, k_ref, v_ref, bias_ref, prob_ref, mixed_ref, total_ref):
    tokens, lanes = q_ref.shape
    half = lanes // 2
    lane = lax.broadcasted_iota(jnp.int32, (tokens, lanes), 1)
    block = lax.broadcasted_iota(jnp.int32, (tokens, lanes), 0) // BLOCK
    scale = half ** -0.5
    q = q_ref[...].astype(jnp.float32) * scale
    k = k_ref[...].astype(jnp.float32)
    v = v_ref[...].astype(jnp.float32)
    sides = []
    for head in range(2):
        own = (lane >= half) if head else (lane < half)
        first = 0 if head else half
        bias = jnp.broadcast_to(bias_ref[head][:, None, :], (tokens // BLOCK, BLOCK, lanes)).reshape(tokens, lanes)
        q_ext = jnp.where(own, q, jnp.where(lane - first == block, 1.0, 0.0)).astype(jnp.bfloat16)
        k_ext = jnp.where(own, k, bias).astype(jnp.bfloat16)
        v_ext = jnp.where(own, v, 1.0).astype(jnp.bfloat16)
        sides.append((q_ext, k_ext, v_ext))
    rows = min(512, tokens)
    low_lane = lax.broadcasted_iota(jnp.int32, (rows, lanes), 1) < half
    for start in range(0, tokens, rows):
        sums = []
        for head, (q_ext, k_ext, v_ext) in enumerate(sides):
            scores = contract(q_ext[start:start + rows], k_ext, 1, 1)
            top = jnp.max(scores, axis=1, keepdims=True)
            prob = jnp.exp(scores - top).astype(jnp.bfloat16)
            prob_ref[head, start:start + rows, :] = prob
            sums.append(contract(prob, v_ext, 1, 0))
        result = jnp.where(low_lane, sums[0], sums[1])
        totals = pltpu.roll(jnp.where(low_lane, sums[1], sums[0]), half, 1)
        mixed_ref[start:start + rows, :] = (result / totals).astype(jnp.bfloat16)
        total_ref[start:start + rows, :] = totals

def attn_backward_kernel(q_ref, k_ref, v_ref, prob_ref, mixed_ref, total_ref, grad_ref, dq_ref, dk_ref, dv_ref):
    tokens, lanes = q_ref.shape
    half = lanes // 2
    scale = half ** -0.5
    lane = lax.broadcasted_iota(jnp.int32, (tokens, lanes), 1)
    grad = grad_ref[...].astype(jnp.float32) / total_ref[...]
    inner = grad * mixed_ref[...].astype(jnp.float32)
    grad_low = grad.astype(jnp.bfloat16)
    q_turned = q_ref[...].T
    grad_turned = grad_low.T
    v = v_ref[...].astype(jnp.float32)
    k = k_ref[...]
    rows = 256
    low_lane = lax.broadcasted_iota(jnp.int32, (rows, lanes), 1) < half
    dq = [[None, None] for _ in range(tokens // rows)]
    dk, dv = [], []
    for head in range(2):
        own = (lane >= half) if head else (lane < half)
        first = 0 if head else half
        minus = -jnp.sum(jnp.where(own, inner, 0.0), axis=1, keepdims=True)
        high = minus.astype(jnp.bfloat16).astype(jnp.float32)
        grad_ext = jnp.where(own, grad, jnp.where(lane == first, high, jnp.where(lane == first + 1, minus - high, 0.0))).astype(jnp.bfloat16)
        v_ext = jnp.where(own, v, jnp.where(lane - first < 2, 1.0, 0.0)).astype(jnp.bfloat16)
        dk_sum = dv_sum = None
        for index in range(tokens // rows):
            part = slice(index * rows, (index + 1) * rows)
            prob = prob_ref[head, part, :]
            spread = contract(grad_ext[part], v_ext, 1, 1)
            grad_scores = (prob.astype(jnp.float32) * spread).astype(jnp.bfloat16)
            dq[index][head] = contract(grad_scores, k, 1, 0)
            rows_of = slice(head * half, (head + 1) * half)
            dk_part = contract(q_turned[rows_of, part], grad_scores, 1, 0)
            dv_part = contract(grad_turned[rows_of, part], prob, 1, 0)
            dk_sum = dk_part if dk_sum is None else dk_sum + dk_part
            dv_sum = dv_part if dv_sum is None else dv_sum + dv_part
        dk.append(dk_sum)
        dv.append(dv_sum)
    for index, pair in enumerate(dq):
        dq_ref[index * rows:(index + 1) * rows, :] = (jnp.where(low_lane, pair[0], pair[1]) * scale).astype(jnp.bfloat16)
    dk_ref[...] = (jnp.concatenate(dk, axis=0) * scale).T.astype(jnp.bfloat16)
    dv_ref[...] = jnp.concatenate(dv, axis=0).T.astype(jnp.bfloat16)


def attn_forward(place, qkv, bias, first, count, before=()):
    tokens, width = qkv.shape[0], qkv.shape[1] // 3
    pairs = width // PAIR

    def at(part):
        return pl.BlockSpec((tokens, PAIR), lambda i, _: (0, part * pairs + first + i))

    def body(place_ref, *refs):
        attn_forward_kernel(*refs[:4], *refs[4 + len(before) :])

    return call(
        body,
        "attn_forward",
        (count,),
        [at(0), at(1), at(2), pl.BlockSpec((2, tokens // BLOCK, PAIR), lambda i, _: (first + i, 0, 0))]
        + [whole_ref()] * len(before),
        [pl.BlockSpec((2, tokens, tokens), lambda i, _: (first + i, 0, 0)), at(0), at(0)],
        [
            shape_of(BF16, 2 * pairs, tokens, tokens),
            shape_of(BF16, tokens, width),
            shape_of(F32, tokens, width),
        ],
        (place, qkv, qkv, qkv, bias) + tuple(before),
        vmem=56,
        alias={5 + i: i for i in range(len(before))},
    )


def attn_backward(place, qkv, prob, mixed, total, grad, first, count, before=()):
    tokens, width = qkv.shape[0], qkv.shape[1] // 3
    pairs = width // PAIR

    def at(part):
        return pl.BlockSpec((tokens, PAIR), lambda i, _: (0, part * pairs + first + i))

    def body(place_ref, *refs):
        attn_backward_kernel(*refs[:7], *refs[7 + len(before) :])

    return call(
        body,
        "attn_backward",
        (count,),
        [at(0), at(1), at(2), pl.BlockSpec((2, tokens, tokens), lambda i, _: (first + i, 0, 0))]
        + [at(0)] * 3
        + [whole_ref()] * len(before),
        [at(0)] * 3,
        [shape_of(BF16, tokens, width)] * 3,
        (place, qkv, qkv, qkv, prob, mixed, total, grad) + tuple(before),
        vmem=28,
        alias={8 + i: i for i in range(len(before))},
    )


def key_bias(random_ids, block_ids):
    heads, blocks, _ = random_ids.shape
    row, col = block_ids[:, None], block_ids[None, :]
    last = blocks - 1
    fixed = (row == 0) | (row == last) | (col == 0) | (col == last) | (jnp.abs(row - col) <= 1)
    drawn = jnp.any(random_ids[:, :, :, None] == block_ids, axis=2)
    bias = jnp.where(fixed[None] | drawn, 0.0, -1e30)
    bias = bias.transpose(0, 2, 1).reshape(heads // 2, 2, blocks, blocks)
    lanes = 128
    even = jnp.pad(bias[:, 0], ((0, 0), (0, 0), (lanes // 2, lanes // 2 - blocks)))
    odd = jnp.pad(bias[:, 1], ((0, 0), (0, 0), (0, lanes - blocks)))
    return jnp.stack([even, odd], axis=1).reshape(heads, blocks, lanes)


def pair_swap(value, axis, bit):
    size = lax.axis_size(axis)
    return lax.ppermute(value, axis, [(i, i ^ bit) for i in range(size)])


def pick(value, index, axis):
    return lax.dynamic_index_in_dim(value, index, axis, keepdims=False)


def swap_x(value):
    return pair_swap(value, "dp", 2)


def swap_core(value):
    return pair_swap(value, "dp", 1)


def swap_y(value):
    return pair_swap(value, "seq", 1)


def swap_xy(value):
    pairs = 2 * lax.axis_size("dp")
    return lax.ppermute(value, BOTH, [(i, i ^ 5) for i in range(pairs)])


def ring_z(value, step):
    size = lax.axis_size("dp")
    return lax.ppermute(value, "dp", [(i, (i + 4 * step) % size) for i in range(size)])


def tie(*values):
    return lax.optimization_barrier(values)


class Reduce:
    def __init__(self, place, rows, x_first):
        self.place, self.rows, self.x_first = place, rows, x_first

    def begin(self, mine, other):
        self.mine, self.came = mine, swap_core(other)

    def first(self):
        groups, tall, columns = self.mine.shape
        if self.x_first:
            shape = (groups // 2, 2, tall, columns)
        else:
            shape = (groups, 2, self.rows, columns)
        spot, swap = (1, swap_x) if self.x_first else (3, swap_y)
        sent, kept = split_add(self.place, self.mine.reshape(shape), self.came.reshape(shape), spot)
        self.mine, self.came = kept, swap(sent)

    def second(self, *others, beside=False):
        spot, swap = (3, swap_y) if self.x_first else (1, swap_x)
        mine, came = [], []
        for part in (self,) + others:
            shape = (-1, 2, self.rows, part.mine.shape[-1])
            mine.append(part.mine.reshape(shape))
            came.append(part.came.reshape(shape))
        if beside:
            sent, kept = beside_add(self.place, mine, came, spot)
        elif others:
            sent, kept = merge_add(self.place, mine, came, spot)
        else:
            sent, kept = split_add(self.place, mine[0], came[0], spot)
        self.mine, self.came = kept, swap(sent)

    def third(self, *others, vectors=None, sizes=()):
        parts = (self,) + others
        rows = min(part.rows for part in parts)
        pairs = [(part.mine, part.came) for part in parts]
        own, *sent = split_depth(self.place, pairs, rows, vectors, sizes)
        self.mine = own
        self.came = [ring_z(block, step + 1) for step, block in enumerate(sent)]

    def last(self, *shapes, before={}):
        return last_add(self.place, self.mine, self.came, shapes, before)

    def hold(self, *others):
        self.mine, self.came, others = tie(self.mine, self.came, others)
        return others


def split_depth_spot(place_ref, step, depth):
    return lax.rem(place_ref[0] + depth - step, depth)


def join_depth(place, blocks, cuts, name):
    depth = len(blocks)
    rows = blocks[0].shape[0]
    moves = []
    for step in range(depth):
        for j, (start, stop) in enumerate(cuts):
            cut = (slice(None), slice(start, stop))
            moves.append((step, cut, j, lambda p, step=step: split_depth_spot(p, step, depth)))
    return join(place, blocks, moves, [(depth, rows, stop - start) for start, stop in cuts], name)


def join_plane(place, blocks):
    moves = []
    for at, (dx, dy) in enumerate(((0, 0), (1, 0), (0, 1), (1, 1))):
        moves.append(
            (at, (), 0, lambda p, dx=dx, dy=dy: (flip(p[1], dx), flip(p[3], dy)))
        )
    return join(place, blocks, moves, [(2, 2) + blocks[0].shape], "join_plane")[0]


def near_parts(own, by_x, by_y, by_xy, cores):
    blocks = {(0, 0): own, (1, 0): by_x, (0, 1): by_y, (1, 1): by_xy}
    return [cores[dx, dy] if dc else blocks[dx, dy] for dx, dc, dy in NEAR]


def paired(inputs, grad_out, random_blocks, *shards):
    depth = lax.axis_size("dp") // 4
    dp, y = lax.axis_index("dp"), lax.axis_index("seq")
    z, x, c = dp // 4, (dp // 2) % 2, dp % 2
    spots = (z, x, c, y)
    place = jnp.stack(spots).astype(jnp.int32)
    w_query, w_key, w_value, w_out, w_up, w_down = shards[:6]
    vectors = shards[6:]
    half, width = inputs.shape[1:]
    rows, tall_rows, hidden_width = w_up.shape[0], w_down.shape[0], w_up.shape[1]
    pairs = width // PAIR
    ring = range(1, depth)

    sizes = [vector.shape[0] // rows for vector in vectors]
    small = jnp.concatenate([vector.reshape(-1, rows) for vector in vectors])
    small = jnp.pad(small, ((0, rows - small.shape[0]), (0, PAIR - rows)))
    shard = join_beside(place, [w_query, w_key, w_value, w_out, small])
    turned = [shard] + [ring_z(shard, step) for step in ring]
    tall_cut = tall_rows // 2
    down_near, down_own = w_down[tall_cut:], w_down[:tall_cut]
    down_x = swap_x(down_own)
    random_far = swap_y(pick(random_blocks, 1 - y, 0))
    random_far, far_rows = tie(random_far, cast_far(place, inputs))
    far_rows = swap_y(far_rows)
    up_shard = join_beside(
        place, [w_up] + [down_near[start : start + rows] for start in range(0, tall_cut, rows)]
    )
    at_out = width
    turned, down_x, far_rows, up_shard, down_own, random_far, grad_out = tie(
        turned, down_x, far_rows, up_shard, down_own, random_far, grad_out
    )
    cut = 2 * width
    left, right = join_depth(place, turned, [(0, cut), (cut, shard.shape[1])], "join_first")
    left_y, right_x = swap_y(left), swap_x(right)
    up_turned = {1: ring_z(up_shard, 1), depth - 1: ring_z(up_shard, depth - 1)}
    down_y, down_xy = swap_y(down_own), swap_y(down_x)
    far_grad_low = cast_far(place, grad_out)
    left_y, right_x, up_turned, down_own, down_x, down_y, down_xy, far_grad_low, random_far = tie(
        left_y, right_x, up_turned, down_own, down_x, down_y, down_xy, far_grad_low, random_far
    )
    left_x, left_xy = swap_x(left), swap_x(left_y)
    right_y, right_xy = swap_y(right), swap_y(right_x)
    for step in ring:
        if step not in up_turned:
            up_turned[step] = ring_z(up_shard, step)
    plane = join_plane(place, [down_own, down_x, down_y, down_xy])
    local_blocks = half // BLOCK
    ids = jnp.arange(2 * local_blocks, dtype=jnp.int32)
    block_ids = (ids + y * local_blocks) % (2 * local_blocks)
    random_ids = jnp.concatenate([pick(random_blocks, y, 0), random_far], axis=1)
    bias = key_bias(random_ids, block_ids)
    left_x, left_xy, right_y, right_xy, up_turned, left_y, right_x, plane, bias = tie(
        left_x, left_xy, right_y, right_xy, up_turned, left_y, right_x, plane, bias
    )
    (up_own,) = join_depth(
        place, [up_shard] + [up_turned[step] for step in ring], [(0, up_shard.shape[1])], "join_up"
    )
    up_own, left, left_x, left_y, left_xy, right, right_x, right_y, right_xy = tie(
        up_own, left, left_x, left_y, left_xy, right, right_x, right_y, right_xy
    )
    up_y, up_x = swap_y(up_own), swap_x(up_own)
    left_core = {
        (0, 0): swap_core(left), (0, 1): swap_core(left_y),
        (1, 0): swap_core(left_x), (1, 1): swap_core(left_xy),
    }
    right_core = {
        (0, 0): swap_core(right), (0, 1): swap_core(right_y),
        (1, 0): swap_core(right_x), (1, 1): swap_core(right_xy),
    }
    left_parts = near_parts(left, left_x, left_y, left_xy, left_core)
    right_parts = near_parts(right, right_x, right_y, right_xy, right_core)
    left_parts, right_parts, up_own = tie(left_parts, right_parts, up_own)

    planes = {0: plane, 1: ring_z(plane, 1), depth - 1: ring_z(plane, depth - 1)}
    spans = small_vectors(place, right_parts, cut, sizes, rows)
    (
        ln1_gain,
        ln1_bias,
        query_bias,
        value_bias,
        out_bias,
        ln2_gain,
        ln2_bias,
        up_bias,
        down_bias,
    ) = spans
    qkv_bias = jnp.concatenate([query_bias, jnp.zeros_like(query_bias), value_bias], axis=1)
    normed_low, qkv = norm_project(
        place, inputs, far_rows, ln1_gain, ln1_bias, left_parts, right_parts, qkv_bias
    )
    near_pairs = 3 * pairs // 8
    attended = attn_forward(place, qkv, bias, 0, near_pairs)
    attended, up_y, up_x, planes, far_grad_low = tie(attended, up_y, up_x, planes, far_grad_low)
    up_xy = swap_x(up_y)
    up_core = {(0, 0): swap_core(up_own), (0, 1): swap_core(up_y)}
    far_grad = swap_y(far_grad_low)
    for step in ring:
        if step not in planes:
            planes[step] = ring_z(planes[0], step)
    prob, mixed_low, totals = attn_forward(
        place, qkv, bias, near_pairs, pairs - near_pairs, attended
    )
    mixed_low, far_grad, up_core, up_x, planes = tie(mixed_low, far_grad, up_core, up_x, planes)
    up_core[1, 0] = swap_core(up_x)
    plane_core = {step: swap_core(planes[step]) for step in (0, 1, depth - 1)}
    grad_ff_low, grad_down_bias = join_low(place, grad_out, far_grad)
    mixed_low, grad_ff_low = tie(mixed_low, grad_ff_low)
    middle, normed_two_low = out_norm(
        place, mixed_low, right_parts, at_out, out_bias, inputs, far_rows, ln2_gain, ln2_bias
    )
    normed_two_low, up_xy, plane_core, up_core, planes = tie(
        normed_two_low, up_xy, plane_core, up_core, planes
    )
    up_core[1, 1] = swap_core(up_xy)
    for step in ring:
        if step not in plane_core:
            plane_core[step] = swap_core(planes[step])
    up_parts = near_parts(up_own, up_x, up_y, up_xy, up_core)
    down_parts = [part for step in range(depth) for part in (planes[step], plane_core[step])]

    down_sums = [Reduce(place, tall_rows, True) for _ in range(3)]
    near_sum = Reduce(place, rows, False)
    wide_sum = Reduce(place, rows, True)
    out_sum = Reduce(place, rows, True)
    left_sum = Reduce(place, rows, True)
    right_sum = Reduce(place, rows, False)

    def feed(first, count, state, wide):
        return feed_forward(
            place, first, count, depth, normed_two_low, grad_ff_low, up_parts, down_parts, up_bias,
            down_bias, far_rows, state, wide,
        )

    near = depth // 2
    near_width = hidden_width // 2
    each = hidden_width // depth
    mine, other, up_mine, up_other, bias_0, back, total = feed(
        0, near, (middle, middle), (near_width, 0, ())
    )
    down_sums[0].begin(mine, other)
    near_sum.begin(up_mine, up_other)
    mine, other, up_mine, up_other, bias_1, back, total = feed(
        near, depth - 1 - near, (total, back), (near_width, 0, ())
    )
    (back,) = down_sums[0].hold(back)
    (back,) = near_sum.hold(back)
    down_sums[1].begin(mine, other)
    down_sums[0].first()
    near_sum.first()
    down_sums[0].mine, near_sum.mine, back = tie(down_sums[0].mine, near_sum.mine, back)
    mine, other, up_mine, up_other, bias_2, back, out_part, out_delta = feed(
        depth - 1, 1, (total, back), (near_width, (depth - 1 - near) * each, (up_mine, up_other))
    )
    (back,) = down_sums[0].hold(back)
    (back,) = near_sum.hold(back)
    (back,) = down_sums[1].hold(back)
    down_sums[2].begin(mine, other)
    wide_sum.begin(up_mine, up_other)
    down_sums[1].first()
    down_sums[1].mine, back = tie(down_sums[1].mine, back)
    grad_up_bias = jnp.concatenate([bias_0, bias_1, bias_2], axis=1)
    grad_middle, grad_attn_low, grad_mixed_low, grad_ln2_gain, grad_ln2_bias, grad_out_bias = middle_back(
        place, back, middle, ln2_gain, grad_out, far_grad, right_parts, at_out
    )
    out_sum.begin(*grad_wide(place, mixed_low, (grad_attn_low,), rows, (0, 2)))
    out_sum.mine, grad_mixed_low = tie(out_sum.mine, grad_mixed_low)
    (grad_mixed_low,) = down_sums[1].hold(grad_mixed_low)
    (grad_mixed_low,) = down_sums[2].hold(grad_mixed_low)
    (grad_mixed_low,) = wide_sum.hold(grad_mixed_low)
    down_sums[2].first()
    near_sum.second()
    down_sums[2].mine, near_sum.mine, grad_mixed_low, out_delta = tie(
        down_sums[2].mine, near_sum.mine, grad_mixed_low, out_delta
    )
    out_far = swap_y(out_delta)
    grads = attn_backward(place, qkv, prob, mixed_low, totals, grad_mixed_low, 0, pairs // 2)
    grads, out_far = tie(grads, out_far)
    (grads,) = near_sum.hold(grads)
    (grads,) = down_sums[2].hold(grads)
    (grads,) = out_sum.hold(grads)
    wide_sum.first()
    out_sum.first()
    near_sum.third()
    down_sums[0].second(*down_sums[1:])
    down_sum = down_sums[0]
    down_sum.mine, near_sum.mine, wide_sum.mine, out_sum.mine, grads = tie(
        down_sum.mine, near_sum.mine, wide_sum.mine, out_sum.mine, grads
    )
    grads = attn_backward(
        place, qkv, prob, mixed_low, totals, grad_mixed_low, pairs // 2, pairs - pairs // 2, grads
    )
    (grads,) = near_sum.hold(grads)
    (grads,) = wide_sum.hold(grads)
    (grads,) = down_sum.hold(grads)
    wide_sum.second()
    wide_sum.mine, grads = tie(wide_sum.mine, grads)
    wide = grad_wide(place, normed_low, grads, rows, (0, 6), 2)
    (wide,) = wide_sum.hold(wide)
    (wide,) = out_sum.hold(wide)
    out_sum.second()
    out_sum.mine, wide = tie(out_sum.mine, wide)
    left_sum.begin(*wide[:2])
    right_sum.begin(*wide[2:])
    (grad_up_near,) = near_sum.last((rows, near_width))
    left_sum.mine, grads, grad_up_near = tie(left_sum.mine, grads, grad_up_near)
    (grads,) = out_sum.hold(grads)
    (grads,) = left_sum.hold(grads)
    left_sum.first()
    (grads,) = right_sum.hold(grads)
    right_sum.first()
    down_sum.third(wide_sum, out_sum)
    left_sum.mine, right_sum.mine, down_sum.mine, grads = tie(
        left_sum.mine, right_sum.mine, down_sum.mine, grads
    )
    in_part, in_delta, grad_ln1_gain, grad_ln1_bias, grad_query_bias, grad_value_bias = input_back(
        place, grads, left_parts, right_parts, inputs, far_rows, ln1_gain, grad_middle, far_grad
    )
    (in_delta,) = left_sum.hold(in_delta)
    left_sum.second()
    (in_delta,) = right_sum.hold(in_delta)
    right_sum.second()
    left_sum.mine, right_sum.mine, in_delta, grad_ln1_gain = tie(
        left_sum.mine, right_sum.mine, in_delta, grad_ln1_gain
    )
    grad_vectors = (
        grad_ln1_gain,
        grad_ln1_bias,
        grad_query_bias,
        grad_value_bias,
        grad_out_bias,
        grad_ln2_gain,
        grad_ln2_bias,
        grad_up_bias,
        grad_down_bias,
    )
    packed = jnp.concatenate(grad_vectors, axis=1).reshape(-1, PAIR)
    packed = packed + swap_core(packed)
    packed = packed + swap_x(packed) + swap_y(packed) + swap_xy(packed)
    (in_delta,) = down_sum.hold(in_delta)
    (in_delta,) = left_sum.hold(in_delta)
    (in_delta,) = right_sum.hold(in_delta)
    packed, in_delta = tie(packed, in_delta)
    in_far = swap_y(in_delta)
    left_sum.third(right_sum, vectors=packed, sizes=sizes)
    left_sum.mine, out_far, down_sum.mine = tie(left_sum.mine, out_far, down_sum.mine)
    grad_w_down, grad_w_up, grad_w_out = down_sum.last(
        w_down.shape, (rows, near_width), w_out.shape, before={1: grad_up_near}
    )
    result = fill_far(place, out_part, inputs, out_far)
    result, in_far, grad_w_up = tie(result, in_far, grad_w_up)
    grad_in = fill_far(place, in_part, grad_out, in_far)
    left_sum.came, grad_in = tie(left_sum.came, grad_in)
    square = (rows, width)
    grad_w_query, grad_w_key, grad_w_value, packed = left_sum.last(
        square, square, square, (rows, PAIR)
    )
    packed = packed.reshape(-1)
    out_vectors = []
    for index, size in enumerate(sizes):
        count = size * rows
        lane = (dp * 2 + y) * count % PAIR
        out_vectors.append(lax.dynamic_slice_in_dim(packed, index * PAIR + lane, count))
    return (
        (result, grad_in, grad_w_query, grad_w_key, grad_w_value, grad_w_out, grad_w_up, grad_w_down)
        + tuple(out_vectors)
    )


def solution(mesh):
    tokens, table, matrix, vector = P("dp", "seq", None), P("dp", None, "seq", None), P(BOTH, None), P(BOTH)
    in_specs = (tokens, tokens, table) + (matrix,) * 6 + (vector,) * 9
    out_specs = (tokens, tokens) + (matrix,) * 6 + (vector,) * 9
    paired_fits = mesh.shape["seq"] == 2 and mesh.shape["dp"] % 4 == 0

    def body(inputs, *rest):
        whole = paired if paired_fits and inputs.shape[0] == 2 else on_device
        return whole(inputs, *rest)

    return jax.shard_map(
        body, mesh=mesh, in_specs=in_specs, out_specs=out_specs, check_vma=False
    )
```

```python
import jax
import jax.numpy as jnp
from jax import lax
from jax.experimental import pallas as pl
from jax.experimental.pallas import tpu as pltpu
from jax.sharding import PartitionSpec as P

HEADS = 16
BLOCK = 64
BOTH = ("dp", "seq")


eps_norm = 1e-05
neg_fill = -1e30


def layer_norm(values, norm_gain, norm_shift):
    centre = values - jnp.mean(values, axis=-1, keepdims=True)
    spread = jnp.mean(centre * centre, axis=-1, keepdims=True)
    return centre * lax.rsqrt(spread + eps_norm) * norm_gain + norm_shift


def gelu_tanh(values):
    return jax.nn.gelu(values, approximate=True)


def project(left, right):
    return jnp.dot(left, right, preferred_element_type=jnp.float32)


def project_back(grad_rows, weight):
    return lax.dot_general(
        grad_rows, weight, (((1,), (1,)), ((), ())), preferred_element_type=jnp.float32
    )


def weight_grad(left, grad_rows):
    return lax.dot_general(
        left, grad_rows, (((0,), (0,)), ((), ())), preferred_element_type=jnp.float32
    )


def column_sum(grad_rows):
    return jnp.sum(grad_rows, axis=0, dtype=jnp.float32)


def to_table(block_rows):
    block_count = block_rows.shape[0] // BLOCK
    head_dim = block_rows.shape[1] // HEADS
    shaped = block_rows.reshape(block_count, BLOCK, HEADS, head_dim)
    return shaped.transpose(2, 0, 1, 3).reshape(HEADS, block_count, BLOCK * head_dim)


def from_table(table):
    block_count = table.shape[1]
    head_dim = table.shape[2] // BLOCK
    shaped = table.reshape(HEADS, block_count, BLOCK, head_dim)
    return shaped.transpose(1, 2, 0, 3).reshape(block_count * BLOCK, HEADS * head_dim)


def key_layout(first_block, local_blocks, all_blocks, random_ids):
    query_ids = first_block + jnp.arange(local_blocks, dtype=jnp.int32)
    window = jnp.stack([query_ids - 1, query_ids, query_ids + 1], axis=1)
    inside = (window >= 1) & (window <= all_blocks - 2)
    window = jnp.clip(window, 0, all_blocks - 1)
    end_blocks = jnp.broadcast_to(jnp.array([0, all_blocks - 1], jnp.int32), (local_blocks, 2))
    fixed_slots = jnp.concatenate([end_blocks, window], axis=1)
    key_slots = jnp.concatenate(
        [jnp.broadcast_to(fixed_slots[None], (HEADS, local_blocks, 5)), random_ids], axis=2
    )
    key_valid = jnp.concatenate(
        [
            jnp.ones((local_blocks, 2), jnp.bool_),
            inside,
            jnp.ones((local_blocks, random_ids.shape[2]), jnp.bool_),
        ],
        axis=1,
    )
    return (key_slots, jnp.repeat(key_valid, BLOCK, axis=1))


def pick_blocks(table, key_slots):
    head_index = jnp.arange(HEADS)[:, None, None]
    picked = table[head_index, key_slots]
    head_dim = table.shape[2] // BLOCK
    return picked.reshape(HEADS, key_slots.shape[1], key_slots.shape[2] * BLOCK, head_dim)


def sparse_scores(query_heads, key_picked, key_valid, score_scale):
    raw_scores = jnp.einsum(
        "hqid,hqkd->hqik", query_heads, key_picked, preferred_element_type=jnp.float32
    )
    return jnp.where(key_valid[None, :, None, :], raw_scores * score_scale, neg_fill)


def dense_scores(query_block, key_flat, score_scale):
    return (
        jnp.einsum("hid,hkd->hik", query_block, key_flat, preferred_element_type=jnp.float32)
        * score_scale
    )


def dense_forward(query_block, key_flat, value_flat, score_scale):
    scores = dense_scores(query_block, key_flat, score_scale)
    top_score = jnp.max(scores, axis=-1, keepdims=True)
    expos = jnp.exp(scores - top_score)
    totals = jnp.sum(expos, axis=-1, keepdims=True)
    attn_prob = (expos / totals).astype(jnp.bfloat16)
    result = jnp.einsum("hik,hkd->ihd", attn_prob, value_flat, preferred_element_type=jnp.float32)
    return (result, (top_score + jnp.log(totals))[..., 0])


def softmax_back(attn_prob, grad_prob, score_scale):
    inner = jnp.sum(attn_prob * grad_prob, axis=-1, keepdims=True)
    return (attn_prob * (grad_prob - inner) * score_scale).astype(jnp.bfloat16)


def dense_backward(query_block, key_flat, value_flat, grad_block, log_total, score_scale):
    attn_prob = jnp.exp(dense_scores(query_block, key_flat, score_scale) - log_total[..., None])
    grad_prob = jnp.einsum(
        "ihd,hkd->hik", grad_block, value_flat, preferred_element_type=jnp.float32
    )
    grad_value = jnp.einsum(
        "hik,ihd->hkd",
        attn_prob.astype(jnp.bfloat16),
        grad_block,
        preferred_element_type=jnp.float32,
    )
    grad_scores = softmax_back(attn_prob, grad_prob, score_scale)
    grad_query = jnp.einsum(
        "hik,hkd->ihd", grad_scores, key_flat, preferred_element_type=jnp.float32
    )
    grad_key = jnp.einsum(
        "hik,hid->hkd", grad_scores, query_block, preferred_element_type=jnp.float32
    )
    return (grad_query, grad_key, grad_value)


def run_forward(weights, in_rows, random_ids):
    (
        w_query,
        w_key,
        w_value,
        w_out,
        w_up,
        w_down,
        ln1_gain,
        ln1_bias,
        query_bias,
        value_bias,
        out_bias,
        ln2_gain,
        ln2_bias,
        up_bias,
        down_bias,
    ) = weights
    normed, pull_first = jax.vjp(
        layer_norm, in_rows, ln1_gain.astype(jnp.float32), ln1_bias.astype(jnp.float32)
    )
    normed_low = normed.astype(jnp.bfloat16)
    queries = (project(normed_low, w_query) + query_bias.astype(jnp.float32)).astype(jnp.bfloat16)
    key_rows = project(normed_low, w_key).astype(jnp.bfloat16)
    value_rows = (project(normed_low, w_value) + value_bias.astype(jnp.float32)).astype(
        jnp.bfloat16
    )
    key_all, value_all = (
        lax.all_gather(key_rows, "seq", axis=0, tiled=True),
        lax.all_gather(value_rows, "seq", axis=0, tiled=True),
    )
    place = lax.axis_index("seq")
    ranks = lax.axis_size("seq")
    local_blocks = in_rows.shape[0] // BLOCK
    all_blocks = key_all.shape[0] // BLOCK
    head_dim = queries.shape[1] // HEADS
    score_scale = head_dim ** (-0.5)
    key_slots, key_valid = key_layout(place * local_blocks, local_blocks, all_blocks, random_ids)
    key_table = to_table(key_all)
    value_table = to_table(value_all)
    key_picked = pick_blocks(key_table, key_slots)
    value_picked = pick_blocks(value_table, key_slots)
    query_heads = to_table(queries).reshape(HEADS, local_blocks, BLOCK, head_dim)
    scores = sparse_scores(query_heads, key_picked, key_valid, score_scale)
    top_score = jnp.max(scores, axis=-1, keepdims=True)
    expos = jnp.exp(scores - top_score)
    totals = jnp.sum(expos, axis=-1, keepdims=True)
    prob_low = (expos / totals).astype(jnp.bfloat16)
    log_sparse = (top_score + jnp.log(totals))[..., 0]
    sparse_out = jnp.einsum(
        "hqik,hqkd->qihd", prob_low, value_picked, preferred_element_type=jnp.float32
    )
    is_edge = (place == 0) | (place == ranks - 1)
    edge_slot = jnp.where(place == 0, 0, local_blocks - 1)
    key_flat = key_table.reshape(HEADS, all_blocks * BLOCK, head_dim)
    value_flat = value_table.reshape(HEADS, all_blocks * BLOCK, head_dim)
    query_edge = lax.dynamic_index_in_dim(query_heads, edge_slot, 1, keepdims=False)
    edge_out, log_edge = lax.cond(
        is_edge,
        lambda: dense_forward(query_edge, key_flat, value_flat, score_scale),
        lambda: (
            jnp.zeros((BLOCK, HEADS, head_dim), jnp.float32),
            jnp.zeros((HEADS, BLOCK), jnp.float32),
        ),
    )
    current = lax.dynamic_index_in_dim(sparse_out, edge_slot, 0, keepdims=False)
    mixed_heads = lax.dynamic_update_index_in_dim(
        sparse_out, jnp.where(is_edge, edge_out, current), edge_slot, 0
    )
    mixed_low = mixed_heads.reshape(in_rows.shape[0], queries.shape[1]).astype(jnp.bfloat16)
    middle = in_rows + (project(mixed_low, w_out) + out_bias.astype(jnp.float32))
    normed_two, pull_second = jax.vjp(
        layer_norm, middle, ln2_gain.astype(jnp.float32), ln2_bias.astype(jnp.float32)
    )
    normed_two_low = normed_two.astype(jnp.bfloat16)
    hidden_pre = project(normed_two_low, w_up) + up_bias.astype(jnp.float32)
    hidden, pull_gelu = jax.vjp(gelu_tanh, hidden_pre)
    hidden_low = hidden.astype(jnp.bfloat16)
    result = middle + (project(hidden_low, w_down) + down_bias.astype(jnp.float32))
    saved = {
        "pull_first": pull_first,
        "pull_second": pull_second,
        "pull_gelu": pull_gelu,
        "normed_low": normed_low,
        "normed_two_low": normed_two_low,
        "hidden_low": hidden_low,
        "mixed_low": mixed_low,
        "query_heads": query_heads,
        "query_edge": query_edge,
        "key_picked": key_picked,
        "value_picked": value_picked,
        "key_flat": key_flat,
        "value_flat": value_flat,
        "key_slots": key_slots,
        "key_valid": key_valid,
        "log_sparse": log_sparse,
        "log_edge": log_edge,
        "is_edge": is_edge,
        "edge_slot": edge_slot,
    }
    return (saved, result)


def run_backward(weights, saved, grad_rows):
    (
        w_query,
        w_key,
        w_value,
        w_out,
        w_up,
        w_down,
        ln1_gain,
        ln1_bias,
        query_bias,
        value_bias,
        out_bias,
        ln2_gain,
        ln2_bias,
        up_bias,
        down_bias,
    ) = weights
    query_heads = saved["query_heads"]
    key_picked = saved["key_picked"]
    value_picked = saved["value_picked"]
    key_slots = saved["key_slots"]
    is_edge = saved["is_edge"]
    edge_slot = saved["edge_slot"]
    local_blocks = query_heads.shape[1]
    head_dim = query_heads.shape[3]
    all_blocks = saved["key_flat"].shape[1] // BLOCK
    score_scale = head_dim ** (-0.5)
    token_count = grad_rows.shape[0]
    grad_ff_low = grad_rows.astype(jnp.bfloat16)
    grad_w_down = weight_grad(saved["hidden_low"], grad_ff_low)
    grad_down_bias = column_sum(grad_ff_low)
    (grad_pre,) = saved["pull_gelu"](project_back(grad_ff_low, w_down))
    grad_pre_low = grad_pre.astype(jnp.bfloat16)
    grad_w_up = weight_grad(saved["normed_two_low"], grad_pre_low)
    grad_up_bias = column_sum(grad_pre_low)
    grad_normed_two = project_back(grad_pre_low, w_up)
    grad_middle, grad_ln2_gain, grad_ln2_bias = saved["pull_second"](grad_normed_two)
    grad_middle = grad_middle + grad_rows
    grad_attn_low = grad_middle.astype(jnp.bfloat16)
    grad_w_out = weight_grad(saved["mixed_low"], grad_attn_low)
    grad_out_bias = column_sum(grad_attn_low)
    grad_mixed = (
        project_back(grad_attn_low, w_out)
        .astype(jnp.bfloat16)
        .reshape(local_blocks, BLOCK, HEADS, head_dim)
    )
    block_ids = jnp.arange(local_blocks, dtype=jnp.int32)
    keep_sparse = jnp.where(is_edge & (block_ids == edge_slot), 0.0, 1.0).astype(jnp.bfloat16)
    grad_sparse = grad_mixed * keep_sparse[:, None, None, None]
    scores = sparse_scores(query_heads, key_picked, saved["key_valid"], score_scale)
    attn_prob = jnp.exp(scores - saved["log_sparse"][..., None])
    grad_prob = jnp.einsum(
        "qihd,hqkd->hqik", grad_sparse, value_picked, preferred_element_type=jnp.float32
    )
    grad_value_picked = jnp.einsum(
        "hqik,qihd->hqkd",
        attn_prob.astype(jnp.bfloat16),
        grad_sparse,
        preferred_element_type=jnp.float32,
    )
    grad_scores = softmax_back(attn_prob, grad_prob, score_scale)
    grad_query_sparse = jnp.einsum(
        "hqik,hqkd->qihd", grad_scores, key_picked, preferred_element_type=jnp.float32
    )
    grad_key_picked = jnp.einsum(
        "hqik,hqid->hqkd", grad_scores, query_heads, preferred_element_type=jnp.float32
    )
    head_index = jnp.arange(HEADS)[:, None, None]
    slot_count = key_slots.shape[2]
    table_shape = (HEADS, all_blocks, BLOCK * head_dim)
    grad_key_table = (
        jnp.zeros(table_shape, jnp.float32)
        .at[head_index, key_slots]
        .add(grad_key_picked.reshape(HEADS, local_blocks, slot_count, BLOCK * head_dim))
    )
    grad_value_table = (
        jnp.zeros(table_shape, jnp.float32)
        .at[head_index, key_slots]
        .add(grad_value_picked.reshape(HEADS, local_blocks, slot_count, BLOCK * head_dim))
    )
    grad_edge_block = lax.dynamic_index_in_dim(grad_mixed, edge_slot, 0, keepdims=False)
    flat_shape = (HEADS, all_blocks * BLOCK, head_dim)
    grad_query_edge, grad_key_edge, grad_value_edge = lax.cond(
        is_edge,
        lambda: dense_backward(
            saved["query_edge"],
            saved["key_flat"],
            saved["value_flat"],
            grad_edge_block,
            saved["log_edge"],
            score_scale,
        ),
        lambda: (
            jnp.zeros((BLOCK, HEADS, head_dim), jnp.float32),
            jnp.zeros(flat_shape, jnp.float32),
            jnp.zeros(flat_shape, jnp.float32),
        ),
    )
    grad_key_table = grad_key_table + grad_key_edge.reshape(table_shape)
    grad_value_table = grad_value_table + grad_value_edge.reshape(table_shape)
    grad_key_own, grad_value_own = (
        lax.psum_scatter(
            from_table(grad_key_table).astype(jnp.bfloat16), "seq", scatter_dimension=0, tiled=True
        ).astype(jnp.float32),
        lax.psum_scatter(
            from_table(grad_value_table).astype(jnp.bfloat16),
            "seq",
            scatter_dimension=0,
            tiled=True,
        ).astype(jnp.float32),
    )
    current = lax.dynamic_index_in_dim(grad_query_sparse, edge_slot, 0, keepdims=False)
    grad_query_all = lax.dynamic_update_index_in_dim(
        grad_query_sparse, current + grad_query_edge, edge_slot, 0
    )
    grad_query_low = grad_query_all.reshape(token_count, HEADS * head_dim).astype(jnp.bfloat16)
    grad_key_low = grad_key_own.astype(jnp.bfloat16)
    grad_value_low = grad_value_own.astype(jnp.bfloat16)
    normed_low = saved["normed_low"]
    grad_w_query = weight_grad(normed_low, grad_query_low)
    grad_w_key = weight_grad(normed_low, grad_key_low)
    grad_w_value = weight_grad(normed_low, grad_value_low)
    grad_query_bias = column_sum(grad_query_low)
    grad_value_bias = column_sum(grad_value_low)
    grad_normed = (
        project_back(grad_query_low, w_query)
        + project_back(grad_key_low, w_key)
        + project_back(grad_value_low, w_value)
    )
    grad_inputs, grad_ln1_gain, grad_ln1_bias = saved["pull_first"](grad_normed)
    grad_inputs = grad_inputs + grad_middle
    grads = (
        grad_w_query,
        grad_w_key,
        grad_w_value,
        grad_w_out,
        grad_w_up,
        grad_w_down,
        grad_ln1_gain,
        grad_ln1_bias,
        grad_query_bias,
        grad_value_bias,
        grad_out_bias,
        grad_ln2_gain,
        grad_ln2_bias,
        grad_up_bias,
        grad_down_bias,
    )
    return (grad_inputs, grads)


def on_device(inputs, grad_out, random_blocks, *shards):
    weights = tuple(lax.all_gather(part, BOTH, axis=0, tiled=True) for part in shards)

    def micro_step(totals, sequence):
        in_rows, grad_rows, random_ids = sequence
        saved, result = run_forward(weights, in_rows, random_ids)
        grad_in, grads = run_backward(weights, saved, grad_rows)
        return (tuple(left + right for left, right in zip(totals, grads)), (result, grad_in))

    initial = tuple(jnp.zeros(weight.shape, jnp.float32) for weight in weights)
    totals, (results, grads_in) = lax.scan(micro_step, initial, (inputs, grad_out, random_blocks))
    summed = tuple(
        lax.psum_scatter(total, BOTH, scatter_dimension=0, tiled=True) for total in totals
    )
    return (results, grads_in) + summed


F32, BF16 = jnp.float32, jnp.bfloat16
PAIR = 128
TIMES = dict(
    cast_far=1,
    join_first=2,
    join_beside=1,
    join_up=2,
    join_plane=2,
    small_vectors=2,
    norm_project=4,
    attn_forward=0.5,
    out_norm=1,
    join_low=0.3,
    feed_forward=9,
    split_add=0.1,
    merge_add=0.3,
    beside_add=0.3,
    middle_back=40,
    grad_wide=1.8,
    attn_backward=5,
    split_depth=0.3,
    input_back=1,
    pack_vectors=0.3,
    fill_far=0.05,
    last_add=0.05,
)
COST = 0.3 * 1e9
NEAR = tuple((dx, dc, dy) for dx in range(2) for dc in range(2) for dy in range(2))


def contract(left, right, left_dim, right_dim):
    return lax.dot_general(
        left, right, (((left_dim,), (right_dim,)), ((), ())), preferred_element_type=F32
    )


def held(*shape):
    zeros = (0,) * len(shape)
    return pl.BlockSpec(shape, lambda *_: zeros, pipeline_mode=pl.Buffered(1))


def whole_ref():
    return pl.BlockSpec(memory_space=pltpu.HBM)


def call(body, name, grid, in_specs, out_specs, out_shape, args, scratch=(), vmem=24, alias=None):
    spec = pltpu.PrefetchScalarGridSpec(
        num_scalar_prefetch=1,
        grid=grid,
        in_specs=in_specs,
        out_specs=out_specs,
        scratch_shapes=scratch,
    )
    return pl.pallas_call(
        body,
        grid_spec=spec,
        out_shape=out_shape,
        name=name,
        input_output_aliases=alias or {},
        compiler_params=pltpu.CompilerParams(vmem_limit_bytes=vmem << 20),
        cost_estimate=pl.CostEstimate(
            flops=int(TIMES[name] * grid[0] * COST), bytes_accessed=1, transcendentals=1
        ),
    )(*args)


def shape_of(kind, *shape):
    return jax.ShapeDtypeStruct(shape, kind)


def norm_parts(values):
    mean = jnp.mean(values, axis=-1, keepdims=True)
    centre = values - mean
    spread = jnp.mean(centre * centre, axis=-1, keepdims=True)
    scale = lax.rsqrt(spread + eps_norm)
    return centre * scale, scale


def norm_back(unit, scale, gain, grad):
    inner = grad * gain
    first = jnp.mean(inner, axis=-1, keepdims=True)
    second = jnp.mean(inner * unit, axis=-1, keepdims=True)
    return scale * (inner - first - unit * second)


def column(values):
    return jnp.sum(values, axis=0, keepdims=True)


def gelu_both(values):
    root = 2 * 0.7978845608028654
    cubic = root * 0.044715
    turn = -1.4426950408889634
    square = values * values
    power = jnp.exp2(jnp.minimum(values * (turn * root + (turn * cubic) * square), 126.0))
    part = pl.reciprocal(1.0 + power, approx=True)
    hidden = values * part
    return hidden, part + (hidden - hidden * part) * (root + (3 * cubic) * square)


def flip(value, bit):
    return 1 - value if bit else value


def parts_copies(place_ref, part_refs, weight, sems, start, size, into, chunk):
    copies = []
    for at, (dx, dc, dy) in enumerate(NEAR):
        spot = (slice(None), flip(place_ref[1], dx), flip(place_ref[2], dc), flip(place_ref[3], dy))
        copies.append(
            pltpu.make_async_copy(
                part_refs[at].at[:, :, pl.ds(start, size)],
                weight.at[spot + (slice(None), pl.ds(into, size))],
                sems.at[chunk, at],
            )
        )
    return copies


def weight_scratch(part, columns):
    depth, rows, _ = part.shape
    return pltpu.VMEM((depth, 2, 2, 2, rows, columns), BF16)


def flat(value):
    return value.reshape(-1, value.shape[-1])


def depth_copies(place_ref, part_refs, weight, sems):
    depth = weight.shape[0]
    copies = []
    for step in range(depth):
        there = lax.rem(place_ref[0] + depth - step, depth)
        for dc in range(2):
            core = flip(place_ref[2], dc)
            copies.append(
                pltpu.make_async_copy(
                    part_refs[2 * step + dc], weight.at[there, :, core], sems.at[there, dc]
                )
            )
    return copies


def depth_wait(place_ref, part_refs, weight, sems, at):
    for dc in range(2):
        core = flip(place_ref[2], dc)
        pltpu.make_async_copy(part_refs[dc], weight.at[at, :, core], sems.at[at, dc]).wait()


def own_spec(step, width, parts):
    return pl.BlockSpec((1, step, width), lambda i, p: (p[3], jnp.minimum(i, parts - 1), 0))


def far_spec(step, width, parts):
    return pl.BlockSpec((step, width), lambda i, _: (jnp.maximum(i - parts, 0), 0))


def join(place, blocks, moves, shapes, name):
    def body(place_ref, *refs):
        ins, outs = refs[: len(blocks)], refs[len(blocks) :]
        for i, cut, j, spot in moves:
            outs[j][spot(place_ref)] = ins[i][cut]

    return call(
        body,
        name,
        (1,),
        [held(*block.shape) for block in blocks],
        [held(*shape) for shape in shapes],
        [shape_of(BF16, *shape) for shape in shapes],
        (place,) + tuple(blocks),
        vmem=10,
    )


def join_beside(place, blocks):
    rows = blocks[0].shape[0]
    widths = [block.shape[1] for block in blocks]

    def body(place_ref, *refs):
        start = 0
        for ref, width in zip(refs, widths):
            refs[-1][:, start : start + width] = ref[...]
            start += width

    return call(
        body,
        "join_beside",
        (1,),
        [held(*block.shape) for block in blocks],
        held(rows, sum(widths)),
        shape_of(BF16, rows, sum(widths)),
        (place,) + tuple(blocks),
        vmem=4,
    )


def join_low(place, grad_out, far):
    half, width = far.shape

    def body(place_ref, own_ref, far_ref, low_ref, sum_ref):
        low = own_ref[0].astype(BF16)
        low_ref[:half] = low
        low_ref[half:] = far_ref[...]
        sum_ref[...] = column(low.astype(F32)) + column(far_ref[...].astype(F32))

    return call(
        body,
        "join_low",
        (1,),
        [
            pl.BlockSpec((1, half, width), lambda i, p: (p[3], 0, 0), pipeline_mode=pl.Buffered(1)),
            held(half, width),
        ],
        [held(2 * half, width), held(1, width)],
        [shape_of(BF16, 2 * half, width), shape_of(F32, 1, width)],
        (place, grad_out, far),
        vmem=12,
    )


def cast_far(place, values):
    _, half, width = values.shape
    step = half // 2

    def body(place_ref, values_ref, out_ref):
        out_ref[...] = values_ref[0].astype(BF16)

    return call(
        body,
        "cast_far",
        (half // step,),
        [pl.BlockSpec((1, step, width), lambda i, p: (1 - p[3], i, 0))],
        pl.BlockSpec((step, width), lambda i, _: (i, 0)),
        shape_of(BF16, half, width),
        (place, values),
        vmem=6,
    )


class Transfers:
    def __init__(self, sems):
        self.sems, self.count = sems, 0

    def start(self, source, target):
        copy = pltpu.make_async_copy(source, target, self.sems.at[self.count])
        self.count += 1
        copy.start()
        return copy


def wait_all(copies):
    for copy in copies:
        copy.wait()


def start_parts(moves, place_ref, part_refs, weight, start, size, into):
    copies = []
    for part_ref, (dx, dc, dy) in zip(part_refs, NEAR):
        x, c, y = flip(place_ref[1], dx), flip(place_ref[2], dc), flip(place_ref[3], dy)
        copies.append(
            moves.start(
                part_ref.at[:, :, pl.ds(start, size)],
                weight.at[:, x, c, y, :, pl.ds(into, size)],
            )
        )
    return copies


def start_rows(moves, place_ref, whole_in, far_in, own, far, cuts):
    half = own.shape[0]
    copies = []
    for cut in cuts:
        if cut.start < half:
            copies.append(moves.start(whole_in.at[place_ref[3], cut], own.at[cut]))
        else:
            back = pl.ds(cut.start - half, cut.size)
            copies.append(moves.start(far_in.at[back], far.at[back]))
    return copies


def rows_at(own, far, cut):
    half = own.shape[0]
    if cut.start < half:
        return own[cut]
    return far[pl.ds(cut.start - half, cut.size)].astype(F32)


def row_cuts(tokens, step):
    return [pl.ds(start, step) for start in range(0, tokens, step)]


def norm_project(place, inputs, far, gain, shift, left, right, bias):
    half, width = far.shape
    tokens = 2 * half
    columns = bias.shape[1]
    step = 512
    left_steps = left[0].shape[-1] // step
    steps = columns // step
    cuts = row_cuts(tokens, 256)

    def body(place_ref, gain_ref, shift_ref, bias_ref, inputs_in, far_in, *refs):
        left_refs, right_refs = refs[:8], refs[8:16]
        normed_out, out_ref, own, far_rows, normed, weight, result, sems = refs[16:]
        moves = Transfers(sems)

        def weights(chunk):
            refs, start = (left_refs, chunk) if chunk < left_steps else (right_refs, chunk - left_steps)
            return start_parts(moves, place_ref, refs, weight, start * step, step, chunk * step)

        rows = start_rows(moves, place_ref, inputs_in, far_in, own, far_rows, cuts)
        parts = [weights(chunk) for chunk in range(steps)]
        away = []
        wait_all(rows)
        for chunk in range(steps):
            span = pl.ds(chunk * step, step)
            wait_all(parts[chunk])
            part = flat(weight[:, :, :, :, :, span])
            for cut in cuts:
                if chunk == 0:
                    unit, _ = norm_parts(rows_at(own, far_rows, cut))
                    low = (unit * gain_ref[...] + shift_ref[...]).astype(BF16)
                    normed[cut] = low
                else:
                    low = normed[cut]
                value = contract(low, part, 1, 0) + bias_ref[:, span]
                result[chunk, cut] = value.astype(BF16)
            if chunk == 0:
                away.append(moves.start(normed, normed_out))
            away.append(moves.start(result.at[chunk], out_ref.at[:, span]))
        wait_all(away)

    return call(
        body,
        "norm_project",
        (1,),
        [held(1, width), held(1, width), held(1, columns)] + [whole_ref()] * 18,
        [whole_ref(), whole_ref()],
        [shape_of(BF16, tokens, width), shape_of(BF16, tokens, columns)],
        (place, gain, shift, bias, inputs, far) + tuple(left) + tuple(right),
        scratch=[
            pltpu.VMEM((half, width), F32),
            pltpu.VMEM((half, width), BF16),
            pltpu.VMEM((tokens, width), BF16),
            weight_scratch(left[0], columns),
            pltpu.VMEM((steps, tokens, step), BF16),
            pltpu.SemaphoreType.DMA((2 * len(cuts) + 9 * steps,)),
        ],
        vmem=56,
    )


def out_norm(place, mixed, up_parts, at_out, bias, inputs, far, gain, shift):
    half, width = far.shape
    tokens = 2 * half
    cuts = row_cuts(tokens, 256)

    def body(place_ref, bias_ref, gain_ref, shift_ref, mixed_in, inputs_in, far_in, *refs):
        part_refs = refs[:8]
        middle_out, normed_out, mixed_rows, own, far_rows, middle, normed, weight, sems = refs[8:]
        moves = Transfers(sems)
        parts = start_parts(moves, place_ref, part_refs, weight, at_out, width, 0)
        mixes = [moves.start(mixed_in.at[cut], mixed_rows.at[cut]) for cut in cuts]
        rows = start_rows(moves, place_ref, inputs_in, far_in, own, far_rows, cuts)
        wait_all(parts)
        away = []
        for at, cut in enumerate(cuts):
            mixes[at].wait()
            product = contract(mixed_rows[cut], flat(weight[...]), 1, 0) + bias_ref[...]
            rows[at].wait()
            value = rows_at(own, far_rows, cut) + product
            middle[cut] = value
            away.append(moves.start(middle.at[cut], middle_out.at[cut]))
            unit, _ = norm_parts(value)
            normed[cut] = (unit * gain_ref[...] + shift_ref[...]).astype(BF16)
            away.append(moves.start(normed.at[cut], normed_out.at[cut]))
        wait_all(away)

    return call(
        body,
        "out_norm",
        (1,),
        [held(1, width)] * 3 + [whole_ref()] * 11,
        [whole_ref(), whole_ref()],
        [shape_of(F32, tokens, width), shape_of(BF16, tokens, width)],
        (place, bias, gain, shift, mixed, inputs, far) + tuple(up_parts),
        scratch=[
            pltpu.VMEM((tokens, width), BF16),
            pltpu.VMEM((half, width), F32),
            pltpu.VMEM((half, width), BF16),
            pltpu.VMEM((tokens, width), F32),
            pltpu.VMEM((tokens, width), BF16),
            weight_scratch(up_parts[0], width),
            pltpu.SemaphoreType.DMA((8 + 4 * len(cuts),)),
        ],
        vmem=56,
    )


def fill_far(place, partial, base, delta):
    _, half, width = base.shape
    step = 256

    def body(place_ref, partial_ref, base_ref, delta_ref, out_ref):
        out_ref[0] = base_ref[0] + delta_ref[...].astype(F32)

    there = pl.BlockSpec((1, step, width), lambda i, p: (1 - p[3], i, 0))
    return call(
        body,
        "fill_far",
        (half // step,),
        [whole_ref(), there, pl.BlockSpec((step, width), lambda i, _: (i, 0))],
        there,
        shape_of(F32, 2, half, width),
        (place, partial, base, delta),
        alias={1: 0},
        vmem=8,
    )


def grad_wide(place, left, rights, rows, span, pieces=1):
    tokens, tall = left.shape
    width = rights[0].shape[1]
    step = 512
    each = width // step
    first, stop = span
    steps = stop - first
    per = steps // pieces
    group = 4 * rows
    used = sorted({at // each for at in range(first, stop)})

    def body(place_ref, left_ref, *refs):
        right_refs = refs[: len(used)]
        outs, sums = refs[len(used) : -1], refs[-1]
        at = pl.program_id(0)
        for which, right_ref in zip(used, right_refs):
            @pl.when((at + first) // each == which)
            def _():
                result = contract(left_ref[...], right_ref[...], 0, 0).astype(BF16)
                sums[...] = result.reshape(tall // group, 2, group // 2, step)

        for piece in range(pieces):
            @pl.when(at // per == piece)
            def _():
                outs[2 * piece][...] = sums[:, place_ref[2]]
                outs[2 * piece + 1][...] = sums[:, 1 - place_ref[2]]

    def right_at(which):
        low, high = max(first - which * each, 0), min(stop - which * each, each) - 1
        return lambda i, _: (0, jnp.clip(i + first - which * each, low, high))

    def out_at(piece):
        return lambda i, _: (0, 0, jnp.clip(i - piece * per, 0, per - 1))

    return call(
        body,
        "grad_wide",
        (steps,),
        [held(tokens, tall)] + [pl.BlockSpec((tokens, step), right_at(which)) for which in used],
        [
            pl.BlockSpec((tall // group, group // 2, step), out_at(piece))
            for piece in range(pieces)
            for _ in range(2)
        ],
        [shape_of(BF16, tall // group, group // 2, per * step)] * (2 * pieces),
        (place, left) + tuple(rights[which] for which in used),
        scratch=[pltpu.VMEM((tall // group, 2, group // 2, step), BF16)],
        vmem=20,
    )


def feed_forward(place, first, count, depth, normed, grad_low, up_parts, down_parts, up_bias, down_bias, far, state, wide):
    tokens, width = normed.shape
    half = tokens // 2
    hidden_width = up_bias.shape[1]
    step = hidden_width // (2 * depth)
    steps = 2 * count
    rows = down_parts[0].shape[-2]
    group = width // (2 * depth)
    last = first + count == depth
    columns, offset, before = wide
    offset = offset // step
    lines = up_parts[0].shape[1]
    beside = (up_parts[0].shape[-1] - hidden_width) // width
    rows = rows + beside * lines

    def body(place_ref, bias_ref, down_ref, normed_in, grad_in, far_in, out_in, back_in, *refs):
        up_refs, down_refs = refs[:8], refs[8 : 8 + 2 * depth]
        refs = refs[8 + 2 * depth + len(before) :]
        tall_mine, tall_other, wide_mine, wide_other, sum_ref, back_out = refs[:6]
        outs = refs[6:8] if last else refs[6:7]
        refs = refs[6 + len(outs) :]
        normed_ref, grad_ref, far_ref, total, back, delta = refs[:6]
        up, down, up_sems, down_sems, beside_sems, state_sems, tall_sums, wide_sums = refs[6:]
        at = pl.program_id(0)
        slot = lax.rem(at, 2)

        def up_copies(index, into):
            start = pl.multiple_of((2 * first + index) * step, step)
            copies = []
            for which, (dx, dc, dy) in enumerate(NEAR):
                x, c, y = flip(place_ref[1], dx), flip(place_ref[2], dc), flip(place_ref[3], dy)
                copies.append(
                    pltpu.make_async_copy(
                        up_refs[which].at[:, :, pl.ds(start, step)],
                        up.at[into, :, x, c, y],
                        up_sems.at[into, which],
                    )
                )
            return copies

        def down_copies(index, into, turn):
            x = lax.rem(index, 2)
            return [
                pltpu.make_async_copy(
                    down_refs[2 * turn + dc].at[x],
                    down.at[into, flip(place_ref[2], dc), :, pl.ds(0, rows - beside * lines)],
                    down_sems.at[into, dc],
                )
                for dc in range(2)
            ]

        def beside_copies(index, into, dx):
            copies = []
            for dc in range(2):
                for dy in range(2):
                    which = NEAR.index((dx, dc, dy))
                    c, y = flip(place_ref[2], dc), flip(place_ref[3], dy)
                    for part in range(beside):
                        copies.append(
                            pltpu.make_async_copy(
                                up_refs[which].at[
                                    first + index // 2, :, pl.ds(hidden_width + part * width, width)
                                ],
                                down.at[into, c, y, pl.ds(rows - (beside - part) * lines, lines)],
                                beside_sems.at[into, len(copies)],
                            )
                        )
            return copies

        def begin(index, into):
            for copy in up_copies(index, into):
                copy.start()
            away = lax.rem(place_ref[0] + depth - first - index // 2, depth)
            for turn in range(depth):
                @pl.when(away == turn)
                def _():
                    for copy in down_copies(index, into, turn):
                        copy.start()
            for dx in range(2):
                @pl.when(flip(place_ref[1], dx) == lax.rem(index, 2))
                def _():
                    for copy in beside_copies(index, into, dx):
                        copy.start()

        normed_copy = pltpu.make_async_copy(normed_in, normed_ref, state_sems.at[0])
        grad_copy = pltpu.make_async_copy(grad_in, grad_ref, state_sems.at[1])
        out_copy = pltpu.make_async_copy(out_in, total, state_sems.at[2])
        if first:
            back_copy = pltpu.make_async_copy(back_in, back, state_sems.at[3])
        back_away = pltpu.make_async_copy(back, back_out, state_sems.at[5])
        if last:
            far_copy = pltpu.make_async_copy(far_in, far_ref, state_sems.at[4])
            away = [
                pltpu.make_async_copy(
                    total.at[pl.ds(0, half)], outs[0].at[place_ref[3]], state_sems.at[6]
                ),
                pltpu.make_async_copy(delta, outs[1], state_sems.at[7]),
            ]
        else:
            away = [pltpu.make_async_copy(total, outs[0], state_sems.at[6])]

        @pl.when(at == 0)
        def _():
            normed_copy.start()
            begin(0, 0)
            grad_copy.start()
            out_copy.start()
            if first:
                back_copy.start()
            else:
                back[...] = jnp.zeros((tokens, width), F32)
            if last:
                far_copy.start()
            normed_copy.wait()

        @pl.when(at + 1 < steps)
        def _():
            begin(at + 1, 1 - slot)

        for copy in up_copies(at, slot):
            copy.wait()
        up_part = flat(up[slot])
        before_gelu = contract(normed_ref[...], up_part, 1, 0) + bias_ref[...]
        hidden, slope = gelu_both(before_gelu)
        hidden = hidden.astype(BF16)

        @pl.when(at == 0)
        def _():
            grad_copy.wait()

        tall = contract(hidden, grad_ref[...], 0, 0).astype(BF16)
        tall_sums[...] = tall.reshape(tall_sums.shape)
        tall_mine[0] = tall_sums[place_ref[2]]
        tall_other[0] = tall_sums[1 - place_ref[2]]

        for copy in down_copies(at, slot, 0) + beside_copies(at, slot, 0):
            copy.wait()

        @pl.when(at == 0)
        def _():
            out_copy.wait()
            if first:
                back_copy.wait()
            if last:
                far_copy.wait()

        down_part = flat(down[slot])
        total[...] += contract(hidden, down_part, 1, 0)

        @pl.when(at == steps - 1)
        def _():
            if last:
                total[...] += down_ref[...]
                delta[...] = (total[half:] - far_ref[...].astype(F32)).astype(BF16)
            for copy in away:
                copy.start()

        low = (contract(grad_ref[...], down_part, 1, 1) * slope).astype(BF16)
        back[...] += contract(low, up_part, 1, 1)

        @pl.when(at == steps - 1)
        def _():
            back_away.start()

        sum_ref[...] = column(low.astype(F32))
        broad = contract(normed_ref[...], low, 0, 0).astype(BF16)
        wide_sums[...] = broad.reshape(wide_sums.shape)
        wide_mine[...] = wide_sums[:, place_ref[2]]
        wide_other[...] = wide_sums[:, 1 - place_ref[2]]

        @pl.when(at == steps - 1)
        def _():
            for copy in away + [back_away]:
                copy.wait()

    tall_spec = pl.BlockSpec((1, 2 * rows, width), lambda i, _: (i, 0, 0))
    broad_spec = pl.BlockSpec((2 * depth, group // 2, step), lambda i, _: (0, 0, offset + i))
    sum_spec = pl.BlockSpec((1, step), lambda i, _: (0, i))
    out_specs = [tall_spec, tall_spec, broad_spec, broad_spec, sum_spec, whole_ref()]
    out_shape = [shape_of(BF16, steps, 2 * rows, width)] * 2
    out_shape += [shape_of(BF16, 2 * depth, group // 2, columns)] * 2
    out_shape += [shape_of(F32, 1, steps * step), shape_of(F32, tokens, width)]
    if last:
        out_specs += [whole_ref()] * 2
        out_shape += [shape_of(F32, 2, half, width), shape_of(BF16, half, width)]
    else:
        out_specs += [whole_ref()]
        out_shape += [shape_of(F32, tokens, width)]
    scratch = [
        pltpu.VMEM((tokens, width), BF16),
        pltpu.VMEM((tokens, width), BF16),
        pltpu.VMEM((half, width), BF16),
        pltpu.VMEM((tokens, width), F32),
        pltpu.VMEM((tokens, width), F32),
        pltpu.VMEM((half, width), BF16),
        pltpu.VMEM((2, depth, 2, 2, 2, group // 4, step), BF16),
        pltpu.VMEM((2, 2, 2, rows, width), BF16),
        pltpu.SemaphoreType.DMA((2, 8)),
        pltpu.SemaphoreType.DMA((2, 2)),
        pltpu.SemaphoreType.DMA((2, 4 * beside)),
        pltpu.SemaphoreType.DMA((8,)),
        pltpu.VMEM((2, 2 * rows, width), BF16),
        pltpu.VMEM((2 * depth, 2, group // 2, step), BF16),
    ]
    args = (place, up_bias, down_bias, normed, grad_low, far) + tuple(state) + tuple(up_parts) + tuple(down_parts)
    alias = {len(args) + i: 2 + i for i in range(len(before))}
    return call(
        body,
        "feed_forward",
        (steps,),
        [pl.BlockSpec((1, step), lambda i, _: (0, 2 * first + i)), held(1, width)]
        + [whole_ref()] * (5 + 8 + 2 * depth + len(before)),
        out_specs,
        out_shape,
        args + tuple(before),
        scratch=scratch,
        vmem=46,
        alias=alias,
    )


def middle_back(place, grad_normed, middle, gain, grad_out, far, up_parts, at_out):
    half, width = far.shape
    tokens = 2 * half
    cuts = row_cuts(tokens, 256)

    def body(place_ref, gain_ref, grad_in, middle_in, grad_out_in, far_in, *refs):
        part_refs = refs[:8]
        total_out, low_out, mixed_out = refs[8:11]
        sum_refs = refs[11:14]
        grads, middles, own, far_rows, total, low, mixed, weight, sems = refs[14:]
        moves = Transfers(sems)
        pairs = []
        for at, cut in enumerate(cuts):
            pairs.append(
                [
                    moves.start(grad_in.at[cut], grads.at[cut]),
                    moves.start(middle_in.at[cut], middles.at[cut]),
                ]
                + start_rows(moves, place_ref, grad_out_in, far_in, own, far_rows, [cut])
            )
            if at == 0:
                parts = start_parts(moves, place_ref, part_refs, weight, at_out, width, 0)
        sums = [jnp.zeros((1, width), F32) for _ in range(3)]
        away = []
        for at, cut in enumerate(cuts):
            wait_all(pairs[at])
            grad = grads[cut]
            unit, scale = norm_parts(middles[cut])
            value = rows_at(own, far_rows, cut) + norm_back(unit, scale, gain_ref[...], grad)
            total[cut] = value
            away.append(moves.start(total.at[cut], total_out.at[cut]))
            value_low = value.astype(BF16)
            low[cut] = value_low
            away.append(moves.start(low.at[cut], low_out.at[cut]))
            sums[0] += column(grad * unit)
            sums[1] += column(grad)
            sums[2] += column(value_low.astype(F32))
            if at == 0:
                wait_all(parts)
            mixed[cut] = contract(value_low, flat(weight[...]), 1, 1).astype(BF16)
            away.append(moves.start(mixed.at[cut], mixed_out.at[cut]))
        for ref, value in zip(sum_refs, sums):
            ref[...] = value
        wait_all(away)

    vector = held(1, width)
    return call(
        body,
        "middle_back",
        (1,),
        [vector] + [whole_ref()] * 12,
        [whole_ref()] * 3 + [vector] * 3,
        [shape_of(F32, tokens, width), shape_of(BF16, tokens, width), shape_of(BF16, tokens, width)]
        + [shape_of(F32, 1, width)] * 3,
        (place, gain, grad_normed, middle, grad_out, far) + tuple(up_parts),
        scratch=[
            pltpu.VMEM((tokens, width), F32),
            pltpu.VMEM((tokens, width), F32),
            pltpu.VMEM((half, width), F32),
            pltpu.VMEM((half, width), BF16),
            pltpu.VMEM((tokens, width), F32),
            pltpu.VMEM((tokens, width), BF16),
            pltpu.VMEM((tokens, width), BF16),
            weight_scratch(up_parts[0], width),
            pltpu.SemaphoreType.DMA((8 + 6 * len(cuts),)),
        ],
        vmem=56,
    )


def input_back(place, grads, left, right, inputs, far, gain, middle_grad, far_grad):
    half, width = far.shape
    tokens = 2 * half
    split = left[0].shape[-1]
    cuts = row_cuts(tokens, 256)

    def body(place_ref, gain_ref, query_in, key_in, value_in, inputs_in, far_in, middle_in, far_grad_in, *refs):
        left_refs, right_refs = refs[:8], refs[8:16]
        out_ref, delta_out = refs[16:18]
        sum_refs = refs[18:22]
        query, key, value, own, far_rows, middle, far_grads, result, delta, weight, sems = refs[22:]
        moves = Transfers(sems)
        first = start_parts(moves, place_ref, left_refs, weight, 0, split, 0)
        pairs, lates = [], []
        for at, cut in enumerate(cuts):
            pairs.append([moves.start(query_in.at[cut], query.at[cut]), moves.start(key_in.at[cut], key.at[cut])])
            late = [moves.start(value_in.at[cut], value.at[cut])]
            if at == 0:
                late += start_parts(moves, place_ref, right_refs, weight, 0, 3 * width - split, split)
            late += start_rows(moves, place_ref, inputs_in, far_in, own, far_rows, [cut])
            late.append(moves.start(middle_in.at[cut], middle.at[cut]))
            if cut.start >= half:
                back = pl.ds(cut.start - half, cut.size)
                late.append(moves.start(far_grad_in.at[back], far_grads.at[back]))
            lates.append(late)

        def part(chunk):
            return flat(weight[:, :, :, :, :, chunk * width : (chunk + 1) * width])

        sums = [jnp.zeros((1, width), F32) for _ in range(4)]
        away = []
        for at, cut in enumerate(cuts):
            wait_all(pairs[at])
            if at == 0:
                wait_all(first)
            grad = contract(query[cut], part(0), 1, 1) + contract(key[cut], part(1), 1, 1)
            wait_all(lates[at])
            grad += contract(value[cut], part(2), 1, 1)
            unit, scale = norm_parts(rows_at(own, far_rows, cut))
            sums[0] += column(grad * unit)
            sums[1] += column(grad)
            sums[2] += column(query[cut].astype(F32))
            sums[3] += column(value[cut].astype(F32))
            total = middle[cut] + norm_back(unit, scale, gain_ref[...], grad)
            if cut.start < half:
                result[cut] = total
                away.append(moves.start(result.at[cut], out_ref.at[place_ref[3], cut]))
            else:
                back = pl.ds(cut.start - half, cut.size)
                delta[back] = (total - far_grads[back].astype(F32)).astype(BF16)
                away.append(moves.start(delta.at[back], delta_out.at[back]))
        for ref, total in zip(sum_refs, sums):
            ref[...] = total
        wait_all(away)

    vector = held(1, width)
    return call(
        body,
        "input_back",
        (1,),
        [vector] + [whole_ref()] * 23,
        [whole_ref()] * 2 + [vector] * 4,
        [shape_of(F32, 2, half, width), shape_of(BF16, half, width)] + [shape_of(F32, 1, width)] * 4,
        (place, gain) + tuple(grads) + (inputs, far, middle_grad, far_grad) + tuple(left) + tuple(right),
        scratch=[pltpu.VMEM((tokens, width), BF16)] * 3
        + [
            pltpu.VMEM((half, width), F32),
            pltpu.VMEM((half, width), BF16),
            pltpu.VMEM((tokens, width), F32),
            pltpu.VMEM((half, width), BF16),
            pltpu.VMEM((half, width), F32),
            pltpu.VMEM((half, width), BF16),
            weight_scratch(left[0], 3 * width),
            pltpu.SemaphoreType.DMA((16 + 8 * len(cuts),)),
        ],
        vmem=34,
    )


def split_add(place, mine, came, spot):
    groups, _, rows, columns = mine.shape

    def body(place_ref, mine_ref, came_ref, sent_ref, kept_ref):
        for ref, at in ((sent_ref, 1 - place_ref[spot]), (kept_ref, place_ref[spot])):
            ref[0] = (mine_ref[0, at].astype(F32) + came_ref[0, at].astype(F32)).astype(BF16)

    block = pl.BlockSpec((1, 2, rows, columns), lambda i, _: (i, 0, 0, 0))
    out = pl.BlockSpec((1, rows, columns), lambda i, _: (i, 0, 0))
    return call(
        body,
        "split_add",
        (groups,),
        [block, block],
        [out, out],
        [shape_of(BF16, groups, rows, columns)] * 2,
        (place, mine, came),
        vmem=8,
    )


def split_depth(place, pairs, rows, vectors=None, sizes=()):
    depth = pairs[0][0].shape[0]
    layout = [(which, part) for which, (mine, _) in enumerate(pairs) for part in range(mine.shape[1] // rows)]
    total = sum(pairs[which][0].shape[2] for which, _ in layout)
    extra = () if vectors is None else (vectors,)
    wide = total + PAIR * len(extra)
    count = depth * 8

    def body(place_ref, *refs):
        outs = refs[2 * len(pairs) + len(extra) :]
        for step, ref in enumerate(outs):
            at = lax.rem(place_ref[0] + step, depth)
            start = 0
            for which, part in layout:
                width = pairs[which][0].shape[2]
                cut = pl.ds(part * rows, rows)
                value = refs[2 * which][at, cut].astype(F32) + refs[2 * which + 1][at, cut].astype(F32)
                ref[:, start : start + width] = value.astype(ref.dtype)
                start += width
            if extra:
                device = ((at * 2 + place_ref[1]) * 2 + place_ref[2]) * 2 + place_ref[3]
                line = lax.broadcasted_iota(jnp.int32, (rows, PAIR), 0)
                block = jnp.zeros((rows, PAIR), F32)
                base = 0
                for index, size in enumerate(sizes):
                    values = refs[2 * len(pairs)][pl.ds(base + device * size * rows // PAIR, 1), :]
                    block = jnp.where(line == index, values, block)
                    base += count * size * rows // PAIR
                ref[:, total:] = block.astype(ref.dtype)

    return call(
        body,
        "split_depth",
        (1,),
        [held(*mine.shape) for mine, _ in pairs for _ in range(2)] + [held(*value.shape) for value in extra],
        [held(rows, wide)] * depth,
        [shape_of(F32, rows, wide)] + [shape_of(BF16, rows, wide)] * (depth - 1),
        (place,) + tuple(value for pair in pairs for value in pair) + extra,
        vmem=12,
    )


def last_add(place, own, came, shapes, before):
    rows, total = own.shape
    layout = [(which, part) for which, shape in enumerate(shapes) for part in range(shape[0] // rows)]
    offsets = [before[which].shape[1] if which in before else 0 for which in range(len(shapes))]
    extra = sorted(before)

    def body(place_ref, own_ref, *refs):
        outs = refs[len(came) + len(extra) :]
        for which, ref in zip(extra, refs[len(came) :]):
            outs[which][:, : offsets[which]] = ref[...]
        start = 0
        for which, part in layout:
            width = shapes[which][1]
            value = own_ref[:, start : start + width]
            for ref in refs[: len(came)]:
                value = value + ref[:, start : start + width].astype(F32)
            first = offsets[which]
            outs[which][part * rows : (part + 1) * rows, first : first + width] = value
            start += width

    wholes = [(shape[0], shape[1] + offset) for shape, offset in zip(shapes, offsets)]
    return call(
        body,
        "last_add",
        (1,),
        [held(rows, total)] * (1 + len(came)) + [held(*before[which].shape) for which in extra],
        [held(*shape) for shape in wholes],
        [shape_of(F32, *shape) for shape in wholes],
        (place, own) + tuple(came) + tuple(before[which] for which in extra),
        vmem=12,
    )


def spread_rows(count, per, size, row):
    span = size * per
    lane = lax.broadcasted_iota(jnp.int32, (per, count * span), 1)
    line = lax.broadcasted_iota(jnp.int32, (per, count * span), 0)
    return jnp.where(lane % span == row * per + line, 1.0, 0.0)


def chosen_rows(count, span):
    lane = lax.broadcasted_iota(jnp.int32, (count, count * span), 1)
    line = lax.broadcasted_iota(jnp.int32, (count, count * span), 0)
    return lane // span == line


def small_vectors(place, right, start, sizes, per):
    depth, rows, _ = right[0].shape
    count = depth * 8

    def body(place_ref, *refs):
        part_refs, outs, held_rows = refs[:8], refs[8:-1], refs[-1]
        for at, (dx, dc, dy) in enumerate(NEAR):
            x, c, y = flip(place_ref[1], dx), flip(place_ref[2], dc), flip(place_ref[3], dy)
            held_rows[:, x, c, y] = part_refs[at][...].astype(F32)
        table = held_rows[...].reshape(count, rows, PAIR)
        at = 0
        for ref, size in zip(outs, sizes):
            chosen = chosen_rows(count, size * per)
            line = jnp.zeros((1, count * size * per), F32)
            for row in range(size):
                spread = spread_rows(count, per, size, row).astype(BF16)
                wide = contract(table[:, at + row, :per].astype(BF16), spread, 1, 0)
                line += column(jnp.where(chosen, wide, 0.0))
            at += size
            ref[...] = line

    return call(
        body,
        "small_vectors",
        (1,),
        [pl.BlockSpec((depth, rows, PAIR), lambda i, _: (0, 0, start // PAIR))] * 8,
        [held(1, count * size * per) for size in sizes],
        [shape_of(F32, 1, count * size * per) for size in sizes],
        (place,) + tuple(right),
        scratch=[pltpu.VMEM((depth, 2, 2, 2, rows, PAIR), F32)],
        vmem=12,
    )


def merge_add(place, mine, came, spot):
    counts = [part.shape[0] for part in mine]
    _, _, rows, columns = mine[0].shape

    def body(place_ref, *refs):
        sent_ref, kept_ref = refs[2 * len(mine) :]
        start = 0
        for which, count in enumerate(counts):
            for ref, at in ((sent_ref, 1 - place_ref[spot]), (kept_ref, place_ref[spot])):
                total = refs[which][:, at].astype(F32) + refs[len(mine) + which][:, at].astype(F32)
                ref[start : start + count] = total.astype(BF16)
            start += count

    shape = (sum(counts), rows, columns)
    return call(
        body,
        "merge_add",
        (1,),
        [held(*part.shape) for part in mine + came],
        [held(*shape)] * 2,
        [shape_of(BF16, *shape)] * 2,
        (place,) + tuple(mine) + tuple(came),
        vmem=12,
    )


def beside_add(place, mine, came, spot):
    groups, _, rows, _ = mine[0].shape
    widths = [part.shape[-1] for part in mine]

    def body(place_ref, *refs):
        sent_ref, kept_ref = refs[2 * len(mine) :]
        for ref, at in ((sent_ref, 1 - place_ref[spot]), (kept_ref, place_ref[spot])):
            start = 0
            for which, width in enumerate(widths):
                total = refs[which][:, at].astype(F32) + refs[len(mine) + which][:, at].astype(F32)
                ref[:, :, start : start + width] = total.astype(BF16)
                start += width

    shape = (groups, rows, sum(widths))
    return call(
        body,
        "beside_add",
        (1,),
        [held(*part.shape) for part in mine + came],
        [held(*shape)] * 2,
        [shape_of(BF16, *shape)] * 2,
        (place,) + tuple(mine) + tuple(came),
        vmem=12,
    )


def attn_forward_kernel(q_ref, k_ref, v_ref, bias_ref, prob_ref, mixed_ref, total_ref):
    tokens, lanes = q_ref.shape
    half = lanes // 2
    lane = lax.broadcasted_iota(jnp.int32, (tokens, lanes), 1)
    block = lax.broadcasted_iota(jnp.int32, (tokens, lanes), 0) // BLOCK
    scale = half ** -0.5
    q = q_ref[...].astype(jnp.float32) * scale
    k = k_ref[...].astype(jnp.float32)
    v = v_ref[...].astype(jnp.float32)
    sides = []
    for head in range(2):
        own = (lane >= half) if head else (lane < half)
        first = 0 if head else half
        bias = jnp.broadcast_to(bias_ref[head][:, None, :], (tokens // BLOCK, BLOCK, lanes)).reshape(tokens, lanes)
        q_ext = jnp.where(own, q, jnp.where(lane - first == block, 1.0, 0.0)).astype(jnp.bfloat16)
        k_ext = jnp.where(own, k, bias).astype(jnp.bfloat16)
        v_ext = jnp.where(own, v, 1.0).astype(jnp.bfloat16)
        sides.append((q_ext, k_ext, v_ext))
    rows = min(512, tokens)
    low_lane = lax.broadcasted_iota(jnp.int32, (rows, lanes), 1) < half
    for start in range(0, tokens, rows):
        sums = []
        for head, (q_ext, k_ext, v_ext) in enumerate(sides):
            scores = contract(q_ext[start:start + rows], k_ext, 1, 1)
            top = jnp.max(scores, axis=1, keepdims=True)
            prob = jnp.exp(scores - top).astype(jnp.bfloat16)
            prob_ref[head, start:start + rows, :] = prob
            sums.append(contract(prob, v_ext, 1, 0))
        result = jnp.where(low_lane, sums[0], sums[1])
        totals = pltpu.roll(jnp.where(low_lane, sums[1], sums[0]), half, 1)
        mixed_ref[start:start + rows, :] = (result / totals).astype(jnp.bfloat16)
        total_ref[start:start + rows, :] = totals

def attn_backward_kernel(q_ref, k_ref, v_ref, prob_ref, mixed_ref, total_ref, grad_ref, dq_ref, dk_ref, dv_ref):
    tokens, lanes = q_ref.shape
    half = lanes // 2
    scale = half ** -0.5
    lane = lax.broadcasted_iota(jnp.int32, (tokens, lanes), 1)
    grad = grad_ref[...].astype(jnp.float32) / total_ref[...]
    inner = grad * mixed_ref[...].astype(jnp.float32)
    grad_low = grad.astype(jnp.bfloat16)
    q_turned = q_ref[...].T
    grad_turned = grad_low.T
    v = v_ref[...].astype(jnp.float32)
    k = k_ref[...]
    rows = 256
    low_lane = lax.broadcasted_iota(jnp.int32, (rows, lanes), 1) < half
    dq = [[None, None] for _ in range(tokens // rows)]
    dk, dv = [], []
    for head in range(2):
        own = (lane >= half) if head else (lane < half)
        first = 0 if head else half
        minus = -jnp.sum(jnp.where(own, inner, 0.0), axis=1, keepdims=True)
        high = minus.astype(jnp.bfloat16).astype(jnp.float32)
        grad_ext = jnp.where(own, grad, jnp.where(lane == first, high, jnp.where(lane == first + 1, minus - high, 0.0))).astype(jnp.bfloat16)
        v_ext = jnp.where(own, v, jnp.where(lane - first < 2, 1.0, 0.0)).astype(jnp.bfloat16)
        dk_sum = dv_sum = None
        for index in range(tokens // rows):
            part = slice(index * rows, (index + 1) * rows)
            prob = prob_ref[head, part, :]
            spread = contract(grad_ext[part], v_ext, 1, 1)
            grad_scores = (prob.astype(jnp.float32) * spread).astype(jnp.bfloat16)
            dq[index][head] = contract(grad_scores, k, 1, 0)
            rows_of = slice(head * half, (head + 1) * half)
            dk_part = contract(q_turned[rows_of, part], grad_scores, 1, 0)
            dv_part = contract(grad_turned[rows_of, part], prob, 1, 0)
            dk_sum = dk_part if dk_sum is None else dk_sum + dk_part
            dv_sum = dv_part if dv_sum is None else dv_sum + dv_part
        dk.append(dk_sum)
        dv.append(dv_sum)
    for index, pair in enumerate(dq):
        dq_ref[index * rows:(index + 1) * rows, :] = (jnp.where(low_lane, pair[0], pair[1]) * scale).astype(jnp.bfloat16)
    dk_ref[...] = (jnp.concatenate(dk, axis=0) * scale).T.astype(jnp.bfloat16)
    dv_ref[...] = jnp.concatenate(dv, axis=0).T.astype(jnp.bfloat16)


def attn_forward(place, qkv, bias, first, count, before=()):
    tokens, width = qkv.shape[0], qkv.shape[1] // 3
    pairs = width // PAIR

    def at(part):
        return pl.BlockSpec((tokens, PAIR), lambda i, _: (0, part * pairs + first + i))

    def body(place_ref, *refs):
        attn_forward_kernel(*refs[:4], *refs[4 + len(before) :])

    return call(
        body,
        "attn_forward",
        (count,),
        [at(0), at(1), at(2), pl.BlockSpec((2, tokens // BLOCK, PAIR), lambda i, _: (first + i, 0, 0))]
        + [whole_ref()] * len(before),
        [pl.BlockSpec((2, tokens, tokens), lambda i, _: (first + i, 0, 0)), at(0), at(0)],
        [
            shape_of(BF16, 2 * pairs, tokens, tokens),
            shape_of(BF16, tokens, width),
            shape_of(F32, tokens, width),
        ],
        (place, qkv, qkv, qkv, bias) + tuple(before),
        vmem=56,
        alias={5 + i: i for i in range(len(before))},
    )


def attn_backward(place, qkv, prob, mixed, total, grad, first, count, before=()):
    tokens, width = qkv.shape[0], qkv.shape[1] // 3
    pairs = width // PAIR

    def at(part):
        return pl.BlockSpec((tokens, PAIR), lambda i, _: (0, part * pairs + first + i))

    def body(place_ref, *refs):
        attn_backward_kernel(*refs[:7], *refs[7 + len(before) :])

    return call(
        body,
        "attn_backward",
        (count,),
        [at(0), at(1), at(2), pl.BlockSpec((2, tokens, tokens), lambda i, _: (first + i, 0, 0))]
        + [at(0)] * 3
        + [whole_ref()] * len(before),
        [at(0)] * 3,
        [shape_of(BF16, tokens, width)] * 3,
        (place, qkv, qkv, qkv, prob, mixed, total, grad) + tuple(before),
        vmem=28,
        alias={8 + i: i for i in range(len(before))},
    )


def key_bias(random_ids, block_ids):
    heads, blocks, _ = random_ids.shape
    row, col = block_ids[:, None], block_ids[None, :]
    last = blocks - 1
    fixed = (row == 0) | (row == last) | (col == 0) | (col == last) | (jnp.abs(row - col) <= 1)
    drawn = jnp.any(random_ids[:, :, :, None] == block_ids, axis=2)
    bias = jnp.where(fixed[None] | drawn, 0.0, -1e30)
    bias = bias.transpose(0, 2, 1).reshape(heads // 2, 2, blocks, blocks)
    lanes = 128
    even = jnp.pad(bias[:, 0], ((0, 0), (0, 0), (lanes // 2, lanes // 2 - blocks)))
    odd = jnp.pad(bias[:, 1], ((0, 0), (0, 0), (0, lanes - blocks)))
    return jnp.stack([even, odd], axis=1).reshape(heads, blocks, lanes)


def pair_swap(value, axis, bit):
    size = lax.axis_size(axis)
    return lax.ppermute(value, axis, [(i, i ^ bit) for i in range(size)])


def pick(value, index, axis):
    return lax.dynamic_index_in_dim(value, index, axis, keepdims=False)


def swap_x(value):
    return pair_swap(value, "dp", 2)


def swap_core(value):
    return pair_swap(value, "dp", 1)


def swap_y(value):
    return pair_swap(value, "seq", 1)


def ring_z(value, step):
    size = lax.axis_size("dp")
    return lax.ppermute(value, "dp", [(i, (i + 4 * step) % size) for i in range(size)])


def tie(*values):
    return lax.optimization_barrier(values)


class Reduce:
    def __init__(self, place, rows, x_first):
        self.place, self.rows, self.x_first = place, rows, x_first

    def begin(self, mine, other):
        self.mine, self.came = mine, swap_core(other)

    def first(self):
        groups, tall, columns = self.mine.shape
        if self.x_first:
            shape = (groups // 2, 2, tall, columns)
        else:
            shape = (groups, 2, self.rows, columns)
        spot, swap = (1, swap_x) if self.x_first else (3, swap_y)
        sent, kept = split_add(self.place, self.mine.reshape(shape), self.came.reshape(shape), spot)
        self.mine, self.came = kept, swap(sent)

    def second(self, *others, beside=False):
        spot, swap = (3, swap_y) if self.x_first else (1, swap_x)
        mine, came = [], []
        for part in (self,) + others:
            shape = (-1, 2, self.rows, part.mine.shape[-1])
            mine.append(part.mine.reshape(shape))
            came.append(part.came.reshape(shape))
        if beside:
            sent, kept = beside_add(self.place, mine, came, spot)
        elif others:
            sent, kept = merge_add(self.place, mine, came, spot)
        else:
            sent, kept = split_add(self.place, mine[0], came[0], spot)
        self.mine, self.came = kept, swap(sent)

    def third(self, *others, vectors=None, sizes=()):
        parts = (self,) + others
        rows = min(part.rows for part in parts)
        pairs = [(part.mine, part.came) for part in parts]
        own, *sent = split_depth(self.place, pairs, rows, vectors, sizes)
        self.mine = own
        self.came = [ring_z(block, step + 1) for step, block in enumerate(sent)]

    def last(self, *shapes, before={}):
        return last_add(self.place, self.mine, self.came, shapes, before)

    def hold(self, *others):
        self.mine, self.came, others = tie(self.mine, self.came, others)
        return others


def split_depth_spot(place_ref, step, depth):
    return lax.rem(place_ref[0] + depth - step, depth)


def join_depth(place, blocks, cuts, name):
    depth = len(blocks)
    rows = blocks[0].shape[0]
    moves = []
    for step in range(depth):
        for j, (start, stop) in enumerate(cuts):
            cut = (slice(None), slice(start, stop))
            moves.append((step, cut, j, lambda p, step=step: split_depth_spot(p, step, depth)))
    return join(place, blocks, moves, [(depth, rows, stop - start) for start, stop in cuts], name)


def join_plane(place, blocks):
    moves = []
    for at, (dx, dy) in enumerate(((0, 0), (1, 0), (0, 1), (1, 1))):
        moves.append(
            (at, (), 0, lambda p, dx=dx, dy=dy: (flip(p[1], dx), flip(p[3], dy)))
        )
    return join(place, blocks, moves, [(2, 2) + blocks[0].shape], "join_plane")[0]


def near_parts(own, by_x, by_y, by_xy, cores):
    blocks = {(0, 0): own, (1, 0): by_x, (0, 1): by_y, (1, 1): by_xy}
    return [cores[dx, dy] if dc else blocks[dx, dy] for dx, dc, dy in NEAR]


def paired(inputs, grad_out, random_blocks, *shards):
    depth = lax.axis_size("dp") // 4
    dp, y = lax.axis_index("dp"), lax.axis_index("seq")
    z, x, c = dp // 4, (dp // 2) % 2, dp % 2
    spots = (z, x, c, y)
    place = jnp.stack(spots).astype(jnp.int32)
    w_query, w_key, w_value, w_out, w_up, w_down = shards[:6]
    vectors = shards[6:]
    half, width = inputs.shape[1:]
    rows, tall_rows, hidden_width = w_up.shape[0], w_down.shape[0], w_up.shape[1]
    pairs = width // PAIR
    ring = range(1, depth)

    sizes = [vector.shape[0] // rows for vector in vectors]
    small = jnp.concatenate([vector.reshape(-1, rows) for vector in vectors])
    small = jnp.pad(small, ((0, rows - small.shape[0]), (0, PAIR - rows)))
    shard = join_beside(place, [w_query, w_key, w_value, w_out, small])
    turned = [shard] + [ring_z(shard, step) for step in ring]
    tall_cut = tall_rows // 2
    down_near, down_own = w_down[tall_cut:], w_down[:tall_cut]
    down_x = swap_x(down_own)
    random_far = swap_y(pick(random_blocks, 1 - y, 0))
    random_far, far_rows = tie(random_far, cast_far(place, inputs))
    far_rows = swap_y(far_rows)
    up_shard = join_beside(
        place, [w_up] + [down_near[start : start + rows] for start in range(0, tall_cut, rows)]
    )
    at_out = width
    turned, down_x, far_rows, up_shard, down_own, random_far, grad_out = tie(
        turned, down_x, far_rows, up_shard, down_own, random_far, grad_out
    )
    cut = 2 * width
    left, right = join_depth(place, turned, [(0, cut), (cut, shard.shape[1])], "join_first")
    left_y, right_x = swap_y(left), swap_x(right)
    up_turned = {1: ring_z(up_shard, 1), depth - 1: ring_z(up_shard, depth - 1)}
    down_y, down_xy = swap_y(down_own), swap_y(down_x)
    far_grad_low = cast_far(place, grad_out)
    left_y, right_x, up_turned, down_own, down_x, down_y, down_xy, far_grad_low, random_far = tie(
        left_y, right_x, up_turned, down_own, down_x, down_y, down_xy, far_grad_low, random_far
    )
    left_x, left_xy = swap_x(left), swap_x(left_y)
    right_y, right_xy = swap_y(right), swap_y(right_x)
    for step in ring:
        if step not in up_turned:
            up_turned[step] = ring_z(up_shard, step)
    plane = join_plane(place, [down_own, down_x, down_y, down_xy])
    local_blocks = half // BLOCK
    ids = jnp.arange(2 * local_blocks, dtype=jnp.int32)
    block_ids = (ids + y * local_blocks) % (2 * local_blocks)
    random_ids = jnp.concatenate([pick(random_blocks, y, 0), random_far], axis=1)
    bias = key_bias(random_ids, block_ids)
    left_x, left_xy, right_y, right_xy, up_turned, left_y, right_x, plane, bias = tie(
        left_x, left_xy, right_y, right_xy, up_turned, left_y, right_x, plane, bias
    )
    (up_own,) = join_depth(
        place, [up_shard] + [up_turned[step] for step in ring], [(0, up_shard.shape[1])], "join_up"
    )
    up_own, left, left_x, left_y, left_xy, right, right_x, right_y, right_xy = tie(
        up_own, left, left_x, left_y, left_xy, right, right_x, right_y, right_xy
    )
    up_y, up_x = swap_y(up_own), swap_x(up_own)
    left_core = {
        (0, 0): swap_core(left), (0, 1): swap_core(left_y),
        (1, 0): swap_core(left_x), (1, 1): swap_core(left_xy),
    }
    right_core = {
        (0, 0): swap_core(right), (0, 1): swap_core(right_y),
        (1, 0): swap_core(right_x), (1, 1): swap_core(right_xy),
    }
    left_parts = near_parts(left, left_x, left_y, left_xy, left_core)
    right_parts = near_parts(right, right_x, right_y, right_xy, right_core)
    left_parts, right_parts, up_own = tie(left_parts, right_parts, up_own)

    planes = {0: plane, 1: ring_z(plane, 1), depth - 1: ring_z(plane, depth - 1)}
    spans = small_vectors(place, right_parts, cut, sizes, rows)
    (
        ln1_gain,
        ln1_bias,
        query_bias,
        value_bias,
        out_bias,
        ln2_gain,
        ln2_bias,
        up_bias,
        down_bias,
    ) = spans
    qkv_bias = jnp.concatenate([query_bias, jnp.zeros_like(query_bias), value_bias], axis=1)
    normed_low, qkv = norm_project(
        place, inputs, far_rows, ln1_gain, ln1_bias, left_parts, right_parts, qkv_bias
    )
    near_pairs = 2 * pairs // 8
    attended = attn_forward(place, qkv, bias, 0, near_pairs)
    attended, up_y, up_x, planes, far_grad_low = tie(attended, up_y, up_x, planes, far_grad_low)
    up_xy = swap_x(up_y)
    up_core = {(0, 0): swap_core(up_own), (0, 1): swap_core(up_y)}
    far_grad = swap_y(far_grad_low)
    for step in ring:
        if step not in planes:
            planes[step] = ring_z(planes[0], step)
    prob, mixed_low, totals = attn_forward(
        place, qkv, bias, near_pairs, pairs - near_pairs, attended
    )
    mixed_low, far_grad, up_core, up_x, planes = tie(mixed_low, far_grad, up_core, up_x, planes)
    up_core[1, 0] = swap_core(up_x)
    plane_core = {step: swap_core(planes[step]) for step in (0, 1, depth - 1)}
    grad_ff_low, grad_down_bias = join_low(place, grad_out, far_grad)
    mixed_low, grad_ff_low = tie(mixed_low, grad_ff_low)
    middle, normed_two_low = out_norm(
        place, mixed_low, right_parts, at_out, out_bias, inputs, far_rows, ln2_gain, ln2_bias
    )
    normed_two_low, up_xy, plane_core, up_core, planes = tie(
        normed_two_low, up_xy, plane_core, up_core, planes
    )
    up_core[1, 1] = swap_core(up_xy)
    for step in ring:
        if step not in plane_core:
            plane_core[step] = swap_core(planes[step])
    up_parts = near_parts(up_own, up_x, up_y, up_xy, up_core)
    down_parts = [part for step in range(depth) for part in (planes[step], plane_core[step])]

    down_sums = [Reduce(place, tall_rows, True) for _ in range(3)]
    near_sum = Reduce(place, rows, False)
    wide_sum = Reduce(place, rows, True)
    out_sum = Reduce(place, rows, True)
    left_sum = Reduce(place, rows, True)
    right_sum = Reduce(place, rows, False)

    def feed(first, count, state, wide):
        return feed_forward(
            place, first, count, depth, normed_two_low, grad_ff_low, up_parts, down_parts, up_bias,
            down_bias, far_rows, state, wide,
        )

    near = depth // 2
    near_width = hidden_width // 2
    each = hidden_width // depth
    mine, other, up_mine, up_other, bias_0, back, total = feed(
        0, near, (middle, middle), (near_width, 0, ())
    )
    down_sums[0].begin(mine, other)
    near_sum.begin(up_mine, up_other)
    mine, other, up_mine, up_other, bias_1, back, total = feed(
        near, depth - 1 - near, (total, back), (near_width, 0, ())
    )
    (back,) = down_sums[0].hold(back)
    (back,) = near_sum.hold(back)
    down_sums[1].begin(mine, other)
    down_sums[0].first()
    near_sum.first()
    down_sums[0].mine, near_sum.mine, back = tie(down_sums[0].mine, near_sum.mine, back)
    mine, other, up_mine, up_other, bias_2, back, out_part, out_delta = feed(
        depth - 1, 1, (total, back), (near_width, (depth - 1 - near) * each, (up_mine, up_other))
    )
    (back,) = down_sums[0].hold(back)
    (back,) = near_sum.hold(back)
    (back,) = down_sums[1].hold(back)
    down_sums[2].begin(mine, other)
    wide_sum.begin(up_mine, up_other)
    down_sums[1].first()
    down_sums[1].mine, back = tie(down_sums[1].mine, back)
    grad_up_bias = jnp.concatenate([bias_0, bias_1, bias_2], axis=1)
    grad_middle, grad_attn_low, grad_mixed_low, grad_ln2_gain, grad_ln2_bias, grad_out_bias = middle_back(
        place, back, middle, ln2_gain, grad_out, far_grad, right_parts, at_out
    )
    out_sum.begin(*grad_wide(place, mixed_low, (grad_attn_low,), rows, (0, 2)))
    out_sum.mine, grad_mixed_low = tie(out_sum.mine, grad_mixed_low)
    (grad_mixed_low,) = down_sums[1].hold(grad_mixed_low)
    (grad_mixed_low,) = down_sums[2].hold(grad_mixed_low)
    (grad_mixed_low,) = wide_sum.hold(grad_mixed_low)
    down_sums[2].first()
    near_sum.second()
    down_sums[2].mine, near_sum.mine, grad_mixed_low, out_delta = tie(
        down_sums[2].mine, near_sum.mine, grad_mixed_low, out_delta
    )
    out_far = swap_y(out_delta)
    grads = attn_backward(place, qkv, prob, mixed_low, totals, grad_mixed_low, 0, pairs // 2)
    grads, out_far = tie(grads, out_far)
    (grads,) = near_sum.hold(grads)
    (grads,) = down_sums[2].hold(grads)
    (grads,) = out_sum.hold(grads)
    wide_sum.first()
    out_sum.first()
    near_sum.third()
    down_sums[0].second(*down_sums[1:])
    down_sum = down_sums[0]
    down_sum.mine, near_sum.mine, wide_sum.mine, out_sum.mine, grads = tie(
        down_sum.mine, near_sum.mine, wide_sum.mine, out_sum.mine, grads
    )
    grads = attn_backward(
        place, qkv, prob, mixed_low, totals, grad_mixed_low, pairs // 2, pairs - pairs // 2, grads
    )
    (grads,) = near_sum.hold(grads)
    (grads,) = wide_sum.hold(grads)
    (grads,) = down_sum.hold(grads)
    wide_sum.second()
    wide_sum.mine, grads = tie(wide_sum.mine, grads)
    wide = grad_wide(place, normed_low, grads, rows, (0, 6), 2)
    (wide,) = wide_sum.hold(wide)
    (wide,) = out_sum.hold(wide)
    out_sum.second()
    out_sum.mine, wide = tie(out_sum.mine, wide)
    left_sum.begin(*wide[:2])
    right_sum.begin(*wide[2:])
    (grad_up_near,) = near_sum.last((rows, near_width))
    left_sum.mine, grads, grad_up_near = tie(left_sum.mine, grads, grad_up_near)
    (grads,) = out_sum.hold(grads)
    (grads,) = left_sum.hold(grads)
    left_sum.first()
    (grads,) = right_sum.hold(grads)
    right_sum.first()
    down_sum.third(wide_sum, out_sum)
    left_sum.mine, right_sum.mine, down_sum.mine, grads = tie(
        left_sum.mine, right_sum.mine, down_sum.mine, grads
    )
    in_part, in_delta, grad_ln1_gain, grad_ln1_bias, grad_query_bias, grad_value_bias = input_back(
        place, grads, left_parts, right_parts, inputs, far_rows, ln1_gain, grad_middle, far_grad
    )
    (in_delta,) = left_sum.hold(in_delta)
    left_sum.second()
    (in_delta,) = right_sum.hold(in_delta)
    right_sum.second()
    left_sum.mine, right_sum.mine, in_delta, grad_ln1_gain = tie(
        left_sum.mine, right_sum.mine, in_delta, grad_ln1_gain
    )
    grad_vectors = (
        grad_ln1_gain,
        grad_ln1_bias,
        grad_query_bias,
        grad_value_bias,
        grad_out_bias,
        grad_ln2_gain,
        grad_ln2_bias,
        grad_up_bias,
        grad_down_bias,
    )
    packed = jnp.concatenate(grad_vectors, axis=1).reshape(-1, PAIR)
    packed = packed + swap_core(packed)
    packed = packed + swap_y(packed)
    (in_delta,) = down_sum.hold(in_delta)
    (in_delta,) = left_sum.hold(in_delta)
    (in_delta,) = right_sum.hold(in_delta)
    packed, in_delta = tie(packed, in_delta)
    in_far = swap_y(in_delta)
    packed = packed + swap_x(packed)
    left_sum.third(right_sum, vectors=packed, sizes=sizes)
    left_sum.mine, out_far, down_sum.mine = tie(left_sum.mine, out_far, down_sum.mine)
    grad_w_down, grad_w_up, grad_w_out = down_sum.last(
        w_down.shape, (rows, near_width), w_out.shape, before={1: grad_up_near}
    )
    result = fill_far(place, out_part, inputs, out_far)
    result, in_far, grad_w_up = tie(result, in_far, grad_w_up)
    grad_in = fill_far(place, in_part, grad_out, in_far)
    left_sum.came, grad_in = tie(left_sum.came, grad_in)
    square = (rows, width)
    grad_w_query, grad_w_key, grad_w_value, packed = left_sum.last(
        square, square, square, (rows, PAIR)
    )
    packed = packed.reshape(-1)
    out_vectors = []
    for index, size in enumerate(sizes):
        count = size * rows
        lane = (dp * 2 + y) * count % PAIR
        out_vectors.append(lax.dynamic_slice_in_dim(packed, index * PAIR + lane, count))
    return (
        (result, grad_in, grad_w_query, grad_w_key, grad_w_value, grad_w_out, grad_w_up, grad_w_down)
        + tuple(out_vectors)
    )


def solution(mesh):
    tokens, table, matrix, vector = P("dp", "seq", None), P("dp", None, "seq", None), P(BOTH, None), P(BOTH)
    in_specs = (tokens, tokens, table) + (matrix,) * 6 + (vector,) * 9
    out_specs = (tokens, tokens) + (matrix,) * 6 + (vector,) * 9
    paired_fits = mesh.shape["seq"] == 2 and mesh.shape["dp"] % 4 == 0

    def body(inputs, *rest):
        whole = paired if paired_fits and inputs.shape[0] == 2 else on_device
        return whole(inputs, *rest)

    return jax.shard_map(
        body, mesh=mesh, in_specs=in_specs, out_specs=out_specs, check_vma=False
    )
```
